32 devices in a mesh: pb: 4 (over y, x), pa: 8 (over z, core).
Axes of the slice: x: 2, y: 2, z: 4, core: 2. Of those that a mesh axis runs over, the one named last changes fastest.
Arguments:
- decoder_in: float32 [16, 20, 768], P('pb'), may hold values from -6 to 6
- encodings: bfloat16 [16, 4096, 768], P('pb', 'pa'), may hold values from -6 to 6
- out_grad: float32 [16, 20, 768], P('pb'), may hold values from -6 to 6
- passage_len: int32 [16], P('pb'), may hold values from 250 to 500, as said below
- passage_count: int32 [16], P('pb'), may hold values from 4 to 16, as said below
- buckets: int32 [20, 20], replicated, may hold values from 0 to 31
- self_query: bfloat16 [768, 768], P('pa'), may hold values from -0.21875 to 0.21875
- self_key: bfloat16 [768, 768], P('pa'), may hold values from -0.21875 to 0.21875
- self_value: bfloat16 [768, 768], P('pa'), may hold values from -0.21875 to 0.21875
- self_out: bfloat16 [768, 768], P('pa'), may hold values from -0.4375 to 0.4375
- cross_query: bfloat16 [768, 768], P('pa'), may hold values from -0.4375 to 0.4375
- cross_key: bfloat16 [768, 768], P('pa'), may hold values from -0.21875 to 0.21875
- cross_value: bfloat16 [768, 768], P('pa'), may hold values from -0.21875 to 0.21875
- cross_out: bfloat16 [768, 768], P('pa'), may hold values from -3.5 to 3.5
- ffn_expand: bfloat16 [768, 3072], P('pa'), may hold values from -0.21875 to 0.21875
- ffn_reduce: bfloat16 [3072, 768], P('pa'), may hold values from -0.15625 to 0.15625
- norm_self: float32 [768], replicated, may hold values from 0.5 to 1.5
- norm_cross: float32 [768], replicated, may hold values from 0.5 to 1.5
- norm_ffn: float32 [768], replicated, may hold values from 0.5 to 1.5
- bias_table: float32 [32, 12], replicated, may hold values from -4 to 4
Outputs:
- decoder_out: float32 [16, 20, 768], P('pb')
- decoder_grad: float32 [16, 20, 768], P('pb')
- encoding_grad: float32 [16, 4096, 768], P('pb', 'pa')
- grad_self_query: float32 [768, 768], P('pa')
- grad_self_key: float32 [768, 768], P('pa')
- grad_self_value: float32 [768, 768], P('pa')
- grad_self_out: float32 [768, 768], P('pa')
- grad_cross_query: float32 [768, 768], P('pa')
- grad_cross_key: float32 [768, 768], P('pa')
- grad_cross_value: float32 [768, 768], P('pa')
- grad_cross_out: float32 [768, 768], P('pa')
- grad_ffn_expand: float32 [768, 3072], P('pa')
- grad_ffn_reduce: float32 [3072, 768], P('pa')
- grad_norm_self: float32 [768], replicated
- grad_norm_cross: float32 [768], replicated
- grad_norm_ffn: float32 [768], replicated
- grad_bias_table: float32 [32, 12], replicated
The draws below stay inside these ranges and needn't reach their ends.
Inputs may be any that keep to these rules, and one draw needn't show every extreme that they name: `passage_len`: each question's passages all have one length, 250 or 500; in the first aligned block of 4 questions some question has short passages and fills every place, in the second some question has long ones and fills every place. `passage_count`: a question with passages of length L has between half and all of (4096 // 512) * (512 // L) passages; in every aligned block of 4 questions one question has all of them.
All inputs are finite; a program needn't handle non-finite values.
Results may differ from the reference program's by a relative error of at most 0.03.
Values may be sent and summed in bfloat16 or wider, within the bound.
A program may use at most 128 MiB of HBM per device.

```python
import jax
import jax.numpy as jnp
from jax import lax

D = 768
HEADS = 12
HEAD_DIM = 64
FF = 3072
BUCKETS = 32
ANS = 20
Q_DEV = 4
SLOT = 512
SHORT_LEN = 250
LONG_LEN = 500
QUESTIONS = 16
KEYS = 4096


def passage_layout(key):
    key_flag, key_pick, key_count = jax.random.split(key, 3)
    longer = jax.random.randint(key_flag, (QUESTIONS,), 0, 2)
    block_count = QUESTIONS // Q_DEV
    picked = jax.random.randint(key_pick, (block_count,), 0, Q_DEV)
    position = jnp.arange(QUESTIONS) % Q_DEV
    block_id = jnp.arange(QUESTIONS) // Q_DEV
    chosen = position == picked[block_id]
    longer = jnp.where(chosen, block_id % 2, longer)
    length = jnp.where(longer == 1, LONG_LEN, SHORT_LEN)
    places = KEYS // SLOT * (SLOT // length)
    span_count = places - places // 2 + 1
    raw_draw = jax.random.randint(key_count, (QUESTIONS,), 0, 1 << 20)
    count = places // 2 + raw_draw % span_count
    count = jnp.where(chosen, places, count)
    return (length.astype(jnp.int32), count.astype(jnp.int32))


def draw_passage_len(key, part):
    length, count = passage_layout(key)
    return length


def draw_passage_count(key, part):
    length, count = passage_layout(key)
    return count


def with_ends(entries, own_key, least, high):
    longest = entries.shape.index(max(entries.shape))
    spots = []
    for shift in (0, 1):
        where = [jax.random.randint(jax.random.fold_in(own_key, axis), (), 0, length) for axis, length in enumerate(entries.shape)]
        where[longest] = (where[longest] + shift) % entries.shape[longest]
        spots.append(tuple(where))
    return entries.at[spots[0]].set(least).at[spots[1]].set(high)


def steps_of(key, shape, shards, least, largest):
    level, own = 1.0, jax.random.fold_in(key, 6)
    for dim, parts in shards:
        steps = jnp.exp(jax.random.uniform(jax.random.fold_in(own, dim), (parts,), jnp.float32, least / len(shards), largest / len(shards)))
        level = level * jnp.repeat(steps, shape[dim] // parts).reshape([-1 if axis == dim else 1 for axis in range(len(shape))])
    return level


def gaussian(own_key, shape, deviation, reach, pieces=(), kind=jnp.bfloat16):
    entries = deviation * jax.random.normal(own_key, shape, jnp.float32)
    if pieces:
        entries = entries * steps_of(own_key, shape, pieces, -0.22, 0.18)
    return jnp.clip(entries, -reach, reach).astype(kind)


def setup_inputs(seed: int = 0) -> dict:
    seeds = jax.random.split(jax.random.key(seed), 21)
    decoder_in = gaussian(seeds[0], (QUESTIONS, ANS, D), 1.0, 6.0, ((0, 4),), jnp.float32)
    encodings = gaussian(seeds[1], (QUESTIONS, KEYS, D), 1.0, 6.0, ((0, 4), (1, 8)))
    out_grad = gaussian(seeds[2], (QUESTIONS, ANS, D), 1.0, 6.0, ((0, 4),), jnp.float32)
    passage_len = draw_passage_len(jax.random.fold_in(seeds[20], 71), 0)
    passage_count = draw_passage_count(jax.random.fold_in(seeds[20], 71), 0)
    buckets = with_ends(jax.random.randint(seeds[5], (ANS, ANS), 0, BUCKETS), jax.random.fold_in(seeds[5], 1), 0, BUCKETS - 1).astype(jnp.int32)
    self_query = gaussian(seeds[6], (D, D), D ** -0.5, 0.21875, ((0, 8),))
    self_key = gaussian(seeds[7], (D, D), D ** -0.5, 0.21875, ((0, 8),))
    self_value = gaussian(seeds[8], (D, D), D ** -0.5, 0.21875, ((0, 8),))
    self_out = gaussian(seeds[9], (D, D), (D // 4) ** -0.5, 0.4375, ((0, 8),))
    cross_query = gaussian(seeds[10], (D, D), (D // 4) ** -0.5, 0.4375, ((0, 8),))
    cross_key = gaussian(seeds[11], (D, D), D ** -0.5, 0.21875, ((0, 8),))
    cross_value = gaussian(seeds[12], (D, D), D ** -0.5, 0.21875, ((0, 8),))
    cross_out = gaussian(seeds[13], (D, D), (D // 256) ** -0.5, 3.5, ((0, 8),))
    ffn_expand = gaussian(seeds[14], (D, FF), D ** -0.5, 0.21875, ((0, 8),))
    ffn_reduce = gaussian(seeds[15], (FF, D), (FF // 2) ** -0.5, 0.15625, ((0, 8),))
    norm_self = jnp.clip(1.0 + 0.1 * jax.random.normal(seeds[16], (D,), jnp.float32), 0.5, 1.5)
    norm_cross = jnp.clip(1.0 + 0.1 * jax.random.normal(seeds[17], (D,), jnp.float32), 0.5, 1.5)
    norm_ffn = jnp.clip(1.0 + 0.1 * jax.random.normal(seeds[18], (D,), jnp.float32), 0.5, 1.5)
    bias_table = gaussian(seeds[19], (BUCKETS, HEADS), 1.0, 4.0, (), jnp.float32)
    return dict(decoder_in=decoder_in, encodings=encodings, out_grad=out_grad, passage_len=passage_len, passage_count=passage_count, buckets=buckets, self_query=self_query, self_key=self_key, self_value=self_value, self_out=self_out, cross_query=cross_query, cross_key=cross_key, cross_value=cross_value, cross_out=cross_out, ffn_expand=ffn_expand, ffn_reduce=ffn_reduce, norm_self=norm_self, norm_cross=norm_cross, norm_ffn=norm_ffn, bias_table=bias_table)


epsilon = 1e-06
highest = lax.Precision.HIGHEST
masked_score = -1e+30

@jax.custom_vjp
def low(v):
    return lax.optimization_barrier(v.astype(jnp.bfloat16)).astype(jnp.float32)

@jax.custom_vjp
def low_back(v):
    return v

def low_keep(v):
    return (low(v), None)

def low_pass(kept, grad):
    return (grad,)

def back_keep(v):
    return (v, None)

def back_low(kept, grad):
    return (low(grad),)
low.defvjp(low_keep, low_pass)
low_back.defvjp(back_keep, back_low)

def round_both(value):
    return low_back(low(value))

def matmul(left, right):
    return jnp.matmul(left, right, precision=highest)

def rms_norm(value, gain):
    return value * lax.rsqrt(lax.optimization_barrier(jnp.mean(value * value, -1, keepdims=True)) + epsilon) * gain

def valid_keys(passage_len, passage_count):
    positions = jnp.arange(KEYS)
    device = positions // SLOT
    within = positions % SLOT
    per_device = SLOT // passage_len
    held_count = jnp.clip(passage_count[:, None] - device[None, :] * per_device[:, None], 0, per_device[:, None])
    return within[None, :] < held_count * passage_len[:, None]

def cross_block(cquery, encoded, valid_rows, key_weight, value_weight, given_max):
    key_heads = round_both(matmul(encoded, key_weight)).reshape(KEYS, HEADS, HEAD_DIM)
    value_heads = round_both(matmul(encoded, value_weight)).reshape(KEYS, HEADS, HEAD_DIM)
    scores = low_back(jnp.einsum('ihd,jhd->hij', cquery, key_heads, precision=highest) * HEAD_DIM ** (-0.5))
    scores = jnp.where(valid_rows[None, None, :], scores, masked_score)
    if given_max is None:
        return lax.optimization_barrier(jnp.max(scores, -1))
    exp_weights = jnp.exp(scores - given_max[:, :, None])
    numerator = low_back(jnp.einsum('hij,jhd->ihd', low(exp_weights), value_heads, precision=highest))
    totals = lax.optimization_barrier(jnp.sum(exp_weights, -1))
    return (numerator, totals)

def forward(decoder_in, encodings, self_query, self_key, self_value, self_out, cross_query, cross_key, cross_value, cross_out, ffn_expand, ffn_reduce, norm_self, norm_cross, norm_ffn, bias_table, buckets, valid_rows, given_max):
    questions = decoder_in.shape[0]
    factor = HEAD_DIM ** (-0.5)

    def heads_of(value):
        return value.reshape(questions, ANS, HEADS, HEAD_DIM)
    hidden_one = low(rms_norm(decoder_in, norm_self))
    query_heads = heads_of(round_both(matmul(hidden_one, self_query)))
    key_heads = heads_of(round_both(matmul(hidden_one, self_key)))
    value_heads = heads_of(round_both(matmul(hidden_one, self_value)))
    onehot = (buckets[:, :, None] == jnp.arange(BUCKETS)[None, None, :]).astype(jnp.float32)
    bias_scores = jnp.einsum('ijb,bh->hij', onehot, bias_table, precision=highest)
    causal = jnp.arange(ANS)[:, None] >= jnp.arange(ANS)[None, :]
    scores = low_back(jnp.einsum('qihd,qjhd->qhij', query_heads, key_heads, precision=highest) * factor + bias_scores[None])
    scores = jnp.where(causal[None, None], scores, masked_score)
    weights_self = low(jax.nn.softmax(scores, -1))
    mixed_self = round_both(jnp.einsum('qhij,qjhd->qihd', weights_self, value_heads, precision=highest)).reshape(questions, ANS, D)
    resid_one = decoder_in + low_back(matmul(mixed_self, self_out))
    hidden_two = low(rms_norm(resid_one, norm_cross))
    cquery = heads_of(round_both(matmul(hidden_two, cross_query)))
    if given_max is None:
        return lax.map(lambda member: cross_block(member[0], member[1], member[2], cross_key, cross_value, None), (cquery, encodings, valid_rows))
    cross_fn = jax.checkpoint(lambda member: cross_block(member[0], member[1], member[2], cross_key, cross_value, member[3]))
    numerator, totals = lax.map(cross_fn, (cquery, encodings, valid_rows, given_max))
    totals_t = jnp.transpose(totals, (0, 2, 1))[..., None]
    mixed_cross = round_both(numerator / totals_t).reshape(questions, ANS, D)
    resid_two = resid_one + low_back(matmul(mixed_cross, cross_out))
    hidden_three = low(rms_norm(resid_two, norm_ffn))
    pre_act = low_back(matmul(hidden_three, ffn_expand))
    activation = low(jax.nn.gelu(pre_act, approximate=True))
    return resid_two + low_back(matmul(activation, ffn_reduce))

def reference(decoder_in, encodings, out_grad, passage_len, passage_count, buckets, self_query, self_key, self_value, self_out, cross_query, cross_key, cross_value, cross_out, ffn_expand, ffn_reduce, norm_self, norm_cross, norm_ffn, bias_table):
    valid_rows = valid_keys(passage_len, passage_count)
    enc_wide = encodings.astype(jnp.float32)
    sq_w = self_query.astype(jnp.float32)
    sk_w = self_key.astype(jnp.float32)
    sv_w = self_value.astype(jnp.float32)
    so_w = self_out.astype(jnp.float32)
    cq_w = cross_query.astype(jnp.float32)
    ck_w = cross_key.astype(jnp.float32)
    cv_w = cross_value.astype(jnp.float32)
    co_w = cross_out.astype(jnp.float32)
    fe_w = ffn_expand.astype(jnp.float32)
    fr_w = ffn_reduce.astype(jnp.float32)
    row_max = forward(decoder_in, enc_wide, sq_w, sk_w, sv_w, so_w, cq_w, ck_w, cv_w, co_w, fe_w, fr_w, norm_self, norm_cross, norm_ffn, bias_table, buckets, valid_rows, None)

    def forward_run(a0, a1, a2, a3, a4, a5, a6, a7, a8, a9, a10, a11, a12, a13, a14, a15):
        return forward(a0, a1, a2, a3, a4, a5, a6, a7, a8, a9, a10, a11, a12, a13, a14, a15, buckets, valid_rows, row_max)
    decoder_out, pullback = jax.vjp(forward_run, decoder_in, enc_wide, sq_w, sk_w, sv_w, so_w, cq_w, ck_w, cv_w, co_w, fe_w, fr_w, norm_self, norm_cross, norm_ffn, bias_table)
    gradients = pullback(out_grad)
    return (decoder_out, gradients[0], gradients[1], gradients[2], gradients[3], gradients[4], gradients[5], gradients[6], gradients[7], gradients[8], gradients[9], gradients[10], gradients[11], gradients[12], gradients[13], gradients[14], gradients[15])
```

```python
import types

import jax
import jax.numpy as jnp
from jax import lax
from jax.experimental import pallas as pl
from jax.experimental.pallas import tpu as pltpu
from jax.sharding import PartitionSpec as P

epsilon = 1e-06
highest = lax.Precision.HIGHEST
masked_score = -1e30


def product(left, right):
    return jnp.dot(left, right, preferred_element_type=jnp.float32)


def lowered(value):
    return value.astype(jnp.bfloat16)


def norm_forward(value):
    factor = lax.rsqrt(jnp.mean(value * value, -1, keepdims=True) + epsilon)
    return (value * factor, factor)


def norm_backward(grad_out, normal, factor, gain):
    inner_term = grad_out * gain
    grad_in = factor * (inner_term - normal * jnp.mean(inner_term * normal, -1, keepdims=True))
    grad_gain = jnp.sum(grad_out * normal, (0, 1))
    return (grad_in, grad_gain)


def activate(value):
    return jax.nn.gelu(value, approximate=True)


def shard_grad(inputs, grad_rows, device_place, row_count):
    sliced = lax.dynamic_slice_in_dim(inputs, device_place * row_count, row_count, 2)
    return jnp.einsum("qak,qae->ke", sliced, grad_rows, preferred_element_type=jnp.float32)


def shards(
    decoder_in,
    encodings,
    out_grad,
    passage_len,
    passage_count,
    buckets,
    self_query,
    self_key,
    self_value,
    self_out,
    cross_query,
    cross_key,
    cross_value,
    cross_out,
    ffn_expand,
    ffn_reduce,
    norm_self,
    norm_cross,
    norm_ffn,
    bias_table,
):
    wide_count = lax.axis_size("pa")
    device_place = lax.axis_index("pa")
    stacked = jnp.stack(
        [self_query, self_key, self_value, self_out, cross_query, cross_key, cross_value, cross_out]
    )
    squares, expand_full, reduce_full = (
        lax.all_gather(stacked, "pa", axis=1, tiled=True),
        lax.all_gather(ffn_expand, "pa", axis=0, tiled=True),
        lax.all_gather(ffn_reduce, "pa", axis=0, tiled=True),
    )
    query_self = squares[0]
    key_self = squares[1]
    value_self = squares[2]
    out_self = squares[3]
    query_cross = squares[4]
    key_cross = squares[5]
    value_cross = squares[6]
    out_cross = squares[7]
    questions, answer, model_width = decoder_in.shape
    head_count = bias_table.shape[1]
    head_size = model_width // head_count
    factor = head_size ** (-0.5)
    slot_rows = encodings.shape[1]
    rows_model = model_width // wide_count
    rows_hidden = expand_full.shape[1] // wide_count

    def heads_of(value):
        return value.reshape(value.shape[0], value.shape[1], head_count, head_size)

    normal_one, factor_one = norm_forward(decoder_in)
    hidden_one = lowered(normal_one * norm_self)
    query_heads = heads_of(lowered(product(hidden_one, query_self)))
    key_heads = heads_of(lowered(product(hidden_one, key_self)))
    value_heads = heads_of(lowered(product(hidden_one, value_self)))
    onehot = (buckets[:, :, None] == jnp.arange(bias_table.shape[0])[None, None, :]).astype(
        jnp.float32
    )
    bias_scores = jnp.einsum("ijb,bh->hij", onehot, bias_table, precision=highest)
    causal = jnp.arange(answer)[:, None] >= jnp.arange(answer)[None, :]
    scores = (
        jnp.einsum("qihd,qjhd->qhij", query_heads, key_heads, preferred_element_type=jnp.float32)
        * factor
        + bias_scores[None]
    )
    scores = jnp.where(causal[None, None], scores, masked_score)
    probabilities = jax.nn.softmax(scores, -1)
    weights_self = lowered(probabilities)
    mixed_self = lowered(
        jnp.einsum("qhij,qjhd->qihd", weights_self, value_heads, preferred_element_type=jnp.float32)
    ).reshape(questions, answer, model_width)
    resid_one = decoder_in + product(mixed_self, out_self)
    normal_two, factor_two = norm_forward(resid_one)
    hidden_two = lowered(normal_two * norm_cross)
    cquery = heads_of(lowered(product(hidden_two, query_cross)))
    per_device = slot_rows // passage_len
    held_count = jnp.clip(passage_count - device_place * per_device, 0, per_device)
    valid_rows = jnp.arange(slot_rows)[None, :] < (held_count * passage_len)[:, None]

    def project(encoded):
        ckeys = lowered(product(encoded, key_cross)).reshape(
            questions, slot_rows, head_count, head_size
        )
        cvalues = lowered(product(encoded, value_cross)).reshape(
            questions, slot_rows, head_count, head_size
        )
        cscores = (
            jnp.einsum("qihd,qjhd->qhij", cquery, ckeys, preferred_element_type=jnp.float32)
            * factor
        )
        cscores = jnp.where(valid_rows[:, None, None, :], cscores, masked_score)
        return (ckeys, cvalues, cscores)

    ckeys, cvalues, cscores = project(encodings)
    row_max = lax.pmax(jnp.max(cscores, -1), "pa")
    exp_weights = jnp.exp(cscores - row_max[..., None])
    part_num = jnp.einsum(
        "qhij,qjhd->qihd", lowered(exp_weights), cvalues, preferred_element_type=jnp.float32
    )
    part_total = jnp.sum(exp_weights, -1)
    numerator, totals = lax.psum((part_num, part_total), "pa")
    totals_t = jnp.transpose(totals, (0, 2, 1))[..., None]
    mixed_cross = lowered(numerator / totals_t).reshape(questions, answer, model_width)
    resid_two = resid_one + product(mixed_cross, out_cross)
    normal_three, factor_three = norm_forward(resid_two)
    hidden_three = lowered(normal_three * norm_ffn)
    pre_act = product(hidden_three, expand_full)
    activation = lowered(activate(pre_act))
    decoder_out = resid_two + product(activation, reduce_full)
    grad_z = lowered(out_grad)
    grad_reduce = shard_grad(activation, grad_z, device_place, rows_hidden)
    grad_act = jnp.einsum("qae,fe->qaf", grad_z, reduce_full, preferred_element_type=jnp.float32)
    unused_out, gelu_back = jax.vjp(activate, pre_act)
    grad_pre = lowered(gelu_back(grad_act)[0])
    grad_expand = shard_grad(hidden_three, grad_pre, device_place, rows_model)
    grad_three = jnp.einsum(
        "qaf,kf->qak", grad_pre, expand_full, preferred_element_type=jnp.float32
    )
    back_term, grad_gain_ffn = norm_backward(grad_three, normal_three, factor_three, norm_ffn)
    grad_two = out_grad + back_term
    grad_c = lowered(grad_two)
    grad_out_cross = shard_grad(mixed_cross, grad_c, device_place, rows_model)
    grad_mix = heads_of(
        lowered(jnp.einsum("qae,ke->qak", grad_c, out_cross, preferred_element_type=jnp.float32))
    )
    grad_mix_wide = grad_mix.astype(jnp.float32)
    grad_num = lowered(grad_mix_wide / totals_t)
    grad_tot = -jnp.sum(grad_mix_wide * numerator, -1) / (totals_t[..., 0] * totals_t[..., 0])
    ckeys, cvalues, cscores = project(encodings)
    exp_weights = jnp.exp(cscores - row_max[..., None])
    grad_expo = jnp.einsum("qihd,qjhd->qhij", grad_num, cvalues, preferred_element_type=jnp.float32)
    grad_expo = grad_expo + jnp.transpose(grad_tot, (0, 2, 1))[..., None]
    grad_score = lowered(exp_weights * grad_expo)
    part_query = (
        jnp.einsum("qhij,qjhd->qihd", grad_score, ckeys, preferred_element_type=jnp.float32)
        * factor
    )
    grad_cquery = lowered(lax.psum(part_query, "pa")).reshape(questions, answer, model_width)
    grad_ckeys = lowered(
        jnp.einsum("qhij,qihd->qjhd", grad_score, cquery, preferred_element_type=jnp.float32)
        * factor
    ).reshape(questions, slot_rows, model_width)
    grad_cvalues = lowered(
        jnp.einsum(
            "qhij,qihd->qjhd", lowered(exp_weights), grad_num, preferred_element_type=jnp.float32
        )
    ).reshape(questions, slot_rows, model_width)
    encoding_grad = jnp.einsum(
        "qse,ke->qsk", grad_ckeys, key_cross, preferred_element_type=jnp.float32
    )
    encoding_grad = encoding_grad + jnp.einsum(
        "qse,ke->qsk", grad_cvalues, value_cross, preferred_element_type=jnp.float32
    )
    full_key = jnp.einsum("qsk,qse->ke", encodings, grad_ckeys, preferred_element_type=jnp.float32)
    full_value = jnp.einsum(
        "qsk,qse->ke", encodings, grad_cvalues, preferred_element_type=jnp.float32
    )
    grad_query_cross = shard_grad(hidden_two, grad_cquery, device_place, rows_model)
    grad_hidden_two = jnp.einsum(
        "qae,ke->qak", grad_cquery, query_cross, preferred_element_type=jnp.float32
    )
    back_term, grad_gain_cross = norm_backward(grad_hidden_two, normal_two, factor_two, norm_cross)
    grad_one = grad_two + back_term
    grad_a = lowered(grad_one)
    grad_out_self = shard_grad(mixed_self, grad_a, device_place, rows_model)
    grad_smix = heads_of(
        lowered(jnp.einsum("qae,ke->qak", grad_a, out_self, preferred_element_type=jnp.float32))
    )
    grad_w = jnp.einsum(
        "qihd,qjhd->qhij", grad_smix, value_heads, preferred_element_type=jnp.float32
    )
    grad_s = lowered(probabilities * (grad_w - jnp.sum(grad_w * probabilities, -1, keepdims=True)))
    grad_table = jnp.einsum(
        "ijb,hij->bh", onehot, jnp.sum(grad_s.astype(jnp.float32), 0), precision=highest
    )
    grad_sq = lowered(
        jnp.einsum("qhij,qjhd->qihd", grad_s, key_heads, preferred_element_type=jnp.float32)
        * factor
    ).reshape(questions, answer, model_width)
    grad_sk = lowered(
        jnp.einsum("qhij,qihd->qjhd", grad_s, query_heads, preferred_element_type=jnp.float32)
        * factor
    ).reshape(questions, answer, model_width)
    grad_sv = lowered(
        jnp.einsum("qhij,qihd->qjhd", weights_self, grad_smix, preferred_element_type=jnp.float32)
    ).reshape(questions, answer, model_width)
    grad_query_self = shard_grad(hidden_one, grad_sq, device_place, rows_model)
    grad_key_self = shard_grad(hidden_one, grad_sk, device_place, rows_model)
    grad_value_self = shard_grad(hidden_one, grad_sv, device_place, rows_model)
    grad_hidden_one = jnp.einsum(
        "qae,ke->qak", grad_sq, query_self, preferred_element_type=jnp.float32
    )
    grad_hidden_one = grad_hidden_one + jnp.einsum(
        "qae,ke->qak", grad_sk, key_self, preferred_element_type=jnp.float32
    )
    grad_hidden_one = grad_hidden_one + jnp.einsum(
        "qae,ke->qak", grad_sv, value_self, preferred_element_type=jnp.float32
    )
    back_term, grad_gain_self = norm_backward(grad_hidden_one, normal_one, factor_one, norm_self)
    decoder_grad = grad_one + back_term
    key_part, value_part = (
        lax.psum_scatter(full_key, "pa", scatter_dimension=0, tiled=True),
        lax.psum_scatter(full_value, "pa", scatter_dimension=0, tiled=True),
    )
    summed = lax.psum(
        (
            grad_query_self,
            grad_key_self,
            grad_value_self,
            grad_out_self,
            grad_query_cross,
            key_part,
            value_part,
            grad_out_cross,
            grad_expand,
            grad_reduce,
            grad_gain_self,
            grad_gain_cross,
            grad_gain_ffn,
            grad_table,
        ),
        "pb",
    )
    key_total = summed[5]
    value_total = summed[6]
    rest_sums = (
        summed[0],
        summed[1],
        summed[2],
        summed[3],
        summed[4],
        summed[7],
        summed[8],
        summed[9],
        summed[10],
        summed[11],
        summed[12],
        summed[13],
    )
    return (
        decoder_out,
        decoder_grad,
        encoding_grad,
        rest_sums[0],
        rest_sums[1],
        rest_sums[2],
        rest_sums[3],
        rest_sums[4],
        key_total,
        value_total,
        rest_sums[5],
        rest_sums[6],
        rest_sums[7],
        rest_sums[8],
        rest_sums[9],
        rest_sums[10],
        rest_sums[11],
    )


def generic(mesh):
    placed = (
        P("pb", None, None),
        P("pb", "pa", None),
        P("pb", None, None),
        P("pb"),
        P("pb"),
        P(),
        P("pa", None),
        P("pa", None),
        P("pa", None),
        P("pa", None),
        P("pa", None),
        P("pa", None),
        P("pa", None),
        P("pa", None),
        P("pa", None),
        P("pa", None),
        P(),
        P(),
        P(),
        P(),
    )
    return jax.shard_map(
        shards,
        mesh=mesh,
        in_specs=placed,
        out_specs=(
            P("pb", None, None),
            P("pb", None, None),
            P("pb", "pa", None),
            P("pa", None),
            P("pa", None),
            P("pa", None),
            P("pa", None),
            P("pa", None),
            P("pa", None),
            P("pa", None),
            P("pa", None),
            P("pa", None),
            P("pa", None),
            P(),
            P(),
            P(),
            P(),
        ),
        check_vma=False,
    )


MESH = pl.DeviceIdType.MESH
F32, BF = jnp.float32, jnp.bfloat16
ANS, PAD, OWN, ALL = 20, 24, 48, 96
WIDTH, HEADS, SIZE, PART = 768, 12, 64, 192
ROWS = HEADS * PAD
SLOT, FF, BUCKETS = 512, 3072, 32
CQ, CK, CV, CO, SO, SQ, SK, SV, EX, RD, EN = range(11)
GELU_A, GELU_B = 0.7978845608028654, 0.044715


def nn(a, b):
    return lax.dot_general(a, b, (((1,), (0,)), ((), ())), preferred_element_type=F32)


def nt(a, b):
    return lax.dot_general(a, b, (((1,), (1,)), ((), ())), preferred_element_type=F32)


def tn(a, b):
    return lax.dot_general(a, b, (((0,), (0,)), ((), ())), preferred_element_type=F32)


def lanes(rows, width):
    return lax.broadcasted_iota(jnp.int32, (rows, width), 1)


def split4(v):
    out = []
    for j in range(4):
        base = PART * j // 128 * 128
        t = v[:, base : base + 256]
        out.append(pltpu.roll(t, PART, 1) if PART * j != base else t)
    return out


def join4(parts):
    low = lanes(parts[0].shape[0], 128) < 64
    tiles = []
    for a, b in ((parts[0], parts[1]), (parts[2], parts[3])):
        b = pltpu.roll(b, 64, 1)
        tiles += [a[:, :128], jnp.where(low, a[:, 128:], b[:, :128]), b[:, 128:]]
    return jnp.concatenate(tiles, 1)


def join3(parts):
    low = lanes(parts[0].shape[0], 128) < 64
    a, b = parts[0], pltpu.roll(parts[1], 64, 1)
    return jnp.concatenate([a[:, :128], jnp.where(low, a[:, 128:], b[:, :128]), b[:, 128:], parts[2]], 1)


def part3(v):
    return [v[:, :256], pltpu.roll(v[:, 128:384], PART, 1), v[:, 384:]]


def choose(parts, index):
    v = parts[0]
    for j in range(1, len(parts)):
        v = lax.select(index == j, parts[j], v)
    return v


def stack_heads(v, count):
    head = lanes(*v.shape) // SIZE
    return jnp.concatenate([jnp.where(head == h, v, 0.0) for h in range(count)], 0)


def pick_heads(v, count):
    head = lanes(PAD, v.shape[1]) // SIZE
    out = jnp.zeros((PAD, v.shape[1]), F32)
    for h in range(count):
        out = out + jnp.where(head == h, v[PAD * h : PAD * (h + 1)], 0.0)
    return out


def pair_stack(v, p):
    t = v[:, 128 * p : 128 * (p + 1)]
    low = lanes(PAD, 128) < SIZE
    return jnp.concatenate([jnp.where(low, t, 0.0), jnp.where(low, 0.0, t)], 0)


SCRATCH = dict(
    sq=((8, WIDTH, WIDTH), BF),
    ex=((WIDTH, FF), BF),
    rd=((WIDTH, WIDTH), BF),
    enc=((4, SLOT, WIDTH), BF),
    xs=((OWN, WIDTH), F32),
    ogs=((OWN, WIDTH), F32),
    bks=((PAD, PAD), jnp.int32),
    bias=((3 * PAD, PAD), F32),
    s1=((4, OWN, 640), BF),
    r1=((3, OWN, 640), BF),
    gact=((4, OWN, WIDTH), BF),
    s2=((4, OWN, 256), BF),
    r2=((3, OWN, 256), BF),
    ag2=((8, OWN, 256), BF),
    x6=((6, 192, 128), BF),
    y6=((6, 192, 128), BF),
    qk=((4, ROWS, WIDTH), BF),
    gv=((4, ROWS, WIDTH), BF),
    bs=((4, ROWS, WIDTH), BF),
    as_=((4, ROWS, WIDTH), BF),
    es=((4, ROWS, SLOT), BF),
    gs=((4, ROWS, SLOT), BF),
    stat=((384, 128), F32),
    stg=((8, 8, 384), F32),
    wrow=((128, 384), F32),
    wcol=((384, 128), F32),
    s5=((2, 4, OWN, 256), BF),
    r5=((8, OWN, 256), BF),
    mixg=((2, 4, OWN, 256), BF),
    gm=((2, OWN, WIDTH), BF),
    s7=((2, 4, OWN, 256), BF),
    r7=((8, OWN, 256), BF),
    gcq=((4, OWN, 256), BF),
    s8=((4, OWN, 256), BF),
    r8=((3, OWN, 256), BF),
    dog=((8, OWN, 256), BF),
    dgr=((2, OWN, WIDTH), F32),
    tot=((ROWS, 128), F32),
    gsg=((4, OWN, 640), BF),
    tg=((4, OWN, 256), BF),
    stz=((4, BUCKETS, 128), F32),
    wg=((8, 96, WIDTH), BF),
    gexs=((96, FF), BF),
    gres=((384, WIDTH), BF),
    p1=((2, 4, OWN, WIDTH), BF),
    p2=((2, 4, OWN, 4096), BF),
    p3=((2, 4, OWN, 1024), BF),
    p4=((2, 4, OWN, 1024), BF),
    p5=((2, 4, OWN, 1024), BF),
    p6=((2, 4, OWN, 2560), BF),
    sgain=((2, 4, 8, WIDTH), F32),
    stab=((2, 4, BUCKETS, 128), F32),
    kw1=((WIDTH, WIDTH), BF),
    kr1=((384, WIDTH), BF),
    kw2=((4, 96, WIDTH), BF),
    kr2=((3, 96, WIDTH), BF),
    kw3=((4, 96, 256), BF),
    kr3=((3, 96, 256), BF),
    kw4=((2, 4, 96, 256), BF),
    vw1=((WIDTH, WIDTH), BF),
    vr1=((384, WIDTH), BF),
    vw2=((4, 96, WIDTH), BF),
    vr2=((3, 96, WIDTH), BF),
    vw3=((4, 96, 256), BF),
    vr3=((3, 96, 256), BF),
    vw4=((2, 4, 96, 256), BF),
    eg=((4, SLOT, WIDTH), BF),
)
SEMAPHORES = 512
NEAR, SCALAR, FAR = pltpu.VMEM, pltpu.SMEM, pl.ANY
IN_KIND = dict(
    x=NEAR, og=NEAR, plen=SCALAR, pcount=SCALAR, buckets=NEAR, table=SCALAR,
    g1=NEAR, g2=NEAR, g3=NEAR, enc_h=FAR,
    wq=FAR, wk=FAR, wv=FAR, wo=FAR, wcq=FAR, wck=FAR, wcv=FAR, wco=FAR, wex=FAR, wre=FAR,
)
OUT_KIND = dict(
    decoder_out=NEAR, decoder_grad=NEAR, encoding_grad=FAR, squares=FAR, gex=FAR, gre=FAR, gains=NEAR, table_grad=NEAR,
)


class Wire:
    def __init__(self, sems):
        self.sems, self.count, self.sent = sems, 0, []
        self.pb, self.pa = lax.axis_index("pb"), lax.axis_index("pa")
        self.z, self.c = self.pa // 2, lax.rem(self.pa, 2)

    def next(self):
        self.count += 1
        return self.sems.at[self.count - 1]

    def local(self, src, dst):
        copy = pltpu.make_async_copy(src, dst, self.next())
        copy.start()
        return copy

    def remote(self, src, dst, pb, pa):
        copy = pltpu.make_async_remote_copy(
            src_ref=src,
            dst_ref=dst,
            send_sem=self.next(),
            recv_sem=self.next(),
            device_id=(pb, pa),
            device_id_type=MESH,
        )
        copy.start()
        self.sent.append(copy)
        return copy

    def zpeer(self, j):
        return lax.rem(self.z + j, 4)

    def ppeer(self, j):
        return lax.rem(self.pb + j, 4)

    def xside(self):
        return self.pb + 1 - 2 * lax.rem(self.pb, 2)

    def yside(self):
        return lax.rem(self.pb + 2, 4)

    def to_core(self, src, dst):
        return self.remote(src, dst, self.pb, self.pa + 1 - 2 * self.c)

    def to_z(self, src_of, dst_of):
        out = []
        for j in (1, 2, 3):
            t = self.zpeer(j)
            out.append(self.remote(src_of(t), dst_of(j), self.pb, 2 * t + self.c))
        return out

    def to_column(self, src_of, dst_of):
        out = []
        for j in range(1, 8):
            t = lax.rem(self.pa + j, 8)
            out.append(self.remote(src_of(t), dst_of(j), self.pb, t))
        return out

    def to_plane(self, src_of, dst_of):
        out = []
        for j in (1, 2, 3):
            t = self.ppeer(j)
            out.append(self.remote(src_of(t), dst_of(j), t, self.pa))
        return out


def received(copies):
    for copy in copies:
        copy.wait_recv()


class PairGather:
    def __init__(self, wire, sq, pair):
        self.w, self.sq, self.pair = wire, sq, pair

    def part(self, z, pb, begin, size):
        row = pl.multiple_of(96 * (2 * z + self.w.c) + 48 * lax.rem(pb, 2), 16)
        return self.sq.at[2 * self.pair + pb // 2, pl.ds(row, 48), pl.ds(begin, size)]

    def start(self):
        w = self.w
        src = self.part(w.z, w.pb, 0, WIDTH)
        self.a = w.to_z(lambda t: src, lambda j: src)

    def plane(self):
        w = self.w
        received(self.a)
        self.b = []
        for i in (1, 2, 3):
            ref = self.part(w.zpeer(i), w.pb, 0, WIDTH)
            self.b += [w.remote(ref, ref, side, w.pa) for side in (w.xside(), w.yside())]

    def relay(self):
        w = self.w
        received(self.b)
        self.d = []
        for i in (1, 2, 3):
            ref = self.part(w.zpeer(i), w.xside(), 0, WIDTH // 2)
            self.d.append(w.remote(ref, ref, w.yside(), w.pa))
            ref = self.part(w.zpeer(i), w.yside(), WIDTH // 2, WIDTH // 2)
            self.d.append(w.remote(ref, ref, w.xside(), w.pa))

    def core(self):
        w = self.w
        received(self.d)
        self.e = []
        for k in (0, 1):
            for i in (1, 2, 3):
                row = pl.multiple_of(96 * (2 * w.zpeer(i) + w.c), 16)
                ref = self.sq.at[2 * self.pair + k, pl.ds(row, 96), :]
                self.e.append(w.to_core(ref, ref))

    def finish(self):
        received(self.e)


class WideGather:
    def __init__(self, wire, ex):
        self.w, self.ex = wire, ex

    def part(self, z, pb, begin, size):
        row = pl.multiple_of(96 * (2 * z + self.w.c), 16)
        lane = pl.multiple_of(WIDTH * pb + begin, 128)
        return self.ex.at[pl.ds(row, 96), pl.ds(lane, size)]

    start, plane, relay = PairGather.start, PairGather.plane, PairGather.relay

    def core(self):
        w = self.w
        received(self.d)
        self.e = []
        for i in (1, 2, 3):
            ref = self.ex.at[pl.ds(pl.multiple_of(96 * (2 * w.zpeer(i) + w.c), 16), 96), :]
            self.e.append(w.to_core(ref, ref))

    finish = PairGather.finish


class PlaneRows:
    def __init__(self, wire, ref):
        self.w, self.ref = w, ref = wire, ref
        src = ref.at[w.c, w.pb]
        self.a = [w.remote(src, src, side, w.pa) for side in (w.xside(), w.yside())]

    def relay(self):
        w = self.w
        received(self.a)
        half = self.ref.shape[3] // 2
        self.a = []
        for k, side, out in ((0, w.xside(), w.yside()), (1, w.yside(), w.xside())):
            src = self.ref.at[w.c, side, :, pl.ds(half * k, half)]
            self.a.append(w.remote(src, src, out, w.pa))

    def core(self):
        received(self.a)
        src = self.ref.at[self.w.c]
        self.b = [self.w.to_core(src, src)]

    def finish(self):
        received(self.b)


class PlaneSmall(PlaneRows):
    def __init__(self, wire, ref):
        self.w, self.ref = wire, ref
        src = ref.at[wire.c, wire.pb]
        self.a = wire.to_plane(lambda t: src, lambda j: src)


class CrossReduce:
    def __init__(self, wire, refs):
        self.w, self.refs = wire, refs

    def core(self):
        w, (w1, r1, w2, r2, w3, r3, w4) = self.w, self.refs
        row = pl.multiple_of(384 * (1 - w.c), 16)
        self.a = w.to_core(w1.at[pl.ds(row, 384), :], r1)

    def plane(self):
        w, (w1, r1, w2, r2, w3, r3, w4) = self.w, self.refs
        self.a.wait_recv()
        for k in range(4):
            row = pl.multiple_of(384 * w.c + 96 * k, 16)
            t = w1[pl.ds(row, 96), :].astype(F32) + r1[96 * k : 96 * (k + 1), :].astype(F32)
            w2[k] = lowered(t)
        self.b = w.to_plane(lambda t: w2.at[t], lambda j: r2.at[j - 1])

    def line(self):
        w, (w1, r1, w2, r2, w3, r3, w4) = self.w, self.refs
        received(self.b)
        t = w2[w.pb].astype(F32)
        for j in range(3):
            t = t + r2[j].astype(F32)
        for j, part in enumerate(split4(t)):
            w3[j] = lowered(part)
        self.d = w.to_z(lambda t: w3.at[t], lambda j: r3.at[j - 1])

    def spread(self):
        w, (w1, r1, w2, r2, w3, r3, w4) = self.w, self.refs
        received(self.d)
        t = w3[w.z].astype(F32)
        for j in range(3):
            t = t + r3[j].astype(F32)
        w4[w.c, w.pb] = lowered(t)
        self.rows = PlaneRows(w, w4)

    def result(self):
        w4 = self.refs[-1]
        t = w4[...].astype(F32).reshape(WIDTH, 256)
        t = lax.select(self.w.c == 1, pltpu.roll(t, 160, 1), t)[:, :128]
        return lowered(t.T[:96])


def inputs_half(a, c):
    t = a.astype(F32).reshape(384, 256)
    t = lax.select(c == 1, pltpu.roll(t, 160, 1), t)[:, :128]
    return lowered(t.T)


def layer(*refs):
    names = (*IN_KIND, *OUT_KIND)
    r = types.SimpleNamespace(**dict(zip(names, refs)))
    s = types.SimpleNamespace(**dict(zip(SCRATCH, refs[len(names) :])))
    w = Wire(refs[-1])
    pb, pa, z, c = w.pb, w.pa, w.z, w.c
    sq, ex, rd, enc = s.sq, s.ex, s.rd, s.enc

    barrier = pltpu.get_barrier_semaphore()
    for j in range(1, 8):
        pl.semaphore_signal(
            barrier, inc=1, device_id=(pb, lax.rem(pa + j, 8)), device_id_type=MESH
        )
    for j in (1, 2, 3):
        pl.semaphore_signal(barrier, inc=1, device_id=(w.ppeer(j), pa), device_id_type=MESH)

    squares = [r.wcq, r.wck, r.wcv, r.wco, r.wo, r.wq, r.wk, r.wv]
    own_rows = pl.ds(pl.multiple_of(96 * pa, 16), 96)
    red_rows = pl.ds(pl.multiple_of(384 * c, 16), 384)
    order = (SQ, SK, SV, CQ, CK, SO, CV, CO)
    held = {i: w.local(squares[i], sq.at[i, own_rows, :]) for i in order}
    held[EX] = w.local(r.wex, ex.at[own_rows, :])
    held[RD] = w.local(r.wre, rd.at[red_rows, :])
    held[EN] = w.local(r.enc_h, enc)

    for dst, src in ((s.xs, r.x), (s.ogs, r.og)):
        dst[...] = jnp.zeros((OWN, WIDTH), F32)
        for k in (0, 1):
            dst[PAD * k : PAD * k + ANS, :] = lax.select(c == 1, src[:, 2 + k, :], src[:, k, :])
    s.bks[...] = jnp.zeros((PAD, PAD), jnp.int32)
    s.bks[:ANS, :ANS] = r.buckets[...]
    g1, g2, g3 = [ref[...].reshape(1, WIDTH) for ref in (r.g1, r.g2, r.g3)]
    x = s.xs[...]
    rs1 = lax.rsqrt(jnp.mean(x * x, -1, keepdims=True) + epsilon)
    h1z = choose(split4(x * rs1 * g1), z)
    xz = choose(split4(x), z)
    h1b = lowered(h1z)
    s.p6[c, pb, :, 2304:2560] = h1b
    s.p1[c, pb] = lowered(s.ogs[...])

    pl.semaphore_wait(barrier, 10)
    other = {}
    for i in order:
        other[i] = w.to_core(squares[i], sq.at[i, own_rows, :])
    other[RD] = w.to_core(r.wre, rd.at[red_rows, :])
    other[EX] = w.to_core(r.wex, ex.at[own_rows, :])
    gather_a, gather_b, gather_c = PairGather(w, sq, 0), PairGather(w, sq, 1), WideGather(w, ex)

    def chip(i):
        return sq[i, pl.ds(pl.multiple_of(PART * z, 16), PART), :]

    parts = []
    for i in (SQ, SK, SV):
        held[i].wait()
        other[i].wait_recv()
        parts.append(split4(nn(h1b[:, :PART], chip(i))))
    blocks = [join3([parts[k][j] for k in range(3)]) for j in range(4)]
    for j in range(4):
        s.s1[j] = lowered(blocks[j])
    own_qkv = choose(blocks, z)
    f1 = w.to_z(lambda t: s.s1.at[t], lambda j: s.r1.at[j - 1])
    held[CQ].wait()
    held[CK].wait()
    gather_a.start()
    held[CV].wait()
    held[CO].wait()
    gather_b.start()

    bucket = s.bks[...]

    def bias_head(h, carry):
        v = jnp.zeros((PAD, PAD), F32)
        for b in range(BUCKETS):
            v = jnp.where(bucket == b, r.table[3 * z + h, b], v)
        s.bias[pl.ds(pl.multiple_of(PAD * h, 8), PAD), :] = v
        return carry

    lax.fori_loop(0, 3, bias_head, 0)
    held[RD].wait()
    other[RD].wait_recv()
    s.gact[z] = lowered(nt(s.p1[c, pb], rd[...]))

    received(f1)
    v = own_qkv
    for j in range(3):
        v = v + s.r1[j].astype(F32)
    q3, k3, v3 = [lowered(t).astype(F32)[:, :PART] for t in part3(v)]

    def attend(stacked, keys, bias):
        i = lax.broadcasted_iota(jnp.int32, (PAD, PAD), 0)
        j = lax.broadcasted_iota(jnp.int32, (PAD, PAD), 1)
        seen = jnp.concatenate([(j <= i).astype(F32)] * 3, 0) > 0.5
        t = jnp.where(seen, nt(lowered(stacked), lowered(keys)) + bias, masked_score)
        t = jnp.exp(t - jnp.max(t, -1, keepdims=True))
        return t / jnp.sum(t, -1, keepdims=True)

    mixes, probs, stacks = [], [], []
    for k in (0, 1):
        rows = slice(PAD * k, PAD * (k + 1))
        stacks.append(stack_heads(q3[rows] * 0.125, 3))
        probs.append(attend(stacks[k], k3[rows], s.bias[...]))
        mixes.append(pick_heads(nn(lowered(probs[k]), lowered(v3[rows])), 3))
    mixb = lowered(jnp.concatenate(mixes, 0))
    s.p5[c, pb, :, 768:960] = mixb
    held[SO].wait()
    other[SO].wait_recv()
    parts = split4(nn(mixb, chip(SO)))
    for j in range(4):
        s.s2[j] = lowered(parts[j])
    own_o = choose(parts, z)
    f2 = w.to_z(lambda t: s.s2.at[t], lambda j: s.r2.at[j - 1])
    gather_a.plane()

    received(f2)
    r1z = xz + own_o
    for j in range(3):
        r1z = r1z + s.r2[j].astype(F32)
    counts = lanes(OWN, 256) < PART
    g2z = choose(split4(jnp.broadcast_to(g2, (OWN, WIDTH))), z)
    square = jnp.sum(jnp.where(counts, r1z * r1z, 0.0), -1, keepdims=True)
    high = lowered(square).astype(F32)
    tail = jnp.where(lanes(OWN, 256) < 224, high, square - high)
    s.ag2[pa] = lowered(jnp.where(counts, r1z * g2z, tail))
    f3 = w.to_column(lambda t: s.ag2.at[pa], lambda j: s.ag2.at[pa])
    gather_b.plane()
    held[EX].wait()
    gather_c.start()
    gather_a.relay()
    gather_a.core()

    received(f3)
    blocks = [[s.ag2[2 * j + k].astype(F32) for j in range(4)] for k in (0, 1)]
    rs2 = []
    for k in (0, 1):
        t = blocks[k][0] + blocks[k][1] + blocks[k][2] + blocks[k][3]
        lane = lanes(OWN, 256)
        t = jnp.sum(jnp.where((lane == 192) | (lane == 224), t, 0.0), -1, keepdims=True)
        rs2.append(lax.rsqrt(t * (1.0 / WIDTH) + epsilon))
    gather_b.relay()
    gather_a.finish()
    other[CQ].wait_recv()
    cq = jnp.zeros((ALL, WIDTH), F32)
    for j in range(4):
        t = jnp.concatenate([s.ag2[2 * j], s.ag2[2 * j + 1]], 0)[:, :PART]
        cq = cq + nn(t, sq[CQ, PART * j : PART * (j + 1), :])
    cq = cq * jnp.concatenate(rs2, 0)
    cq = lowered(cq).astype(F32) * 0.125
    other[CK].wait_recv()
    for p in range(6):
        t = jnp.concatenate([pair_stack(cq[PAD * q : PAD * (q + 1)], p) for q in range(4)], 0)
        s.x6[p] = lowered(t)
        t = lowered(nt(s.x6[p], sq[CK, :, 128 * p : 128 * (p + 1)]))
        for q in range(4):
            s.qk[q, 48 * p : 48 * (p + 1), :] = t[48 * q : 48 * (q + 1)]
    held[EN].wait()
    s.stat[...] = jnp.zeros((384, 128), F32)

    def scores(q, carry):
        size = r.plen[q]
        per = lax.select(size <= SLOT // 2, 2, 1)
        kept = jnp.minimum(jnp.maximum(r.pcount[q] - pa * per, 0), per) * size
        valid = lanes(ROWS, SLOT) < kept
        t = jnp.where(valid, nt(s.qk[q], enc[q]), masked_score)
        top = jnp.max(t, -1, keepdims=True)
        t = jnp.where(valid, jnp.exp(t - top), 0.0)
        total = jnp.sum(t, -1, keepdims=True)
        s.es[q] = lowered(t)
        s.bs[q] = lowered(nn(s.es[q], enc[q]))
        lane = lanes(ROWS, 128)
        old = s.stat[:ROWS, :]
        s.stat[:ROWS, :] = jnp.where(lane == q, top, jnp.where(lane == 4 + q, total, old))
        return carry

    lax.fori_loop(0, 4, scores, 0)
    s.stg[pa] = s.stat[...].T[:8]
    f5 = w.to_column(lambda t: s.stg.at[pa], lambda j: s.stg.at[pa])
    gather_b.core()
    gather_c.plane()
    gather_b.finish()
    other[CV].wait_recv()
    low = lanes(PAD, 128) < SIZE
    tiles = [[] for q in range(4)]
    for p in range(6):
        t = jnp.concatenate([s.bs[q, 48 * p : 48 * (p + 1), :] for q in range(4)], 0)
        t = nn(t, sq[CV, :, 128 * p : 128 * (p + 1)])
        for q in range(4):
            a = t[48 * q : 48 * (q + 1)]
            tiles[q].append(jnp.where(low, a[:PAD], a[PAD:]))
    num = jnp.concatenate([jnp.concatenate(tiles[q], 1) for q in range(4)], 0)
    for k in (0, 1):
        for j, part in enumerate(split4(num[OWN * k : OWN * (k + 1)])):
            s.s5[k, j] = lowered(part)
    f5 += w.to_column(lambda t: s.s5.at[lax.rem(t, 2), t // 2], lambda j: s.r5.at[pa])
    s.r5[pa] = s.s5[c, z]
    gact_copies = w.to_z(lambda t: s.gact.at[z], lambda j: s.gact.at[z])
    rows1 = PlaneRows(w, s.p1)
    r1full = join4(blocks_of(s.ag2, c)) / g2
    rs2o = lax.select(c == 1, rs2[1], rs2[0])
    n2 = r1full * rs2o
    s.p4[c, pb, :, 768:1024] = lowered(choose(split4(n2 * g2), z))

    received(f5)
    stats = [s.stg[k] for k in range(8)]
    top = stats[0]
    for k in range(1, 8):
        top = jnp.maximum(top, stats[k])
    scale = [jnp.exp(t - top) for t in stats]
    total = jnp.zeros((8, 384), F32)
    for k in range(8):
        total = total + scale[k] * pltpu.roll(stats[k], 4, 0)
    inverse = 1.0 / total
    s.wrow[...] = jnp.zeros((128, 384), F32)
    mine = jnp.zeros((8, 384), F32)
    for k in range(8):
        t = scale[k] * inverse
        mine = lax.select(pa == k, t, mine)
        s.wrow[2 * k : 2 * k + 2, :] = lax.select(c == 1, t[2:4], t[0:2])
    s.wrow[16:20, :] = mine[0:4]
    s.wcol[...] = s.wrow[...].T
    w3 = s.wcol[pl.ds(pl.multiple_of(3 * PAD * z, 8), 3 * PAD), :]
    lane = lanes(PAD, 256)
    sums = [jnp.zeros((PAD, 256), F32) for k in (0, 1)]
    for m in range(8):
        block = s.r5[m].astype(F32)
        for k in (0, 1):
            col = [w3[PAD * h : PAD * (h + 1), 2 * m + k : 2 * m + k + 1] for h in range(3)]
            t = jnp.where(lane < 64, col[0], jnp.where(lane < 128, col[1], col[2]))
            sums[k] = sums[k] + t * block[PAD * k : PAD * (k + 1)]
    mixc = lowered(jnp.concatenate(sums, 0))
    s.mixg[c, z] = mixc
    s.p3[c, pb, :, 768:1024] = mixc
    f6 = w.to_z(lambda t: s.mixg.at[c, z], lambda j: s.mixg.at[c, z])
    gather_c.relay()
    gather_c.core()
    other[CO].wait_recv()
    received(f6)
    mix_core = w.to_core(s.mixg.at[c], s.mixg.at[c])
    after = jnp.zeros((OWN, WIDTH), F32)
    for j in range(4):
        after = after + nn(s.mixg[c, j][:, :PART], sq[CO, PART * j : PART * (j + 1), :])
    r2z = r1z + choose(split4(after), z)
    resid = r1full + after
    rs3 = lax.rsqrt(jnp.mean(resid * resid, -1, keepdims=True) + epsilon)
    n3 = resid * rs3
    h3 = lowered(n3 * g3)
    s.p2[c, pb, :, 3072:3328] = lowered(choose(split4(n3 * g3), z))
    received(gact_copies)
    gather_c.finish()
    other[EX].wait_recv()
    gh3 = jnp.zeros((OWN, WIDTH), F32)
    for j in range(4):
        cols = slice(WIDTH * j, WIDTH * (j + 1))
        v = nn(h3, ex[:, cols])
        t = jnp.tanh(GELU_A * (v + GELU_B * v * v * v))
        act = lowered(0.5 * v * (1.0 + t))
        slope = 0.5 * (1.0 + t) + 0.5 * v * (1.0 - t * t) * GELU_A * (1.0 + 3.0 * GELU_B * v * v)
        gp = lowered(s.gact[j].astype(F32) * slope)
        s.p2[c, pb, :, cols] = gp

        @pl.when(z == j)
        def keep():
            s.p2[c, pb, :, 3328:4096] = act

        gh3 = gh3 + nt(gp, ex[:, cols])
    og = s.ogs[...]
    gain3 = jnp.sum(gh3 * n3, 0, keepdims=True)
    t = gh3 * g3
    grad_two = og + rs3 * (t - n3 * jnp.mean(t * n3, -1, keepdims=True))
    gcb = lowered(grad_two)
    s.p3[c, pb, :, :768] = gcb
    s.gm[c] = lowered(nt(gcb, sq[CO]))
    f7 = w.to_core(s.gm.at[c], s.gm.at[c])
    rows1.relay()
    rows3 = PlaneRows(w, s.p3)
    rows2 = PlaneRows(w, s.p2)
    mix_core.wait_recv()
    f7.wait_recv()

    gms = [s.gm[k].astype(F32) for k in (0, 1)]
    mxs = [join4([s.mixg[k, j].astype(F32) for j in range(4)]) for k in (0, 1)]
    gm_q = [gms[q // 2][PAD * (q % 2) : PAD * (q % 2 + 1)] for q in range(4)]
    mx_q = [mxs[q // 2][PAD * (q % 2) : PAD * (q % 2 + 1)] for q in range(4)]
    tots = [[] for q in range(4)]
    for p in range(6):
        blocks_p = []
        for q in range(4):
            col = s.wcol[48 * p : 48 * (p + 1), 16 + q : 17 + q]
            y = pair_stack(gm_q[q], p) * col
            m = mx_q[q][:, 128 * p : 128 * (p + 1)]
            tots[q].append(-jnp.sum(y * jnp.concatenate([m, m], 0), -1, keepdims=True))
            blocks_p.append(y)
        s.y6[p] = lowered(jnp.concatenate(blocks_p, 0))
        t = lowered(nt(s.y6[p], sq[CV, :, 128 * p : 128 * (p + 1)]))
        for q in range(4):
            s.gv[q, 48 * p : 48 * (p + 1), :] = t[48 * q : 48 * (q + 1)]
    lane = lanes(ROWS, 128)
    t = jnp.zeros((ROWS, 128), F32)
    for q in range(4):
        t = jnp.where(lane == q, jnp.concatenate(tots[q], 0), t)
    s.tot[...] = t
    for p in range(6):
        t = jnp.concatenate([s.bs[q, 48 * p : 48 * (p + 1), :] for q in range(4)], 0)
        s.vw1[128 * p : 128 * (p + 1), :] = lowered(tn(s.y6[p], t))
    vred = CrossReduce(w, [s.vw1, s.vr1, s.vw2, s.vr2, s.vw3, s.vr3, s.vw4])
    vred.core()

    def grads(q, carry):
        pick = lanes(ROWS, 128) == q
        tot = jnp.sum(jnp.where(pick, s.tot[...], 0.0), -1, keepdims=True)
        t = nt(s.gv[q], enc[q]) + tot
        s.gs[q] = lowered(s.es[q].astype(F32) * t)
        s.as_[q] = lowered(nn(s.gs[q], enc[q]))
        return carry

    lax.fori_loop(0, 4, grads, 0)
    tiles = [[] for q in range(4)]
    for p in range(6):
        t = jnp.concatenate([s.as_[q, 48 * p : 48 * (p + 1), :] for q in range(4)], 0)
        t = nn(t, sq[CK, :, 128 * p : 128 * (p + 1)])
        for q in range(4):
            a = t[48 * q : 48 * (q + 1)]
            tiles[q].append(jnp.where(low, a[:PAD], a[PAD:]))
    num = jnp.concatenate([jnp.concatenate(tiles[q], 1) for q in range(4)], 0) * 0.125
    for k in (0, 1):
        for j, part in enumerate(split4(num[OWN * k : OWN * (k + 1)])):
            s.s7[k, j] = lowered(part)
    f8 = w.to_column(lambda t: s.s7.at[lax.rem(t, 2), t // 2], lambda j: s.r7.at[pa])
    s.r7[pa] = s.s7[c, z]
    vred.plane()
    for p in range(6):
        t = jnp.concatenate([s.as_[q, 48 * p : 48 * (p + 1), :] for q in range(4)], 0)
        s.kw1[128 * p : 128 * (p + 1), :] = lowered(tn(s.x6[p], t))
    kred = CrossReduce(w, [s.kw1, s.kr1, s.kw2, s.kr2, s.kw3, s.kr3, s.kw4])
    kred.core()
    rows3.relay()
    rows2.relay()
    rows1.core()
    out_copies = []

    def encoding_grad(q):
        s.eg[q] = lowered(tn(s.es[q], s.gv[q]) + tn(s.gs[q], s.qk[q]))
        out_copies.append(w.local(s.eg.at[q], r.encoding_grad.at[q]))

    encoding_grad(0)
    encoding_grad(1)

    received(f8)
    t = s.r7[0].astype(F32)
    for k in range(1, 8):
        t = t + s.r7[k].astype(F32)
    s.gcq[z] = lowered(t)
    f9 = w.to_z(lambda t: s.gcq.at[z], lambda j: s.gcq.at[z])
    kred.plane()
    rows3.core()
    parts = split4(nn(s.p2[c, pb, :, 3328:4096], rd[...]))
    for j in range(4):
        s.s8[j] = lowered(parts[j])
    own_d = choose(parts, z)
    fo = w.to_z(lambda t: s.s8.at[t], lambda j: s.r8.at[j - 1])
    encoding_grad(2)
    encoding_grad(3)

    received(f9)
    gcq = lowered(join4([s.gcq[j].astype(F32) for j in range(4)]))
    s.p4[c, pb, :, :768] = gcq
    rows4 = PlaneRows(w, s.p4)
    gh2 = nt(gcq, sq[CQ])
    gain2 = jnp.sum(gh2 * n2, 0, keepdims=True)
    t = gh2 * g2
    grad_one = grad_two + rs2o * (t - n2 * jnp.mean(t * n2, -1, keepdims=True))
    gab = lowered(grad_one)
    s.p5[c, pb, :, :768] = gab
    rows5 = PlaneRows(w, s.p5)
    gsm = lowered(nt(gab, chip(SO))).astype(F32)
    gsum = jnp.zeros((3 * PAD, PAD), F32)
    dq, dk, dv = [], [], []
    for k in (0, 1):
        rows = slice(PAD * k, PAD * (k + 1))
        prob = probs[k]
        stacked = lowered(stack_heads(gsm[rows], 3))
        gw = nt(stacked, lowered(v3[rows]))
        gsb = lowered(prob * (gw - jnp.sum(gw * prob, -1, keepdims=True)))
        gsum = gsum + gsb.astype(F32)
        dq.append(pick_heads(nn(gsb, lowered(k3[rows])), 3) * 0.125)
        dk.append(tn(gsb, lowered(stacks[k])))
        dv.append(tn(lowered(prob), stacked))
    gap = jnp.zeros((OWN, 64), F32)
    three = [jnp.concatenate([jnp.concatenate(t, 0), gap], 1) for t in (dq, dk, dv)]
    s.gsg[z] = lowered(join3(three))
    f10 = w.to_z(lambda t: s.gsg.at[z], lambda j: s.gsg.at[z])
    s.bias[...] = gsum

    def table_head(h, carry):
        v = s.bias[pl.ds(pl.multiple_of(PAD * h, 8), PAD), :]
        rows = [jnp.sum(jnp.where(bucket == b, v, 0.0), 0, keepdims=True) for b in range(BUCKETS)]
        col = jnp.sum(jnp.concatenate(rows, 0), -1, keepdims=True)
        return jnp.where(lanes(BUCKETS, 128) == 3 * z + h, col, carry)

    s.stz[z] = lax.fori_loop(0, 3, table_head, jnp.zeros((BUCKETS, 128), F32))
    ft = w.to_z(lambda t: s.stz.at[z], lambda j: s.stz.at[z])
    rows2.core()
    vred.line()
    received(fo)
    t = r2z + own_d
    for j in range(3):
        t = t + s.r8[j].astype(F32)
    s.dog[pa] = lowered(t)
    fg = w.to_column(lambda t: s.dog.at[pa], lambda j: s.dog.at[pa])
    rows1.finish()

    def half_product(ref, begin, index, rows):
        rows.finish()
        lhs = inputs_half(ref[:, :, :, begin : begin + 256], c)
        s.wg[index] = lowered(nn(lhs, ref[:, :, :, :768].reshape(384, WIDTH))[:96])
        out_copies.append(w.local(s.wg.at[index], r.squares.at[index]))

    half_product(s.p3, 768, 7, rows3)

    received(f10)
    unpacked = [part3(s.gsg[j].astype(F32)) for j in range(4)]
    three = [lowered(join4([unpacked[j][k] for j in range(4)])) for k in range(3)]
    for k in range(3):
        s.p6[c, pb, :, 768 * k : 768 * (k + 1)] = three[k]
    rows6 = PlaneRows(w, s.p6)
    gh1 = nt(three[0], chip(SQ)) + nt(three[1], chip(SK)) + nt(three[2], chip(SV))
    g1z = choose(split4(jnp.broadcast_to(g1, (OWN, WIDTH))), z)
    s.tg[z] = lowered(jnp.concatenate([gh1 * g1z[:, :PART], gap], 1))
    f11 = w.to_z(lambda t: s.tg.at[z], lambda j: s.tg.at[z])
    received(ft)
    s.stab[c, pb] = s.stz[0] + s.stz[1] + s.stz[2] + s.stz[3]
    tab_rows = PlaneSmall(w, s.stab)
    kred.line()
    rows4.relay()
    rows5.relay()
    vred.spread()
    rows2.finish()
    p2 = s.p2
    lhs = inputs_half(p2[:, :, :, 3072:3328], c)
    for j in range(4):
        cols = slice(WIDTH * j, WIDTH * (j + 1))
        s.gexs[:, cols] = lowered(nn(lhs, p2[:, :, :, cols].reshape(384, WIDTH))[:96])
    out_copies.append(w.local(s.gexs, r.gex))
    received(f11)
    t = join4([s.tg[j].astype(F32) for j in range(4)])
    n1 = s.xs[...] * rs1
    gain1 = jnp.sum(t * n1, 0, keepdims=True) / g1
    s.dgr[c] = grad_one + rs1 * (t - n1 * jnp.mean(t * n1, -1, keepdims=True))
    fd = w.to_core(s.dgr.at[c], s.dgr.at[c])
    s.sgain[c, pb] = jnp.concatenate([gain1, gain2, gain3, jnp.zeros((5, WIDTH), F32)], 0)
    gain_rows = PlaneSmall(w, s.sgain)
    rows6.relay()
    kred.spread()
    vred.rows.relay()
    rows4.core()
    rows5.core()
    half = pl.ds(pl.multiple_of(3328 + 384 * c, 128), 384)
    lhs = lowered(p2[:, :, :, half].astype(F32).reshape(384, 384).T)
    s.gres[...] = lowered(nn(lhs, s.p1[...].reshape(384, WIDTH)))
    out_copies.append(w.local(s.gres, r.gre))
    half_product(s.p4, 768, 4, rows4)
    half_product(s.p5, 768, 3, rows5)
    vred.rows.core()
    kred.rows.relay()
    tab_rows.core()
    gain_rows.core()
    received(fg)
    fd.wait_recv()
    for k in (0, 1):
        t = join4([s.dog[2 * j + k].astype(F32) for j in range(4)])
        for m in (0, 1):
            r.decoder_out[:, 2 * k + m, :] = t[PAD * m : PAD * m + ANS]
            r.decoder_grad[:, 2 * k + m, :] = s.dgr[k, PAD * m : PAD * m + ANS, :]
    rows6.core()
    kred.rows.core()
    vred.rows.finish()
    s.wg[6] = vred.result()
    out_copies.append(w.local(s.wg.at[6], r.squares.at[6]))
    gain_rows.finish()
    tab_rows.finish()
    t = s.sgain[0, 0]
    u = s.stab[0, 0]
    for k in range(1, 8):
        t = t + s.sgain[k // 4, k % 4]
        u = u + s.stab[k // 4, k % 4]
    r.gains[...] = t
    r.table_grad[...] = u
    kred.rows.finish()
    s.wg[5] = kred.result()
    out_copies.append(w.local(s.wg.at[5], r.squares.at[5]))
    rows6.finish()
    ref = s.p6
    lhs = inputs_half(ref[:, :, :, 2304:2560], c)
    for k in range(3):
        s.wg[k] = lowered(nn(lhs, ref[:, :, :, 768 * k : 768 * (k + 1)].reshape(384, WIDTH))[:96])
        out_copies.append(w.local(s.wg.at[k], r.squares.at[k]))
    for copy in out_copies:
        copy.wait()
    for copy in w.sent:
        copy.wait_send()


def blocks_of(ref, c):
    return [ref[2 * j + c].astype(F32) for j in range(4)]


def write(dout, dgrad, eg, sq, gex, gre, gains, table, *refs):
    outs, (veg, vsq, vex, vre, weg, wsq, wex, wre, sems) = refs[:17], refs[17:]
    o_out, o_grad, o_eg, outs = outs[0], outs[1], outs[2], outs[3:]
    jobs = [(eg.at[q], veg.at[q], weg.at[q], o_eg.at[q]) for q in range(4)]
    jobs += [(gex, vex, wex, outs[8]), (gre, vre, wre, outs[9])]
    jobs += [(sq.at[k], vsq.at[k], wsq.at[k], outs[k]) for k in range(8)]
    loads = [pltpu.make_async_copy(j[0], j[1], sems.at[k]) for k, j in enumerate(jobs)]
    for copy in loads:
        copy.start()
    o_out[...] = dout[...]
    o_grad[...] = dgrad[...]
    for k in range(3):
        outs[10 + k][...] = gains[k : k + 1, :].reshape(WIDTH)
    outs[13][...] = table[...].T[:HEADS]
    stores = []
    for k, (src, near, wide, dst) in enumerate(jobs):
        loads[k].wait()
        wide[...] = near[...].astype(F32)
        stores.append(pltpu.make_async_copy(wide, dst, sems.at[len(jobs) + k]))
        stores[-1].start()
    for copy in stores:
        copy.wait()


def fused(x, enc, og, plen, pcount, buckets, wq, wk, wv, wo, wcq, wck, wcv, wco, wex, wre, g1, g2, g3, table):
    def shape(*dims, kind=F32):
        return jax.ShapeDtypeStruct(dims, kind)

    rows = shape(ANS, 4, WIDTH)
    mid = pl.pallas_call(
        layer,
        out_shape=[
            rows,
            rows,
            shape(4, SLOT, WIDTH, kind=BF),
            shape(8, 96, WIDTH, kind=BF),
            shape(96, FF, kind=BF),
            shape(384, WIDTH, kind=BF),
            shape(8, WIDTH),
            shape(BUCKETS, 128),
        ],
        in_specs=[pl.BlockSpec(memory_space=k) for k in IN_KIND.values()],
        out_specs=[pl.BlockSpec(memory_space=k) for k in OUT_KIND.values()],
        scratch_shapes=[pltpu.VMEM(*v) for v in SCRATCH.values()]
        + [pltpu.SemaphoreType.DMA((SEMAPHORES,))],
        compiler_params=pltpu.CompilerParams(
            collective_id=0, has_side_effects=True, vmem_limit_bytes=62 * 2**20
        ),
    )(
        jnp.transpose(x, (1, 0, 2)),
        jnp.transpose(og, (1, 0, 2)),
        *(plen, pcount, buckets, table.T, g1, g2, g3, enc),
        *(wq, wk, wv, wo, wcq, wck, wcv, wco, wex, wre),
    )
    near, far = pl.BlockSpec(memory_space=NEAR), pl.BlockSpec(memory_space=FAR)
    square = shape(96, WIDTH)
    out = pl.pallas_call(
        write,
        out_shape=[
            *(rows, rows, shape(4, SLOT, WIDTH)),
            *[square] * 8,
            *(shape(96, FF), shape(384, WIDTH)),
            *[shape(WIDTH)] * 3,
            shape(HEADS, BUCKETS),
        ],
        in_specs=[near, near, far, far, far, far, near, near],
        out_specs=[near, near, far, *[far] * 10, *[near] * 4],
        scratch_shapes=[
            pltpu.VMEM(dims, kind)
            for kind in (BF, F32)
            for dims in ((4, SLOT, WIDTH), (8, 96, WIDTH), (96, FF), (384, WIDTH))
        ]
        + [pltpu.SemaphoreType.DMA((28,))],
        compiler_params=pltpu.CompilerParams(vmem_limit_bytes=62 * 2**20),
    )(*mid)
    out = list(out)
    out[0], out[1] = (jnp.transpose(v, (1, 0, 2)) for v in out[:2])
    out[16] = out[16].T
    return tuple(out)


def solution(mesh):
    if dict(mesh.shape) != {"pb": 4, "pa": 8}:
        return generic(mesh)
    wide, tall = P("pb", "pa", None), P("pa", None)
    rows, whole = P("pb", None, None), P()
    return jax.shard_map(
        fused,
        mesh=mesh,
        in_specs=(rows, wide, rows, P("pb"), P("pb"), whole, *[tall] * 10, *[whole] * 4),
        out_specs=(rows, rows, wide, *[tall] * 10, *[whole] * 4),
        check_vma=False,
    )
```

```python
import math
import types

import jax
import jax.numpy as jnp
from jax import lax
from jax.experimental import pallas as pl
from jax.experimental.pallas import tpu as pltpu
from jax.sharding import PartitionSpec as P

epsilon = 1e-06
highest = lax.Precision.HIGHEST
masked_score = -1e30


def product(left, right):
    return jnp.dot(left, right, preferred_element_type=jnp.float32)


def lowered(value):
    return value.astype(jnp.bfloat16)


def norm_forward(value):
    factor = lax.rsqrt(jnp.mean(value * value, -1, keepdims=True) + epsilon)
    return (value * factor, factor)


def norm_backward(grad_out, normal, factor, gain):
    inner_term = grad_out * gain
    grad_in = factor * (inner_term - normal * jnp.mean(inner_term * normal, -1, keepdims=True))
    grad_gain = jnp.sum(grad_out * normal, (0, 1))
    return (grad_in, grad_gain)


def activate(value):
    return jax.nn.gelu(value, approximate=True)


def shard_grad(inputs, grad_rows, device_place, row_count):
    sliced = lax.dynamic_slice_in_dim(inputs, device_place * row_count, row_count, 2)
    return jnp.einsum("qak,qae->ke", sliced, grad_rows, preferred_element_type=jnp.float32)


def shards(
    decoder_in,
    encodings,
    out_grad,
    passage_len,
    passage_count,
    buckets,
    self_query,
    self_key,
    self_value,
    self_out,
    cross_query,
    cross_key,
    cross_value,
    cross_out,
    ffn_expand,
    ffn_reduce,
    norm_self,
    norm_cross,
    norm_ffn,
    bias_table,
):
    wide_count = lax.axis_size("pa")
    device_place = lax.axis_index("pa")
    stacked = jnp.stack(
        [self_query, self_key, self_value, self_out, cross_query, cross_key, cross_value, cross_out]
    )
    squares, expand_full, reduce_full = (
        lax.all_gather(stacked, "pa", axis=1, tiled=True),
        lax.all_gather(ffn_expand, "pa", axis=0, tiled=True),
        lax.all_gather(ffn_reduce, "pa", axis=0, tiled=True),
    )
    query_self = squares[0]
    key_self = squares[1]
    value_self = squares[2]
    out_self = squares[3]
    query_cross = squares[4]
    key_cross = squares[5]
    value_cross = squares[6]
    out_cross = squares[7]
    questions, answer, model_width = decoder_in.shape
    head_count = bias_table.shape[1]
    head_size = model_width // head_count
    factor = head_size ** (-0.5)
    slot_rows = encodings.shape[1]
    rows_model = model_width // wide_count
    rows_hidden = expand_full.shape[1] // wide_count

    def heads_of(value):
        return value.reshape(value.shape[0], value.shape[1], head_count, head_size)

    normal_one, factor_one = norm_forward(decoder_in)
    hidden_one = lowered(normal_one * norm_self)
    query_heads = heads_of(lowered(product(hidden_one, query_self)))
    key_heads = heads_of(lowered(product(hidden_one, key_self)))
    value_heads = heads_of(lowered(product(hidden_one, value_self)))
    onehot = (buckets[:, :, None] == jnp.arange(bias_table.shape[0])[None, None, :]).astype(
        jnp.float32
    )
    bias_scores = jnp.einsum("ijb,bh->hij", onehot, bias_table, precision=highest)
    causal = jnp.arange(answer)[:, None] >= jnp.arange(answer)[None, :]
    scores = (
        jnp.einsum("qihd,qjhd->qhij", query_heads, key_heads, preferred_element_type=jnp.float32)
        * factor
        + bias_scores[None]
    )
    scores = jnp.where(causal[None, None], scores, masked_score)
    probabilities = jax.nn.softmax(scores, -1)
    weights_self = lowered(probabilities)
    mixed_self = lowered(
        jnp.einsum("qhij,qjhd->qihd", weights_self, value_heads, preferred_element_type=jnp.float32)
    ).reshape(questions, answer, model_width)
    resid_one = decoder_in + product(mixed_self, out_self)
    normal_two, factor_two = norm_forward(resid_one)
    hidden_two = lowered(normal_two * norm_cross)
    cquery = heads_of(lowered(product(hidden_two, query_cross)))
    per_device = slot_rows // passage_len
    held_count = jnp.clip(passage_count - device_place * per_device, 0, per_device)
    valid_rows = jnp.arange(slot_rows)[None, :] < (held_count * passage_len)[:, None]

    def project(encoded):
        ckeys = lowered(product(encoded, key_cross)).reshape(
            questions, slot_rows, head_count, head_size
        )
        cvalues = lowered(product(encoded, value_cross)).reshape(
            questions, slot_rows, head_count, head_size
        )
        cscores = (
            jnp.einsum("qihd,qjhd->qhij", cquery, ckeys, preferred_element_type=jnp.float32)
            * factor
        )
        cscores = jnp.where(valid_rows[:, None, None, :], cscores, masked_score)
        return (ckeys, cvalues, cscores)

    ckeys, cvalues, cscores = project(encodings)
    row_max = lax.pmax(jnp.max(cscores, -1), "pa")
    exp_weights = jnp.exp(cscores - row_max[..., None])
    part_num = jnp.einsum(
        "qhij,qjhd->qihd", lowered(exp_weights), cvalues, preferred_element_type=jnp.float32
    )
    part_total = jnp.sum(exp_weights, -1)
    numerator, totals = lax.psum((part_num, part_total), "pa")
    totals_t = jnp.transpose(totals, (0, 2, 1))[..., None]
    mixed_cross = lowered(numerator / totals_t).reshape(questions, answer, model_width)
    resid_two = resid_one + product(mixed_cross, out_cross)
    normal_three, factor_three = norm_forward(resid_two)
    hidden_three = lowered(normal_three * norm_ffn)
    pre_act = product(hidden_three, expand_full)
    activation = lowered(activate(pre_act))
    decoder_out = resid_two + product(activation, reduce_full)
    grad_z = lowered(out_grad)
    grad_reduce = shard_grad(activation, grad_z, device_place, rows_hidden)
    grad_act = jnp.einsum("qae,fe->qaf", grad_z, reduce_full, preferred_element_type=jnp.float32)
    unused_out, gelu_back = jax.vjp(activate, pre_act)
    grad_pre = lowered(gelu_back(grad_act)[0])
    grad_expand = shard_grad(hidden_three, grad_pre, device_place, rows_model)
    grad_three = jnp.einsum(
        "qaf,kf->qak", grad_pre, expand_full, preferred_element_type=jnp.float32
    )
    back_term, grad_gain_ffn = norm_backward(grad_three, normal_three, factor_three, norm_ffn)
    grad_two = out_grad + back_term
    grad_c = lowered(grad_two)
    grad_out_cross = shard_grad(mixed_cross, grad_c, device_place, rows_model)
    grad_mix = heads_of(
        lowered(jnp.einsum("qae,ke->qak", grad_c, out_cross, preferred_element_type=jnp.float32))
    )
    grad_mix_wide = grad_mix.astype(jnp.float32)
    grad_num = lowered(grad_mix_wide / totals_t)
    grad_tot = -jnp.sum(grad_mix_wide * numerator, -1) / (totals_t[..., 0] * totals_t[..., 0])
    ckeys, cvalues, cscores = project(encodings)
    exp_weights = jnp.exp(cscores - row_max[..., None])
    grad_expo = jnp.einsum("qihd,qjhd->qhij", grad_num, cvalues, preferred_element_type=jnp.float32)
    grad_expo = grad_expo + jnp.transpose(grad_tot, (0, 2, 1))[..., None]
    grad_score = lowered(exp_weights * grad_expo)
    part_query = (
        jnp.einsum("qhij,qjhd->qihd", grad_score, ckeys, preferred_element_type=jnp.float32)
        * factor
    )
    grad_cquery = lowered(lax.psum(part_query, "pa")).reshape(questions, answer, model_width)
    grad_ckeys = lowered(
        jnp.einsum("qhij,qihd->qjhd", grad_score, cquery, preferred_element_type=jnp.float32)
        * factor
    ).reshape(questions, slot_rows, model_width)
    grad_cvalues = lowered(
        jnp.einsum(
            "qhij,qihd->qjhd", lowered(exp_weights), grad_num, preferred_element_type=jnp.float32
        )
    ).reshape(questions, slot_rows, model_width)
    encoding_grad = jnp.einsum(
        "qse,ke->qsk", grad_ckeys, key_cross, preferred_element_type=jnp.float32
    )
    encoding_grad = encoding_grad + jnp.einsum(
        "qse,ke->qsk", grad_cvalues, value_cross, preferred_element_type=jnp.float32
    )
    full_key = jnp.einsum("qsk,qse->ke", encodings, grad_ckeys, preferred_element_type=jnp.float32)
    full_value = jnp.einsum(
        "qsk,qse->ke", encodings, grad_cvalues, preferred_element_type=jnp.float32
    )
    grad_query_cross = shard_grad(hidden_two, grad_cquery, device_place, rows_model)
    grad_hidden_two = jnp.einsum(
        "qae,ke->qak", grad_cquery, query_cross, preferred_element_type=jnp.float32
    )
    back_term, grad_gain_cross = norm_backward(grad_hidden_two, normal_two, factor_two, norm_cross)
    grad_one = grad_two + back_term
    grad_a = lowered(grad_one)
    grad_out_self = shard_grad(mixed_self, grad_a, device_place, rows_model)
    grad_smix = heads_of(
        lowered(jnp.einsum("qae,ke->qak", grad_a, out_self, preferred_element_type=jnp.float32))
    )
    grad_w = jnp.einsum(
        "qihd,qjhd->qhij", grad_smix, value_heads, preferred_element_type=jnp.float32
    )
    grad_s = lowered(probabilities * (grad_w - jnp.sum(grad_w * probabilities, -1, keepdims=True)))
    grad_table = jnp.einsum(
        "ijb,hij->bh", onehot, jnp.sum(grad_s.astype(jnp.float32), 0), precision=highest
    )
    grad_sq = lowered(
        jnp.einsum("qhij,qjhd->qihd", grad_s, key_heads, preferred_element_type=jnp.float32)
        * factor
    ).reshape(questions, answer, model_width)
    grad_sk = lowered(
        jnp.einsum("qhij,qihd->qjhd", grad_s, query_heads, preferred_element_type=jnp.float32)
        * factor
    ).reshape(questions, answer, model_width)
    grad_sv = lowered(
        jnp.einsum("qhij,qihd->qjhd", weights_self, grad_smix, preferred_element_type=jnp.float32)
    ).reshape(questions, answer, model_width)
    grad_query_self = shard_grad(hidden_one, grad_sq, device_place, rows_model)
    grad_key_self = shard_grad(hidden_one, grad_sk, device_place, rows_model)
    grad_value_self = shard_grad(hidden_one, grad_sv, device_place, rows_model)
    grad_hidden_one = jnp.einsum(
        "qae,ke->qak", grad_sq, query_self, preferred_element_type=jnp.float32
    )
    grad_hidden_one = grad_hidden_one + jnp.einsum(
        "qae,ke->qak", grad_sk, key_self, preferred_element_type=jnp.float32
    )
    grad_hidden_one = grad_hidden_one + jnp.einsum(
        "qae,ke->qak", grad_sv, value_self, preferred_element_type=jnp.float32
    )
    back_term, grad_gain_self = norm_backward(grad_hidden_one, normal_one, factor_one, norm_self)
    decoder_grad = grad_one + back_term
    key_part, value_part = (
        lax.psum_scatter(full_key, "pa", scatter_dimension=0, tiled=True),
        lax.psum_scatter(full_value, "pa", scatter_dimension=0, tiled=True),
    )
    summed = lax.psum(
        (
            grad_query_self,
            grad_key_self,
            grad_value_self,
            grad_out_self,
            grad_query_cross,
            key_part,
            value_part,
            grad_out_cross,
            grad_expand,
            grad_reduce,
            grad_gain_self,
            grad_gain_cross,
            grad_gain_ffn,
            grad_table,
        ),
        "pb",
    )
    key_total = summed[5]
    value_total = summed[6]
    rest_sums = (
        summed[0],
        summed[1],
        summed[2],
        summed[3],
        summed[4],
        summed[7],
        summed[8],
        summed[9],
        summed[10],
        summed[11],
        summed[12],
        summed[13],
    )
    return (
        decoder_out,
        decoder_grad,
        encoding_grad,
        rest_sums[0],
        rest_sums[1],
        rest_sums[2],
        rest_sums[3],
        rest_sums[4],
        key_total,
        value_total,
        rest_sums[5],
        rest_sums[6],
        rest_sums[7],
        rest_sums[8],
        rest_sums[9],
        rest_sums[10],
        rest_sums[11],
    )


def generic(mesh):
    placed = (
        P("pb", None, None),
        P("pb", "pa", None),
        P("pb", None, None),
        P("pb"),
        P("pb"),
        P(),
        P("pa", None),
        P("pa", None),
        P("pa", None),
        P("pa", None),
        P("pa", None),
        P("pa", None),
        P("pa", None),
        P("pa", None),
        P("pa", None),
        P("pa", None),
        P(),
        P(),
        P(),
        P(),
    )
    return jax.shard_map(
        shards,
        mesh=mesh,
        in_specs=placed,
        out_specs=(
            P("pb", None, None),
            P("pb", None, None),
            P("pb", "pa", None),
            P("pa", None),
            P("pa", None),
            P("pa", None),
            P("pa", None),
            P("pa", None),
            P("pa", None),
            P("pa", None),
            P("pa", None),
            P("pa", None),
            P("pa", None),
            P(),
            P(),
            P(),
            P(),
        ),
        check_vma=False,
    )


MESH = pl.DeviceIdType.MESH
F32, BF = jnp.float32, jnp.bfloat16
ANS, PAD, OWN, ALL = 20, 24, 48, 96
WIDTH, HEADS, SIZE, PART = 768, 12, 64, 192
ROWS = HEADS * PAD
SLOT, FF, BUCKETS = 512, 3072, 32
CQ, CK, CV, CO, SO, SQ, SK, SV, EX, RD, EN = range(11)
GELU_A, GELU_B = 0.7978845608028654, 0.044715


def nn(a, b):
    return lax.dot_general(a, b, (((1,), (0,)), ((), ())), preferred_element_type=F32)


def nt(a, b):
    return lax.dot_general(a, b, (((1,), (1,)), ((), ())), preferred_element_type=F32)


def tn(a, b):
    return lax.dot_general(a, b, (((0,), (0,)), ((), ())), preferred_element_type=F32)


def lanes(rows, width):
    return lax.broadcasted_iota(jnp.int32, (rows, width), 1)


def split4(v):
    out = []
    for j in range(4):
        base = PART * j // 128 * 128
        t = v[:, base : base + 256]
        out.append(pltpu.roll(t, PART, 1) if PART * j != base else t)
    return out


def join4(parts):
    low = lanes(parts[0].shape[0], 128) < 64
    tiles = []
    for a, b in ((parts[0], parts[1]), (parts[2], parts[3])):
        b = pltpu.roll(b, 64, 1)
        tiles += [a[:, :128], jnp.where(low, a[:, 128:], b[:, :128]), b[:, 128:]]
    return jnp.concatenate(tiles, 1)


def join3(parts):
    low = lanes(parts[0].shape[0], 128) < 64
    a, b = parts[0], pltpu.roll(parts[1], 64, 1)
    return jnp.concatenate([a[:, :128], jnp.where(low, a[:, 128:], b[:, :128]), b[:, 128:], parts[2]], 1)


def part3(v):
    return [v[:, :256], pltpu.roll(v[:, 128:384], PART, 1), v[:, 384:]]


def choose(parts, index):
    v = parts[0]
    for j in range(1, len(parts)):
        v = lax.select(index == j, parts[j], v)
    return v


def stack_heads(v, count):
    head = lanes(*v.shape) // SIZE
    return jnp.concatenate([jnp.where(head == h, v, 0.0) for h in range(count)], 0)


def pick_heads(v, count):
    head = lanes(PAD, v.shape[1]) // SIZE
    out = jnp.zeros((PAD, v.shape[1]), F32)
    for h in range(count):
        out = out + jnp.where(head == h, v[PAD * h : PAD * (h + 1)], 0.0)
    return out


def pair_stack(v, p):
    t = v[:, 128 * p : 128 * (p + 1)]
    low = lanes(PAD, 128) < SIZE
    return jnp.concatenate([jnp.where(low, t, 0.0), jnp.where(low, 0.0, t)], 0)


SCRATCH = dict(
    sq=((9, WIDTH, WIDTH), BF),
    rd=((WIDTH, WIDTH), BF),
    enc=((4, SLOT, WIDTH), BF),
    xs=((OWN, WIDTH), F32),
    ogs=((OWN, WIDTH), F32),
    bks=((PAD, PAD), jnp.int32),
    bias=((3 * PAD, PAD), F32),
    s1=((4, OWN, 640), BF),
    r1=((3, OWN, 640), BF),
    gact=((OWN, WIDTH), F32),
    s9=((4, OWN, 256), BF),
    r9=((3, OWN, 256), BF),
    t3=((4, OWN, 256), BF),
    s2=((4, OWN, 256), BF),
    r2=((3, OWN, 256), BF),
    ag2=((2, 4, OWN, 256), BF),
    gz=((OWN, WIDTH), BF),
    acts=((OWN, WIDTH), BF),
    span=((128, 384), F32),
    x6=((6, 192, 128), BF),
    y6=((6, 192, 128), BF),
    qk=((4, ROWS, WIDTH), BF),
    gv=((4, ROWS, WIDTH), BF),
    bs=((4, ROWS, WIDTH), BF),
    as_=((4, ROWS, WIDTH), BF),
    es=((4, ROWS, SLOT), BF),
    gs=((4, ROWS, SLOT), BF),
    stat=((384, 128), F32),
    stg=((8, 8, 384), F32),
    wrow=((128, 384), F32),
    wcol=((384, 128), F32),
    s5=((2, 4, OWN, 256), BF),
    r5=((8, OWN, 256), BF),
    mixg=((2, 4, OWN, 256), BF),
    gm=((2, OWN, WIDTH), BF),
    s7=((2, 4, OWN, 256), BF),
    c7=((4, OWN, 256), BF),
    z7=((4, OWN, 256), BF),
    r7=((3, OWN, 256), BF),
    gcq=((4, OWN, 256), BF),
    s8=((4, OWN, 256), BF),
    r8=((3, OWN, 256), BF),
    dog=((2, 4, OWN, 256), BF),
    dgr=((2, OWN, WIDTH), F32),
    tot=((ROWS, 128), F32),
    gsg=((4, OWN, 640), BF),
    tg=((4, OWN, 256), BF),
    stz=((4, BUCKETS, 128), F32),
    wg=((8, 96, WIDTH), BF),
    gexs=((96, FF), BF),
    gres=((384, WIDTH), BF),
    p1=((2, 4, 16, 1920), BF),
    p2=((2, 4, 16, 10240), BF),
    p3=((2, 4, 16, 2560), BF),
    p4=((2, 4, 16, 2560), BF),
    p5=((2, 4, 16, 2560), BF),
    p6=((2, 4, 16, 6400), BF),
    sgain=((2, 4, 8, WIDTH), F32),
    stab=((2, 4, BUCKETS, 128), F32),
    kw1=((WIDTH, WIDTH), BF),
    kr1=((384, WIDTH), BF),
    kw2=((4, 96, WIDTH), BF),
    kr2=((3, 96, WIDTH), BF),
    kw3=((4, 96, 256), BF),
    kr3=((3, 96, 256), BF),
    kw4=((2, 4, 96, 256), BF),
    vw1=((WIDTH, WIDTH), BF),
    vr1=((384, WIDTH), BF),
    vw2=((4, 96, WIDTH), BF),
    vr2=((3, 96, WIDTH), BF),
    vw3=((4, 96, 256), BF),
    vr3=((3, 96, 256), BF),
    vw4=((2, 4, 96, 256), BF),
    eg=((4, SLOT, WIDTH), BF),
)
SEMAPHORES = 188
NEAR, SCALAR, FAR = pltpu.VMEM, pltpu.SMEM, pl.ANY
IN_KIND = dict(
    x=NEAR, og=NEAR, plen=SCALAR, pcount=SCALAR, buckets=NEAR, table=SCALAR,
    g1=NEAR, g2=NEAR, g3=NEAR, enc_h=FAR,
    wq=FAR, wk=FAR, wv=FAR, wo=FAR, wcq=FAR, wck=FAR, wcv=FAR, wco=FAR, wex=FAR, wre=FAR,
)
OUT_KIND = dict(
    decoder_out=NEAR, decoder_grad=NEAR, encoding_grad=FAR, squares=FAR, gex=FAR, gre=FAR, gains=NEAR, table_grad=NEAR,
)


class Batch:
    def __init__(self, wire, span):
        self.span, self.sent, self.landed = span, wire.next(), wire.next()
        wire.batches.append(self)

    def wait_recv(self):
        pltpu.make_async_copy(self.span, self.span, self.landed).wait()

    def wait_send(self):
        pltpu.make_async_copy(self.span, self.span, self.sent).wait()


class Wire:
    def __init__(self, sems, narrow, wide):
        self.sems, self.count, self.batches = sems, 0, []
        self.narrow, self.wide = narrow, wide
        self.pb, self.pa = lax.axis_index("pb"), lax.axis_index("pa")
        self.z, self.c = self.pa // 2, lax.rem(self.pa, 2)

    def next(self):
        self.count += 1
        return self.sems.at[self.count - 1]

    def local(self, src, dst):
        copy = pltpu.make_async_copy(src, dst, self.next())
        copy.start()
        return copy

    def span(self, size, dtype):
        if dtype == F32:
            return self.wide.at[pl.ds(0, size // 384), :]
        lane = next(n for n in (384, 768, 640, 512, 256, 128) if size % (16 * n) == 0 and size <= n * WIDTH)
        return self.narrow.at[0, pl.ds(0, size // lane), pl.ds(0, lane)]

    def batch(self, copies):
        first = copies[0][0]
        span = first
        if len(copies) > 1:
            span = self.span(sum(math.prod(src.shape) for src, _, _, _ in copies), first.dtype)
        out = Batch(self, span)
        for src, dst, pb, pa in copies:
            pltpu.make_async_remote_copy(
                src_ref=src,
                dst_ref=dst,
                send_sem=out.sent,
                recv_sem=out.landed,
                device_id=(pb, pa),
                device_id_type=MESH,
            ).start()
        return out

    def zpeer(self, j):
        return lax.rem(self.z + j, 4)

    def ppeer(self, j):
        return lax.rem(self.pb + j, 4)

    def xside(self):
        return self.pb + 1 - 2 * lax.rem(self.pb, 2)

    def yside(self):
        return lax.rem(self.pb + 2, 4)

    def to_core(self, *pairs):
        return self.batch([(src, dst, self.pb, self.pa + 1 - 2 * self.c) for src, dst in pairs])

    def to_z(self, src_of, dst_of):
        peers = [(self.zpeer(j), j) for j in (1, 2, 3)]
        return self.batch([(src_of(t), dst_of(j), self.pb, 2 * t + self.c) for t, j in peers])

    def to_column(self, src_of, dst_of):
        peers = [(lax.rem(self.pa + j, 8), j) for j in range(1, 8)]
        return self.batch([(src_of(t), dst_of(j), self.pb, t) for t, j in peers])

    def to_plane(self, src_of, dst_of):
        peers = [(self.ppeer(j), j) for j in (1, 2, 3)]
        return self.batch([(src_of(t), dst_of(j), t, self.pa) for t, j in peers])

    def to_sides(self, refs):
        sides = (self.xside(), self.yside())
        return self.batch([(ref, ref, side, self.pa) for ref in refs for side in sides])


class Gather:
    def __init__(self, wire, sq, index, source, wide=False):
        self.w, self.sq, self.index, self.source, self.wide = wire, sq, index, source, wide
        row = pl.multiple_of(48 * lax.rem(wire.pb, 2), 16)

        def block(t):
            lane = 384 * (wire.pb // 2) + (WIDTH * t if wide else 0)
            return source.at[pl.ds(row, 48), pl.ds(pl.multiple_of(lane, 128), 384)]

        self.a = wire.to_z(block, lambda j: self.part(wire.z, wire.pb, 0, 384))

    def part(self, z, pb, begin, size):
        row = pl.multiple_of(96 * (2 * z + self.w.c) + 48 * lax.rem(pb, 2), 16)
        lane = pl.multiple_of(384 * (pb // 2) + begin, 128)
        return self.sq.at[self.index, pl.ds(row, 48), pl.ds(lane, size)]

    def plane(self):
        w = self.w
        self.a.wait_recv()
        self.a = w.to_sides([self.part(w.zpeer(i), w.pb, 0, 384) for i in (1, 2, 3)])

    def relay(self):
        w = self.w
        self.a.wait_recv()
        copies = []
        cut = 128 if self.index % 2 else 256
        for i in (1, 2, 3):
            ref = self.part(w.zpeer(i), w.xside(), 0, cut)
            copies.append((ref, ref, w.yside(), w.pa))
            ref = self.part(w.zpeer(i), w.yside(), cut, 384 - cut)
            copies.append((ref, ref, w.xside(), w.pa))
        self.a = w.batch(copies)

    def core(self):
        w = self.w
        self.a.wait_recv()
        refs = []
        for i in (1, 2, 3):
            row = pl.multiple_of(96 * (2 * w.zpeer(i) + w.c), 16)
            refs.append(self.sq.at[self.index, pl.ds(row, 96), :])
        self.a = w.to_core(*[(ref, ref) for ref in refs])

    def finish(self):
        self.a.wait_recv()


class PlaneRows:
    def __init__(self, wire, ref):
        self.w, self.ref = wire, ref
        self.a = wire.to_sides([ref.at[wire.c, wire.pb]])

    def relay(self):
        w = self.w
        self.a.wait_recv()
        size = self.ref.shape[3]
        half = size // 256 * 128
        a = self.ref.at[w.c, w.xside(), :, pl.ds(0, half)]
        b = self.ref.at[w.c, w.yside(), :, pl.ds(half, size - half)]
        self.a = w.batch([(a, a, w.yside(), w.pa), (b, b, w.xside(), w.pa)])

    def core(self):
        self.a.wait_recv()
        src = self.ref.at[self.w.c]
        self.a = self.w.to_core((src, src))

    def finish(self):
        self.a.wait_recv()


class PlaneSmall(PlaneRows):
    def __init__(self, wire, ref):
        self.w, self.ref = wire, ref
        src = ref.at[wire.c, wire.pb]
        self.a = wire.to_plane(lambda t: src, lambda j: src)


def pack(v):
    half = v.shape[1] // 2
    last = jnp.where(
        lax.broadcasted_iota(jnp.int32, (8, v.shape[1]), 0) < 4, v[16:24], pltpu.roll(v[40:48], 4, 0)
    )
    last = jnp.concatenate([last[:, :half], last[:, half:]], 0)
    return lowered(jnp.concatenate([v[:16], v[24:40], last], 1))


def unpack(ref, begin, width):
    begin = begin * 5 // 2
    a = ref[:, :, :, begin : begin + width].reshape(128, width)
    b = ref[:, :, :, begin + width : begin + 2 * width].reshape(128, width)
    t = ref[:, :, :, begin + 2 * width : begin + width * 5 // 2].astype(F32)
    t = [t[:, :, 8 * k : 8 * k + 8, :].reshape(64, width // 2) for k in (0, 1)]
    return jnp.concatenate([a, b, lowered(jnp.concatenate(t, 1))], 0)


class CrossReduce:
    def __init__(self, wire, refs):
        self.w, self.refs = wire, refs

    def core(self):
        w, (w1, r1, w2, r2, w3, r3, w4) = self.w, self.refs
        row = pl.multiple_of(384 * (1 - w.c), 16)
        self.a = w.to_core((w1.at[pl.ds(row, 384), :], r1))

    def plane(self):
        w, (w1, r1, w2, r2, w3, r3, w4) = self.w, self.refs
        self.a.wait_recv()
        for k in range(4):
            row = pl.multiple_of(384 * w.c + 96 * k, 16)
            t = w1[pl.ds(row, 96), :].astype(F32) + r1[96 * k : 96 * (k + 1), :].astype(F32)
            w2[k] = lowered(t)
        self.b = w.to_plane(lambda t: w2.at[t], lambda j: r2.at[j - 1])

    def line(self):
        w, (w1, r1, w2, r2, w3, r3, w4) = self.w, self.refs
        self.b.wait_recv()
        t = w2[w.pb].astype(F32)
        for j in range(3):
            t = t + r2[j].astype(F32)
        for j, part in enumerate(split4(t)):
            w3[j] = lowered(part)
        self.d = w.to_z(lambda t: w3.at[t], lambda j: r3.at[j - 1])

    def spread(self):
        w, (w1, r1, w2, r2, w3, r3, w4) = self.w, self.refs
        self.d.wait_recv()
        t = w3[w.z].astype(F32)
        for j in range(3):
            t = t + r3[j].astype(F32)
        w4[w.c, w.pb] = lowered(t)
        self.rows = PlaneRows(w, w4)

    def result(self):
        w4 = self.refs[-1]
        t = w4[...].astype(F32).reshape(WIDTH, 256)
        t = lax.select(self.w.c == 1, pltpu.roll(t, 160, 1), t)[:, :128]
        return lowered(t.T[:96])


def inputs_half(t, c):
    t = t.astype(F32)
    t = lax.select(c == 1, pltpu.roll(t, 160, 1), t)[:, :128]
    return lowered(t.T)


def layer(*refs):
    names = (*IN_KIND, *OUT_KIND)
    r = types.SimpleNamespace(**dict(zip(names, refs)))
    s = types.SimpleNamespace(**dict(zip(SCRATCH, refs[len(names) :])))
    w = Wire(refs[-1], s.sq, s.span)
    pb, pa, z, c = w.pb, w.pa, w.z, w.c
    sq, rd, enc = s.sq, s.rd, s.enc

    barrier = pltpu.get_barrier_semaphore()
    for j in range(1, 8):
        pl.semaphore_signal(
            barrier, inc=1, device_id=(pb, lax.rem(pa + j, 8)), device_id_type=MESH
        )
    for j in (1, 2, 3):
        pl.semaphore_signal(barrier, inc=1, device_id=(w.ppeer(j), pa), device_id_type=MESH)

    squares = [r.wcq, r.wck, r.wcv, r.wco, r.wo, r.wq, r.wk, r.wv]
    own_rows = pl.ds(pl.multiple_of(96 * pa, 16), 96)
    red_rows = pl.ds(pl.multiple_of(384 * c, 16), 384)
    order = (SQ, SK, SV, CQ, CK, SO, CV, CO)
    held = {i: w.local(squares[i], sq.at[i, own_rows, :]) for i in order}
    chip_cols = pl.ds(pl.multiple_of(WIDTH * z, 128), WIDTH)
    held[EX] = w.local(r.wex.at[:, chip_cols], sq.at[EX, own_rows, :])
    held[RD] = w.local(r.wre, rd.at[red_rows, :])
    held[EN] = w.local(r.enc_h, enc)

    for dst, src in ((s.xs, r.x), (s.ogs, r.og)):
        dst[...] = jnp.zeros((OWN, WIDTH), F32)
        for k in (0, 1):
            dst[PAD * k : PAD * k + ANS, :] = lax.select(c == 1, src[:, 2 + k, :], src[:, k, :])
    s.bks[...] = jnp.zeros((PAD, PAD), jnp.int32)
    s.bks[:ANS, :ANS] = r.buckets[...]
    g1, g2, g3 = [ref[...].reshape(1, WIDTH) for ref in (r.g1, r.g2, r.g3)]
    x = s.xs[...]
    rs1 = lax.rsqrt(jnp.mean(x * x, -1, keepdims=True) + epsilon)
    h1z = choose(split4(x * rs1 * g1), z)
    xz = choose(split4(x), z)
    h1b = lowered(h1z)
    s.p6[c, pb, :, 5760:6400] = pack(h1z)
    s.p1[c, pb] = pack(s.ogs[...])
    s.gz[...] = lowered(s.ogs[...])

    pl.semaphore_wait(barrier, 10)
    other = [
        w.to_core(*[(squares[i], sq.at[i, own_rows, :]) for i in (SQ, SK, SV)]),
        w.to_core((r.wre, rd.at[red_rows, :])),
        w.to_core(*[(squares[i], sq.at[i, own_rows, :]) for i in (SO, CQ, CK)]),
        w.to_core(
            *[(squares[i], sq.at[i, own_rows, :]) for i in (CV, CO)],
            (r.wex.at[:, chip_cols], sq.at[EX, own_rows, :]),
        ),
    ]

    def chip(i):
        return sq[i, pl.ds(pl.multiple_of(PART * z, 16), PART), :]

    parts = []
    for i in (SQ, SK, SV):
        held[i].wait()
        if i == SQ:
            other[0].wait_recv()
        parts.append(split4(nn(h1b[:, :PART], chip(i))))
    blocks = [join3([parts[k][j] for k in range(3)]) for j in range(4)]
    for j in range(4):
        s.s1[j] = lowered(blocks[j])
    own_qkv = choose(blocks, z)
    f1 = w.to_z(lambda t: s.s1.at[t], lambda j: s.r1.at[j - 1])
    gather_q = Gather(w, sq, CQ, r.wcq)
    gather_k = Gather(w, sq, CK, r.wck)

    bucket = s.bks[...]

    def bias_head(h, carry):
        v = jnp.zeros((PAD, PAD), F32)
        for b in range(BUCKETS):
            v = jnp.where(bucket == b, r.table[3 * z + h, b], v)
        s.bias[pl.ds(pl.multiple_of(PAD * h, 8), PAD), :] = v
        return carry

    lax.fori_loop(0, 3, bias_head, 0)
    held[RD].wait()
    other[1].wait_recv()
    s.gact[...] = nt(s.gz[...], rd[...])

    f1.wait_recv()
    v = own_qkv
    for j in range(3):
        v = v + s.r1[j].astype(F32)
    q3, k3, v3 = [lowered(t).astype(F32)[:, :PART] for t in part3(v)]

    def attend(stacked, keys, bias):
        i = lax.broadcasted_iota(jnp.int32, (PAD, PAD), 0)
        j = lax.broadcasted_iota(jnp.int32, (PAD, PAD), 1)
        seen = jnp.concatenate([(j <= i).astype(F32)] * 3, 0) > 0.5
        t = jnp.where(seen, nt(lowered(stacked), lowered(keys)) + bias, masked_score)
        t = jnp.exp(t - jnp.max(t, -1, keepdims=True))
        return t / jnp.sum(t, -1, keepdims=True)

    mixes, probs, stacks = [], [], []
    for k in (0, 1):
        rows = slice(PAD * k, PAD * (k + 1))
        stacks.append(stack_heads(q3[rows] * 0.125, 3))
        probs.append(attend(stacks[k], k3[rows], s.bias[...]))
        mixes.append(pick_heads(nn(lowered(probs[k]), lowered(v3[rows])), 3))
    mixb = lowered(jnp.concatenate(mixes, 0))
    gap = jnp.zeros((OWN, 64), F32)
    s.p5[c, pb, :, 1920:2560] = pack(jnp.concatenate([jnp.concatenate(mixes, 0), gap], 1))
    held[SO].wait()
    other[2].wait_recv()
    parts = split4(nn(mixb, chip(SO)))
    for j in range(4):
        s.s2[j] = lowered(parts[j])
    own_o = choose(parts, z)
    f2 = w.to_z(lambda t: s.s2.at[t], lambda j: s.r2.at[j - 1])
    gather_q.plane()
    gather_k.plane()

    f2.wait_recv()
    r1z = xz + own_o
    for j in range(3):
        r1z = r1z + s.r2[j].astype(F32)
    counts = lanes(OWN, 256) < PART
    g2z = choose(split4(jnp.broadcast_to(g2, (OWN, WIDTH))), z)
    square = jnp.sum(jnp.where(counts, r1z * r1z, 0.0), -1, keepdims=True)
    high = lowered(square).astype(F32)
    tail = jnp.where(lanes(OWN, 256) < 224, high, square - high)
    s.ag2[c, z] = lowered(jnp.where(counts, r1z * g2z, tail))
    f3 = w.to_z(lambda t: s.ag2.at[c, z], lambda j: s.ag2.at[c, z])
    gather_v = Gather(w, sq, CV, r.wcv)
    gather_q.relay()
    gather_q.core()
    gather_k.relay()

    f3.wait_recv()
    f3c = w.to_core((s.ag2.at[c], s.ag2.at[c]))
    gather_o = Gather(w, sq, CO, r.wco)
    gather_x = Gather(w, sq, EX, r.wex, True)
    gather_v.plane()
    f3c.wait_recv()
    blocks = [[s.ag2[k, j].astype(F32) for j in range(4)] for k in (0, 1)]
    rs2 = []
    for k in (0, 1):
        t = blocks[k][0] + blocks[k][1] + blocks[k][2] + blocks[k][3]
        lane = lanes(OWN, 256)
        t = jnp.sum(jnp.where((lane == 192) | (lane == 224), t, 0.0), -1, keepdims=True)
        rs2.append(lax.rsqrt(t * (1.0 / WIDTH) + epsilon))
    gather_q.finish()
    held[CQ].wait()
    cq = jnp.zeros((ALL, WIDTH), F32)
    for j in range(4):
        t = jnp.concatenate([s.ag2[0, j], s.ag2[1, j]], 0)[:, :PART]
        cq = cq + nn(t, sq[CQ, PART * j : PART * (j + 1), :])
    cq = cq * jnp.concatenate(rs2, 0)
    cq = lowered(cq).astype(F32) * 0.125
    gather_k.core()
    gather_v.relay()
    gather_k.finish()
    held[CK].wait()
    for p in range(6):
        t = jnp.concatenate([pair_stack(cq[PAD * q : PAD * (q + 1)], p) for q in range(4)], 0)
        s.x6[p] = lowered(t)
        t = lowered(nt(s.x6[p], sq[CK, :, 128 * p : 128 * (p + 1)]))
        for q in range(4):
            s.qk[q, 48 * p : 48 * (p + 1), :] = t[48 * q : 48 * (q + 1)]
    held[EN].wait()
    s.stat[...] = jnp.zeros((384, 128), F32)

    def scores(q, carry):
        size = r.plen[q]
        per = lax.select(size <= SLOT // 2, 2, 1)
        kept = jnp.minimum(jnp.maximum(r.pcount[q] - pa * per, 0), per) * size
        valid = lanes(ROWS, SLOT) < kept
        t = jnp.where(valid, nt(s.qk[q], enc[q]), masked_score)
        top = jnp.max(t, -1, keepdims=True)
        t = jnp.where(valid, jnp.exp(t - top), 0.0)
        total = jnp.sum(t, -1, keepdims=True)
        s.es[q] = lowered(t)
        s.bs[q] = lowered(nn(s.es[q], enc[q]))
        lane = lanes(ROWS, 128)
        old = s.stat[:ROWS, :]
        s.stat[:ROWS, :] = jnp.where(lane == q, top, jnp.where(lane == 4 + q, total, old))
        return carry

    lax.fori_loop(0, 4, scores, 0)
    s.stg[pa] = s.stat[...].T[:8]
    f4 = w.to_column(lambda t: s.stg.at[pa], lambda j: s.stg.at[pa])
    gather_v.core()
    gather_o.plane()
    gather_x.plane()
    gather_v.finish()
    held[CV].wait()
    other[3].wait_recv()
    low = lanes(PAD, 128) < SIZE
    tiles = [[] for q in range(4)]
    for p in range(6):
        t = jnp.concatenate([s.bs[q, 48 * p : 48 * (p + 1), :] for q in range(4)], 0)
        t = nn(t, sq[CV, :, 128 * p : 128 * (p + 1)])
        for q in range(4):
            a = t[48 * q : 48 * (q + 1)]
            tiles[q].append(jnp.where(low, a[:PAD], a[PAD:]))
    num = jnp.concatenate([jnp.concatenate(tiles[q], 1) for q in range(4)], 0)
    for k in (0, 1):
        for j, part in enumerate(split4(num[OWN * k : OWN * (k + 1)])):
            s.s5[k, j] = lowered(part)
    f5 = w.to_column(lambda t: s.s5.at[lax.rem(t, 2), t // 2], lambda j: s.r5.at[pa])
    s.r5[pa] = s.s5[c, z]
    rows1 = PlaneRows(w, s.p1)
    r1full = join4([s.ag2[c, j].astype(F32) for j in range(4)]) / g2
    rs2o = lax.select(c == 1, rs2[1], rs2[0])
    n2 = r1full * rs2o
    s.p4[c, pb, :, 1920:2560] = pack(choose(split4(n2 * g2), z))
    gather_o.relay()
    gather_x.relay()

    f4.wait_recv()
    f5.wait_recv()
    stats = [s.stg[k] for k in range(8)]
    top = stats[0]
    for k in range(1, 8):
        top = jnp.maximum(top, stats[k])
    scale = [jnp.exp(t - top) for t in stats]
    total = jnp.zeros((8, 384), F32)
    for k in range(8):
        total = total + scale[k] * pltpu.roll(stats[k], 4, 0)
    inverse = 1.0 / total
    s.wrow[...] = jnp.zeros((128, 384), F32)
    mine = jnp.zeros((8, 384), F32)
    for k in range(8):
        t = scale[k] * inverse
        mine = lax.select(pa == k, t, mine)
        s.wrow[2 * k : 2 * k + 2, :] = lax.select(c == 1, t[2:4], t[0:2])
    s.wrow[16:20, :] = mine[0:4]
    s.wcol[...] = s.wrow[...].T
    w3 = s.wcol[pl.ds(pl.multiple_of(3 * PAD * z, 8), 3 * PAD), :]
    lane = lanes(PAD, 256)
    sums = [jnp.zeros((PAD, 256), F32) for k in (0, 1)]
    for m in range(8):
        block = s.r5[m].astype(F32)
        for k in (0, 1):
            col = [w3[PAD * h : PAD * (h + 1), 2 * m + k : 2 * m + k + 1] for h in range(3)]
            t = jnp.where(lane < 64, col[0], jnp.where(lane < 128, col[1], col[2]))
            sums[k] = sums[k] + t * block[PAD * k : PAD * (k + 1)]
    mixc = jnp.concatenate(sums, 0)
    s.mixg[c, z] = lowered(mixc)
    s.p3[c, pb, :, 1920:2560] = pack(mixc)
    f6 = w.to_z(lambda t: s.mixg.at[c, z], lambda j: s.mixg.at[c, z])
    gather_o.core()
    gather_x.core()
    held[CO].wait()
    gather_o.finish()
    f6.wait_recv()
    mix_core = w.to_core((s.mixg.at[c], s.mixg.at[c]))
    after = jnp.zeros((OWN, WIDTH), F32)
    for j in range(4):
        after = after + nn(s.mixg[c, j][:, :PART], sq[CO, PART * j : PART * (j + 1), :])
    r2z = r1z + choose(split4(after), z)
    resid = r1full + after
    rs3 = lax.rsqrt(jnp.mean(resid * resid, -1, keepdims=True) + epsilon)
    n3 = resid * rs3
    h3 = lowered(n3 * g3)
    s.p2[c, pb, :, 7680:8320] = pack(choose(split4(n3 * g3), z))
    gather_x.finish()
    held[EX].wait()
    v = nn(h3, sq[EX])
    t = jnp.tanh(GELU_A * (v + GELU_B * v * v * v))
    act = 0.5 * v * (1.0 + t)
    s.acts[...] = lowered(act)
    s.p2[c, pb, :, 8320:10240] = pack(act)
    slope = 0.5 * (1.0 + t) + 0.5 * v * (1.0 - t * t) * GELU_A * (1.0 + 3.0 * GELU_B * v * v)
    gp = s.gact[...] * slope
    gp_cols = pl.ds(pl.multiple_of(1920 * z, 128), 1920)
    s.p2[c, pb, :, gp_cols] = pack(gp)
    gp = lowered(gp)
    parts = split4(nt(gp, sq[EX]))
    for j in range(4):
        s.s9[j] = lowered(parts[j])
    own_g = choose(parts, z)
    fe = w.to_z(lambda t: s.s9.at[t], lambda j: s.r9.at[j - 1])
    rows1.relay()
    g3z = choose(split4(jnp.broadcast_to(g3, (OWN, WIDTH))), z)
    fe.wait_recv()
    t = own_g
    for j in range(3):
        t = t + s.r9[j].astype(F32)
    s.t3[z] = lowered(t * g3z)
    ff = w.to_z(lambda t: s.t3.at[z], lambda j: s.t3.at[z])
    fp = w.to_z(lambda t: s.p2.at[c, pb, :, gp_cols], lambda j: s.p2.at[c, pb, :, gp_cols])
    ff.wait_recv()
    og = s.ogs[...]
    t = join4([s.t3[j].astype(F32) for j in range(4)])
    gain3 = jnp.sum(t * n3, 0, keepdims=True) / g3
    grad_two = og + rs3 * (t - n3 * jnp.mean(t * n3, -1, keepdims=True))
    gcb = lowered(grad_two)
    s.p3[c, pb, :, :1920] = pack(grad_two)
    s.gm[c] = lowered(nt(gcb, sq[CO]))
    f7 = w.to_core((s.gm.at[c], s.gm.at[c]))
    rows3 = PlaneRows(w, s.p3)
    mix_core.wait_recv()
    f7.wait_recv()

    gms = [s.gm[k].astype(F32) for k in (0, 1)]
    mxs = [join4([s.mixg[k, j].astype(F32) for j in range(4)]) for k in (0, 1)]
    gm_q = [gms[q // 2][PAD * (q % 2) : PAD * (q % 2 + 1)] for q in range(4)]
    mx_q = [mxs[q // 2][PAD * (q % 2) : PAD * (q % 2 + 1)] for q in range(4)]
    tots = [[] for q in range(4)]
    for p in range(6):
        blocks_p = []
        for q in range(4):
            col = s.wcol[48 * p : 48 * (p + 1), 16 + q : 17 + q]
            y = pair_stack(gm_q[q], p) * col
            m = mx_q[q][:, 128 * p : 128 * (p + 1)]
            tots[q].append(-jnp.sum(y * jnp.concatenate([m, m], 0), -1, keepdims=True))
            blocks_p.append(y)
        s.y6[p] = lowered(jnp.concatenate(blocks_p, 0))
        t = lowered(nt(s.y6[p], sq[CV, :, 128 * p : 128 * (p + 1)]))
        for q in range(4):
            s.gv[q, 48 * p : 48 * (p + 1), :] = t[48 * q : 48 * (q + 1)]
    lane = lanes(ROWS, 128)
    t = jnp.zeros((ROWS, 128), F32)
    for q in range(4):
        t = jnp.where(lane == q, jnp.concatenate(tots[q], 0), t)
    s.tot[...] = t
    for p in range(6):
        t = jnp.concatenate([s.bs[q, 48 * p : 48 * (p + 1), :] for q in range(4)], 0)
        s.vw1[128 * p : 128 * (p + 1), :] = lowered(tn(s.y6[p], t))
    vred = CrossReduce(w, [s.vw1, s.vr1, s.vw2, s.vr2, s.vw3, s.vr3, s.vw4])
    vred.core()
    fp.wait_recv()
    rows2 = PlaneRows(w, s.p2)

    def grads(q, carry):
        pick = lanes(ROWS, 128) == q
        tot = jnp.sum(jnp.where(pick, s.tot[...], 0.0), -1, keepdims=True)
        t = nt(s.gv[q], enc[q]) + tot
        s.gs[q] = lowered(s.es[q].astype(F32) * t)
        s.as_[q] = lowered(nn(s.gs[q], enc[q]))
        return carry

    lax.fori_loop(0, 4, grads, 0)
    tiles = [[] for q in range(4)]
    for p in range(6):
        t = jnp.concatenate([s.as_[q, 48 * p : 48 * (p + 1), :] for q in range(4)], 0)
        t = nn(t, sq[CK, :, 128 * p : 128 * (p + 1)])
        for q in range(4):
            a = t[48 * q : 48 * (q + 1)]
            tiles[q].append(jnp.where(low, a[:PAD], a[PAD:]))
    num = jnp.concatenate([jnp.concatenate(tiles[q], 1) for q in range(4)], 0) * 0.125
    for k in (0, 1):
        for j, part in enumerate(split4(num[OWN * k : OWN * (k + 1)])):
            s.s7[k, j] = lowered(part)
    fc = w.to_core((s.s7.at[1 - c], s.c7))
    vred.plane()
    fc.wait_recv()
    for j in range(4):
        s.z7[j] = lowered(s.s7[c, j].astype(F32) + s.c7[j].astype(F32))
    f8 = w.to_z(lambda t: s.z7.at[t], lambda j: s.r7.at[j - 1])
    for p in range(6):
        t = jnp.concatenate([s.as_[q, 48 * p : 48 * (p + 1), :] for q in range(4)], 0)
        s.kw1[128 * p : 128 * (p + 1), :] = lowered(tn(s.x6[p], t))
    kred = CrossReduce(w, [s.kw1, s.kr1, s.kw2, s.kr2, s.kw3, s.kr3, s.kw4])
    kred.core()
    rows3.relay()
    rows1.core()
    out_copies = []

    def encoding_grad(q):
        s.eg[q] = lowered(tn(s.es[q], s.gv[q]) + tn(s.gs[q], s.qk[q]))
        out_copies.append(w.local(s.eg.at[q], r.encoding_grad.at[q]))

    encoding_grad(0)
    encoding_grad(1)

    f8.wait_recv()
    t = s.z7[z].astype(F32)
    for k in range(3):
        t = t + s.r7[k].astype(F32)
    s.gcq[z] = lowered(t)
    f9 = w.to_z(lambda t: s.gcq.at[z], lambda j: s.gcq.at[z])
    kred.plane()
    rows2.relay()
    rows3.core()
    parts = split4(nn(s.acts[...], rd[...]))
    for j in range(4):
        s.s8[j] = lowered(parts[j])
    own_d = choose(parts, z)
    fo = w.to_z(lambda t: s.s8.at[t], lambda j: s.r8.at[j - 1])
    encoding_grad(2)
    encoding_grad(3)

    f9.wait_recv()
    gcq = join4([s.gcq[j].astype(F32) for j in range(4)])
    s.p4[c, pb, :, :1920] = pack(gcq)
    gcq = lowered(gcq)
    rows4 = PlaneRows(w, s.p4)
    gh2 = nt(gcq, sq[CQ])
    gain2 = jnp.sum(gh2 * n2, 0, keepdims=True)
    t = gh2 * g2
    grad_one = grad_two + rs2o * (t - n2 * jnp.mean(t * n2, -1, keepdims=True))
    gab = lowered(grad_one)
    s.p5[c, pb, :, :1920] = pack(grad_one)
    rows5 = PlaneRows(w, s.p5)
    gsm = lowered(nt(gab, chip(SO))).astype(F32)
    gsum = jnp.zeros((3 * PAD, PAD), F32)
    dq, dk, dv = [], [], []
    for k in (0, 1):
        rows = slice(PAD * k, PAD * (k + 1))
        prob = probs[k]
        stacked = lowered(stack_heads(gsm[rows], 3))
        gw = nt(stacked, lowered(v3[rows]))
        gsb = lowered(prob * (gw - jnp.sum(gw * prob, -1, keepdims=True)))
        gsum = gsum + gsb.astype(F32)
        dq.append(pick_heads(nn(gsb, lowered(k3[rows])), 3) * 0.125)
        dk.append(tn(gsb, lowered(stacks[k])))
        dv.append(tn(lowered(prob), stacked))
    three = [jnp.concatenate([jnp.concatenate(t, 0), gap], 1) for t in (dq, dk, dv)]
    s.gsg[z] = lowered(join3(three))
    f10 = w.to_z(lambda t: s.gsg.at[z], lambda j: s.gsg.at[z])
    s.bias[...] = gsum

    def table_head(h, carry):
        v = s.bias[pl.ds(pl.multiple_of(PAD * h, 8), PAD), :]
        rows = [jnp.sum(jnp.where(bucket == b, v, 0.0), 0, keepdims=True) for b in range(BUCKETS)]
        col = jnp.sum(jnp.concatenate(rows, 0), -1, keepdims=True)
        return jnp.where(lanes(BUCKETS, 128) == 3 * z + h, col, carry)

    s.stz[z] = lax.fori_loop(0, 3, table_head, jnp.zeros((BUCKETS, 128), F32))
    ft = w.to_z(lambda t: s.stz.at[z], lambda j: s.stz.at[z])
    rows2.core()
    vred.line()
    fo.wait_recv()
    t = r2z + own_d
    for j in range(3):
        t = t + s.r8[j].astype(F32)
    s.dog[c, z] = lowered(t)
    fg = w.to_z(lambda t: s.dog.at[c, z], lambda j: s.dog.at[c, z])
    rows1.finish()

    def half_product(ref, begin, index, rows):
        rows.finish()
        lhs = inputs_half(unpack(ref, begin, 256), c)
        s.wg[index] = lowered(nn(lhs, unpack(ref, 0, WIDTH))[:96])
        out_copies.append(w.local(s.wg.at[index], r.squares.at[index]))

    half_product(s.p3, 768, 7, rows3)

    f10.wait_recv()
    unpacked = [part3(s.gsg[j].astype(F32)) for j in range(4)]
    three = [join4([unpacked[j][k] for j in range(4)]) for k in range(3)]
    for k in range(3):
        s.p6[c, pb, :, 1920 * k : 1920 * (k + 1)] = pack(three[k])
    three = [lowered(v) for v in three]
    rows6 = PlaneRows(w, s.p6)
    gh1 = nt(three[0], chip(SQ)) + nt(three[1], chip(SK)) + nt(three[2], chip(SV))
    g1z = choose(split4(jnp.broadcast_to(g1, (OWN, WIDTH))), z)
    s.tg[z] = lowered(jnp.concatenate([gh1 * g1z[:, :PART], gap], 1))
    f11 = w.to_z(lambda t: s.tg.at[z], lambda j: s.tg.at[z])
    ft.wait_recv()
    s.stab[c, pb] = s.stz[0] + s.stz[1] + s.stz[2] + s.stz[3]
    tab_rows = PlaneSmall(w, s.stab)
    kred.line()
    rows4.relay()
    rows5.relay()
    vred.spread()
    rows2.finish()
    p2 = s.p2
    lhs = inputs_half(unpack(p2, 3072, 256), c)
    for j in range(4):
        cols = slice(WIDTH * j, WIDTH * (j + 1))
        s.gexs[:, cols] = lowered(nn(lhs, unpack(p2, WIDTH * j, WIDTH))[:96])
    out_copies.append(w.local(s.gexs, r.gex))
    f11.wait_recv()
    fg.wait_recv()
    fgc = w.to_core((s.dog.at[c], s.dog.at[c]))
    t = join4([s.tg[j].astype(F32) for j in range(4)])
    n1 = s.xs[...] * rs1
    gain1 = jnp.sum(t * n1, 0, keepdims=True) / g1
    s.dgr[c] = grad_one + rs1 * (t - n1 * jnp.mean(t * n1, -1, keepdims=True))
    fd = w.to_core((s.dgr.at[c], s.dgr.at[c]))
    s.sgain[c, pb] = jnp.concatenate([gain1, gain2, gain3, jnp.zeros((5, WIDTH), F32)], 0)
    gain_rows = PlaneSmall(w, s.sgain)
    rows6.relay()
    kred.spread()
    vred.rows.relay()
    rows4.core()
    rows5.core()
    t = unpack(p2, 3328, WIDTH).astype(F32)
    lhs = lowered(lax.select(c == 1, t[:, 384:], t[:, :384]).T)
    s.gres[...] = lowered(nn(lhs, unpack(s.p1, 0, WIDTH)))
    out_copies.append(w.local(s.gres, r.gre))
    half_product(s.p4, 768, 4, rows4)
    half_product(s.p5, 768, 3, rows5)
    vred.rows.core()
    kred.rows.relay()
    tab_rows.core()
    gain_rows.core()
    fgc.wait_recv()
    fd.wait_recv()
    for k in (0, 1):
        t = join4([s.dog[k, j].astype(F32) for j in range(4)])
        for m in (0, 1):
            r.decoder_out[:, 2 * k + m, :] = t[PAD * m : PAD * m + ANS]
            r.decoder_grad[:, 2 * k + m, :] = s.dgr[k, PAD * m : PAD * m + ANS, :]
    rows6.core()
    kred.rows.core()
    vred.rows.finish()
    s.wg[6] = vred.result()
    out_copies.append(w.local(s.wg.at[6], r.squares.at[6]))
    gain_rows.finish()
    tab_rows.finish()
    t = s.sgain[0, 0]
    u = s.stab[0, 0]
    for k in range(1, 8):
        t = t + s.sgain[k // 4, k % 4]
        u = u + s.stab[k // 4, k % 4]
    r.gains[...] = t
    r.table_grad[...] = u
    kred.rows.finish()
    s.wg[5] = kred.result()
    out_copies.append(w.local(s.wg.at[5], r.squares.at[5]))
    rows6.finish()
    ref = s.p6
    lhs = inputs_half(unpack(ref, 2304, 256), c)
    for k in range(3):
        s.wg[k] = lowered(nn(lhs, unpack(ref, WIDTH * k, WIDTH))[:96])
        out_copies.append(w.local(s.wg.at[k], r.squares.at[k]))
    for copy in out_copies:
        copy.wait()
    for batch in w.batches:
        batch.wait_send()


def write(dout, dgrad, eg, sq, gex, gre, gains, table, *refs):
    outs, (veg, vsq, vex, vre, weg, wsq, wex, wre, sems) = refs[:17], refs[17:]
    o_out, o_grad, o_eg, outs = outs[0], outs[1], outs[2], outs[3:]
    jobs = [(eg.at[q], veg.at[q], weg.at[q], o_eg.at[q]) for q in range(4)]
    jobs += [(gex, vex, wex, outs[8]), (gre, vre, wre, outs[9])]
    jobs += [(sq.at[k], vsq.at[k], wsq.at[k], outs[k]) for k in range(8)]
    loads = [pltpu.make_async_copy(j[0], j[1], sems.at[k]) for k, j in enumerate(jobs)]
    for copy in loads:
        copy.start()
    o_out[...] = dout[...]
    o_grad[...] = dgrad[...]
    for k in range(3):
        outs[10 + k][...] = gains[k : k + 1, :].reshape(WIDTH)
    outs[13][...] = table[...].T[:HEADS]
    stores = []
    for k, (src, near, wide, dst) in enumerate(jobs):
        loads[k].wait()
        wide[...] = near[...].astype(F32)
        stores.append(pltpu.make_async_copy(wide, dst, sems.at[len(jobs) + k]))
        stores[-1].start()
    for copy in stores:
        copy.wait()


def fused(x, enc, og, plen, pcount, buckets, wq, wk, wv, wo, wcq, wck, wcv, wco, wex, wre, g1, g2, g3, table):
    def shape(*dims, kind=F32):
        return jax.ShapeDtypeStruct(dims, kind)

    rows = shape(ANS, 4, WIDTH)
    mid = pl.pallas_call(
        layer,
        out_shape=[
            rows,
            rows,
            shape(4, SLOT, WIDTH, kind=BF),
            shape(8, 96, WIDTH, kind=BF),
            shape(96, FF, kind=BF),
            shape(384, WIDTH, kind=BF),
            shape(8, WIDTH),
            shape(BUCKETS, 128),
        ],
        in_specs=[pl.BlockSpec(memory_space=k) for k in IN_KIND.values()],
        out_specs=[pl.BlockSpec(memory_space=k) for k in OUT_KIND.values()],
        scratch_shapes=[pltpu.VMEM(*v) for v in SCRATCH.values()]
        + [pltpu.SemaphoreType.DMA((SEMAPHORES,))],
        compiler_params=pltpu.CompilerParams(
            collective_id=0, has_side_effects=True, vmem_limit_bytes=62 * 2**20
        ),
    )(
        jnp.transpose(x, (1, 0, 2)),
        jnp.transpose(og, (1, 0, 2)),
        *(plen, pcount, buckets, table.T, g1, g2, g3, enc),
        *(wq, wk, wv, wo, wcq, wck, wcv, wco, wex, wre),
    )
    near, far = pl.BlockSpec(memory_space=NEAR), pl.BlockSpec(memory_space=FAR)
    square = shape(96, WIDTH)
    out = pl.pallas_call(
        write,
        out_shape=[
            *(rows, rows, shape(4, SLOT, WIDTH)),
            *[square] * 8,
            *(shape(96, FF), shape(384, WIDTH)),
            *[shape(WIDTH)] * 3,
            shape(HEADS, BUCKETS),
        ],
        in_specs=[near, near, far, far, far, far, near, near],
        out_specs=[near, near, far, *[far] * 10, *[near] * 4],
        scratch_shapes=[
            pltpu.VMEM(dims, kind)
            for kind in (BF, F32)
            for dims in ((4, SLOT, WIDTH), (8, 96, WIDTH), (96, FF), (384, WIDTH))
        ]
        + [pltpu.SemaphoreType.DMA((28,))],
        compiler_params=pltpu.CompilerParams(vmem_limit_bytes=62 * 2**20),
    )(*mid)
    out = list(out)
    out[0], out[1] = (jnp.transpose(v, (1, 0, 2)) for v in out[:2])
    out[16] = out[16].T
    return tuple(out)


def solution(mesh):
    if dict(mesh.shape) != {"pb": 4, "pa": 8}:
        return generic(mesh)
    wide, tall = P("pb", "pa", None), P("pa", None)
    rows, whole = P("pb", None, None), P()
    return jax.shard_map(
        fused,
        mesh=mesh,
        in_specs=(rows, wide, rows, P("pb"), P("pb"), whole, *[tall] * 10, *[whole] * 4),
        out_specs=(rows, rows, wide, *[tall] * 10, *[whole] * 4),
        check_vma=False,
    )
```

```python
import math
import types

import jax
import jax.numpy as jnp
from jax import lax
from jax.experimental import pallas as pl
from jax.experimental.pallas import tpu as pltpu
from jax.sharding import PartitionSpec as P

epsilon = 1e-06
highest = lax.Precision.HIGHEST
masked_score = -1e30


def product(left, right):
    return jnp.dot(left, right, preferred_element_type=jnp.float32)


def lowered(value):
    return value.astype(jnp.bfloat16)


def norm_forward(value):
    factor = lax.rsqrt(jnp.mean(value * value, -1, keepdims=True) + epsilon)
    return (value * factor, factor)


def norm_backward(grad_out, normal, factor, gain):
    inner_term = grad_out * gain
    grad_in = factor * (inner_term - normal * jnp.mean(inner_term * normal, -1, keepdims=True))
    grad_gain = jnp.sum(grad_out * normal, (0, 1))
    return (grad_in, grad_gain)


def activate(value):
    return jax.nn.gelu(value, approximate=True)


def shard_grad(inputs, grad_rows, device_place, row_count):
    sliced = lax.dynamic_slice_in_dim(inputs, device_place * row_count, row_count, 2)
    return jnp.einsum("qak,qae->ke", sliced, grad_rows, preferred_element_type=jnp.float32)


def shards(
    decoder_in,
    encodings,
    out_grad,
    passage_len,
    passage_count,
    buckets,
    self_query,
    self_key,
    self_value,
    self_out,
    cross_query,
    cross_key,
    cross_value,
    cross_out,
    ffn_expand,
    ffn_reduce,
    norm_self,
    norm_cross,
    norm_ffn,
    bias_table,
):
    wide_count = lax.axis_size("pa")
    device_place = lax.axis_index("pa")
    stacked = jnp.stack(
        [self_query, self_key, self_value, self_out, cross_query, cross_key, cross_value, cross_out]
    )
    squares, expand_full, reduce_full = (
        lax.all_gather(stacked, "pa", axis=1, tiled=True),
        lax.all_gather(ffn_expand, "pa", axis=0, tiled=True),
        lax.all_gather(ffn_reduce, "pa", axis=0, tiled=True),
    )
    query_self = squares[0]
    key_self = squares[1]
    value_self = squares[2]
    out_self = squares[3]
    query_cross = squares[4]
    key_cross = squares[5]
    value_cross = squares[6]
    out_cross = squares[7]
    questions, answer, model_width = decoder_in.shape
    head_count = bias_table.shape[1]
    head_size = model_width // head_count
    factor = head_size ** (-0.5)
    slot_rows = encodings.shape[1]
    rows_model = model_width // wide_count
    rows_hidden = expand_full.shape[1] // wide_count

    def heads_of(value):
        return value.reshape(value.shape[0], value.shape[1], head_count, head_size)

    normal_one, factor_one = norm_forward(decoder_in)
    hidden_one = lowered(normal_one * norm_self)
    query_heads = heads_of(lowered(product(hidden_one, query_self)))
    key_heads = heads_of(lowered(product(hidden_one, key_self)))
    value_heads = heads_of(lowered(product(hidden_one, value_self)))
    onehot = (buckets[:, :, None] == jnp.arange(bias_table.shape[0])[None, None, :]).astype(
        jnp.float32
    )
    bias_scores = jnp.einsum("ijb,bh->hij", onehot, bias_table, precision=highest)
    causal = jnp.arange(answer)[:, None] >= jnp.arange(answer)[None, :]
    scores = (
        jnp.einsum("qihd,qjhd->qhij", query_heads, key_heads, preferred_element_type=jnp.float32)
        * factor
        + bias_scores[None]
    )
    scores = jnp.where(causal[None, None], scores, masked_score)
    probabilities = jax.nn.softmax(scores, -1)
    weights_self = lowered(probabilities)
    mixed_self = lowered(
        jnp.einsum("qhij,qjhd->qihd", weights_self, value_heads, preferred_element_type=jnp.float32)
    ).reshape(questions, answer, model_width)
    resid_one = decoder_in + product(mixed_self, out_self)
    normal_two, factor_two = norm_forward(resid_one)
    hidden_two = lowered(normal_two * norm_cross)
    cquery = heads_of(lowered(product(hidden_two, query_cross)))
    per_device = slot_rows // passage_len
    held_count = jnp.clip(passage_count - device_place * per_device, 0, per_device)
    valid_rows = jnp.arange(slot_rows)[None, :] < (held_count * passage_len)[:, None]

    def project(encoded):
        ckeys = lowered(product(encoded, key_cross)).reshape(
            questions, slot_rows, head_count, head_size
        )
        cvalues = lowered(product(encoded, value_cross)).reshape(
            questions, slot_rows, head_count, head_size
        )
        cscores = (
            jnp.einsum("qihd,qjhd->qhij", cquery, ckeys, preferred_element_type=jnp.float32)
            * factor
        )
        cscores = jnp.where(valid_rows[:, None, None, :], cscores, masked_score)
        return (ckeys, cvalues, cscores)

    ckeys, cvalues, cscores = project(encodings)
    row_max = lax.pmax(jnp.max(cscores, -1), "pa")
    exp_weights = jnp.exp(cscores - row_max[..., None])
    part_num = jnp.einsum(
        "qhij,qjhd->qihd", lowered(exp_weights), cvalues, preferred_element_type=jnp.float32
    )
    part_total = jnp.sum(exp_weights, -1)
    numerator, totals = lax.psum((part_num, part_total), "pa")
    totals_t = jnp.transpose(totals, (0, 2, 1))[..., None]
    mixed_cross = lowered(numerator / totals_t).reshape(questions, answer, model_width)
    resid_two = resid_one + product(mixed_cross, out_cross)
    normal_three, factor_three = norm_forward(resid_two)
    hidden_three = lowered(normal_three * norm_ffn)
    pre_act = product(hidden_three, expand_full)
    activation = lowered(activate(pre_act))
    decoder_out = resid_two + product(activation, reduce_full)
    grad_z = lowered(out_grad)
    grad_reduce = shard_grad(activation, grad_z, device_place, rows_hidden)
    grad_act = jnp.einsum("qae,fe->qaf", grad_z, reduce_full, preferred_element_type=jnp.float32)
    unused_out, gelu_back = jax.vjp(activate, pre_act)
    grad_pre = lowered(gelu_back(grad_act)[0])
    grad_expand = shard_grad(hidden_three, grad_pre, device_place, rows_model)
    grad_three = jnp.einsum(
        "qaf,kf->qak", grad_pre, expand_full, preferred_element_type=jnp.float32
    )
    back_term, grad_gain_ffn = norm_backward(grad_three, normal_three, factor_three, norm_ffn)
    grad_two = out_grad + back_term
    grad_c = lowered(grad_two)
    grad_out_cross = shard_grad(mixed_cross, grad_c, device_place, rows_model)
    grad_mix = heads_of(
        lowered(jnp.einsum("qae,ke->qak", grad_c, out_cross, preferred_element_type=jnp.float32))
    )
    grad_mix_wide = grad_mix.astype(jnp.float32)
    grad_num = lowered(grad_mix_wide / totals_t)
    grad_tot = -jnp.sum(grad_mix_wide * numerator, -1) / (totals_t[..., 0] * totals_t[..., 0])
    ckeys, cvalues, cscores = project(encodings)
    exp_weights = jnp.exp(cscores - row_max[..., None])
    grad_expo = jnp.einsum("qihd,qjhd->qhij", grad_num, cvalues, preferred_element_type=jnp.float32)
    grad_expo = grad_expo + jnp.transpose(grad_tot, (0, 2, 1))[..., None]
    grad_score = lowered(exp_weights * grad_expo)
    part_query = (
        jnp.einsum("qhij,qjhd->qihd", grad_score, ckeys, preferred_element_type=jnp.float32)
        * factor
    )
    grad_cquery = lowered(lax.psum(part_query, "pa")).reshape(questions, answer, model_width)
    grad_ckeys = lowered(
        jnp.einsum("qhij,qihd->qjhd", grad_score, cquery, preferred_element_type=jnp.float32)
        * factor
    ).reshape(questions, slot_rows, model_width)
    grad_cvalues = lowered(
        jnp.einsum(
            "qhij,qihd->qjhd", lowered(exp_weights), grad_num, preferred_element_type=jnp.float32
        )
    ).reshape(questions, slot_rows, model_width)
    encoding_grad = jnp.einsum(
        "qse,ke->qsk", grad_ckeys, key_cross, preferred_element_type=jnp.float32
    )
    encoding_grad = encoding_grad + jnp.einsum(
        "qse,ke->qsk", grad_cvalues, value_cross, preferred_element_type=jnp.float32
    )
    full_key = jnp.einsum("qsk,qse->ke", encodings, grad_ckeys, preferred_element_type=jnp.float32)
    full_value = jnp.einsum(
        "qsk,qse->ke", encodings, grad_cvalues, preferred_element_type=jnp.float32
    )
    grad_query_cross = shard_grad(hidden_two, grad_cquery, device_place, rows_model)
    grad_hidden_two = jnp.einsum(
        "qae,ke->qak", grad_cquery, query_cross, preferred_element_type=jnp.float32
    )
    back_term, grad_gain_cross = norm_backward(grad_hidden_two, normal_two, factor_two, norm_cross)
    grad_one = grad_two + back_term
    grad_a = lowered(grad_one)
    grad_out_self = shard_grad(mixed_self, grad_a, device_place, rows_model)
    grad_smix = heads_of(
        lowered(jnp.einsum("qae,ke->qak", grad_a, out_self, preferred_element_type=jnp.float32))
    )
    grad_w = jnp.einsum(
        "qihd,qjhd->qhij", grad_smix, value_heads, preferred_element_type=jnp.float32
    )
    grad_s = lowered(probabilities * (grad_w - jnp.sum(grad_w * probabilities, -1, keepdims=True)))
    grad_table = jnp.einsum(
        "ijb,hij->bh", onehot, jnp.sum(grad_s.astype(jnp.float32), 0), precision=highest
    )
    grad_sq = lowered(
        jnp.einsum("qhij,qjhd->qihd", grad_s, key_heads, preferred_element_type=jnp.float32)
        * factor
    ).reshape(questions, answer, model_width)
    grad_sk = lowered(
        jnp.einsum("qhij,qihd->qjhd", grad_s, query_heads, preferred_element_type=jnp.float32)
        * factor
    ).reshape(questions, answer, model_width)
    grad_sv = lowered(
        jnp.einsum("qhij,qihd->qjhd", weights_self, grad_smix, preferred_element_type=jnp.float32)
    ).reshape(questions, answer, model_width)
    grad_query_self = shard_grad(hidden_one, grad_sq, device_place, rows_model)
    grad_key_self = shard_grad(hidden_one, grad_sk, device_place, rows_model)
    grad_value_self = shard_grad(hidden_one, grad_sv, device_place, rows_model)
    grad_hidden_one = jnp.einsum(
        "qae,ke->qak", grad_sq, query_self, preferred_element_type=jnp.float32
    )
    grad_hidden_one = grad_hidden_one + jnp.einsum(
        "qae,ke->qak", grad_sk, key_self, preferred_element_type=jnp.float32
    )
    grad_hidden_one = grad_hidden_one + jnp.einsum(
        "qae,ke->qak", grad_sv, value_self, preferred_element_type=jnp.float32
    )
    back_term, grad_gain_self = norm_backward(grad_hidden_one, normal_one, factor_one, norm_self)
    decoder_grad = grad_one + back_term
    key_part, value_part = (
        lax.psum_scatter(full_key, "pa", scatter_dimension=0, tiled=True),
        lax.psum_scatter(full_value, "pa", scatter_dimension=0, tiled=True),
    )
    summed = lax.psum(
        (
            grad_query_self,
            grad_key_self,
            grad_value_self,
            grad_out_self,
            grad_query_cross,
            key_part,
            value_part,
            grad_out_cross,
            grad_expand,
            grad_reduce,
            grad_gain_self,
            grad_gain_cross,
            grad_gain_ffn,
            grad_table,
        ),
        "pb",
    )
    key_total = summed[5]
    value_total = summed[6]
    rest_sums = (
        summed[0],
        summed[1],
        summed[2],
        summed[3],
        summed[4],
        summed[7],
        summed[8],
        summed[9],
        summed[10],
        summed[11],
        summed[12],
        summed[13],
    )
    return (
        decoder_out,
        decoder_grad,
        encoding_grad,
        rest_sums[0],
        rest_sums[1],
        rest_sums[2],
        rest_sums[3],
        rest_sums[4],
        key_total,
        value_total,
        rest_sums[5],
        rest_sums[6],
        rest_sums[7],
        rest_sums[8],
        rest_sums[9],
        rest_sums[10],
        rest_sums[11],
    )


def generic(mesh):
    placed = (
        P("pb", None, None),
        P("pb", "pa", None),
        P("pb", None, None),
        P("pb"),
        P("pb"),
        P(),
        P("pa", None),
        P("pa", None),
        P("pa", None),
        P("pa", None),
        P("pa", None),
        P("pa", None),
        P("pa", None),
        P("pa", None),
        P("pa", None),
        P("pa", None),
        P(),
        P(),
        P(),
        P(),
    )
    return jax.shard_map(
        shards,
        mesh=mesh,
        in_specs=placed,
        out_specs=(
            P("pb", None, None),
            P("pb", None, None),
            P("pb", "pa", None),
            P("pa", None),
            P("pa", None),
            P("pa", None),
            P("pa", None),
            P("pa", None),
            P("pa", None),
            P("pa", None),
            P("pa", None),
            P("pa", None),
            P("pa", None),
            P(),
            P(),
            P(),
            P(),
        ),
        check_vma=False,
    )


MESH = pl.DeviceIdType.MESH
F32, BF = jnp.float32, jnp.bfloat16
ANS, PAD, OWN, ALL = 20, 24, 48, 96
WIDTH, HEADS, SIZE, PART = 768, 12, 64, 192
ROWS = HEADS * PAD
SLOT, FF, BUCKETS = 512, 3072, 32
CQ, CK, CV, CO, SO, SQ, SK, SV, EX, RD, EN = range(11)
GELU_A, GELU_B = 0.7978845608028654, 0.044715


def nn(a, b):
    return lax.dot_general(a, b, (((1,), (0,)), ((), ())), preferred_element_type=F32)


def nt(a, b):
    return lax.dot_general(a, b, (((1,), (1,)), ((), ())), preferred_element_type=F32)


def tn(a, b):
    return lax.dot_general(a, b, (((0,), (0,)), ((), ())), preferred_element_type=F32)


def lanes(rows, width):
    return lax.broadcasted_iota(jnp.int32, (rows, width), 1)


def split4(v):
    out = []
    for j in range(4):
        base = PART * j // 128 * 128
        t = v[:, base : base + 256]
        out.append(pltpu.roll(t, PART, 1) if PART * j != base else t)
    return out


def join4(parts):
    low = lanes(parts[0].shape[0], 128) < 64
    tiles = []
    for a, b in ((parts[0], parts[1]), (parts[2], parts[3])):
        b = pltpu.roll(b, 64, 1)
        tiles += [a[:, :128], jnp.where(low, a[:, 128:], b[:, :128]), b[:, 128:]]
    return jnp.concatenate(tiles, 1)


def join3(parts):
    low = lanes(parts[0].shape[0], 128) < 64
    a, b = parts[0], pltpu.roll(parts[1], 64, 1)
    return jnp.concatenate([a[:, :128], jnp.where(low, a[:, 128:], b[:, :128]), b[:, 128:], parts[2]], 1)


def part3(v):
    return [v[:, :256], pltpu.roll(v[:, 128:384], PART, 1), v[:, 384:]]


def choose(parts, index):
    v = parts[0]
    for j in range(1, len(parts)):
        v = lax.select(index == j, parts[j], v)
    return v


def stack_heads(v, count):
    head = lanes(*v.shape) // SIZE
    return jnp.concatenate([jnp.where(head == h, v, 0.0) for h in range(count)], 0)


def pick_heads(v, count):
    head = lanes(PAD, v.shape[1]) // SIZE
    out = jnp.zeros((PAD, v.shape[1]), F32)
    for h in range(count):
        out = out + jnp.where(head == h, v[PAD * h : PAD * (h + 1)], 0.0)
    return out


def pair_stack(v, p):
    t = v[:, 128 * p : 128 * (p + 1)]
    low = lanes(PAD, 128) < SIZE
    return jnp.concatenate([jnp.where(low, t, 0.0), jnp.where(low, 0.0, t)], 0)


SCRATCH = dict(
    sq=((9, WIDTH, WIDTH), BF),
    rd=((WIDTH, WIDTH), BF),
    enc=((4, SLOT, WIDTH), BF),
    xs=((OWN, WIDTH), F32),
    ogs=((OWN, WIDTH), F32),
    bks=((PAD, PAD), jnp.int32),
    bias=((3 * PAD, PAD), F32),
    s1=((4, OWN, 640), BF),
    r1=((3, OWN, 640), BF),
    gact=((OWN, WIDTH), F32),
    s9=((4, OWN, 256), BF),
    r9=((3, OWN, 256), BF),
    t3=((4, OWN, 256), BF),
    s2=((4, OWN, 256), BF),
    r2=((3, OWN, 256), BF),
    ag2=((2, 4, OWN, 256), BF),
    gz=((OWN, WIDTH), BF),
    acts=((OWN, WIDTH), BF),
    span=((128, 384), F32),
    x6=((6, 192, 128), BF),
    y6=((6, 192, 128), BF),
    qk=((4, ROWS, WIDTH), BF),
    gv=((4, ROWS, WIDTH), BF),
    bs=((4, ROWS, WIDTH), BF),
    as_=((4, ROWS, WIDTH), BF),
    es=((4, ROWS, SLOT), BF),
    gs=((4, ROWS, SLOT), BF),
    stat=((384, 128), F32),
    stg=((8, 8, 384), F32),
    wrow=((128, 384), F32),
    wcol=((384, 128), F32),
    s5=((2, 4, OWN, 256), BF),
    r5=((8, OWN, 256), BF),
    mixg=((2, 4, OWN, 256), BF),
    gm=((2, OWN, WIDTH), BF),
    s7=((2, 4, OWN, 256), BF),
    c7=((4, OWN, 256), BF),
    z7=((4, OWN, 256), BF),
    r7=((3, OWN, 256), BF),
    gcq=((4, OWN, 256), BF),
    s8=((4, OWN, 256), BF),
    r8=((3, OWN, 256), BF),
    dog=((2, 4, OWN, 256), BF),
    dgr=((2, OWN, WIDTH), F32),
    tot=((ROWS, 128), F32),
    gsg=((4, OWN, 640), BF),
    tg=((4, OWN, 256), BF),
    stz=((4, BUCKETS, 128), F32),
    wg=((8, 96, WIDTH), BF),
    gexs=((96, FF), BF),
    gres=((384, WIDTH), BF),
    p1=((2, 4, 16, 1920), BF),
    p2=((2, 4, 16, 10240), BF),
    p3=((2, 4, 16, 2560), BF),
    p4=((2, 4, 16, 2560), BF),
    p5=((2, 4, 16, 2560), BF),
    p6=((2, 4, 16, 6400), BF),
    sgain=((2, 4, 8, WIDTH), F32),
    stab=((2, 4, BUCKETS, 128), F32),
    kw1=((WIDTH, WIDTH), BF),
    kr1=((384, WIDTH), BF),
    kw2=((4, 96, WIDTH), BF),
    kr2=((3, 96, WIDTH), BF),
    kw3=((4, 96, 256), BF),
    kr3=((3, 96, 256), BF),
    kw4=((2, 4, 96, 256), BF),
    vw1=((WIDTH, WIDTH), BF),
    vr1=((384, WIDTH), BF),
    vw2=((4, 96, WIDTH), BF),
    vr2=((3, 96, WIDTH), BF),
    vw3=((4, 96, 256), BF),
    vr3=((3, 96, 256), BF),
    vw4=((2, 4, 96, 256), BF),
    eg=((4, SLOT, WIDTH), BF),
)
SEMAPHORES = 181
NEAR, SCALAR, FAR = pltpu.VMEM, pltpu.SMEM, pl.ANY
IN_KIND = dict(
    x=NEAR, og=NEAR, plen=SCALAR, pcount=SCALAR, buckets=NEAR, table=SCALAR,
    g1=NEAR, g2=NEAR, g3=NEAR, enc_h=FAR,
    wq=FAR, wk=FAR, wv=FAR, wo=FAR, wcq=FAR, wck=FAR, wcv=FAR, wco=FAR, wex=FAR, wre=FAR,
)
OUT_KIND = dict(
    decoder_out=NEAR, decoder_grad=NEAR, encoding_grad=FAR, squares=FAR, gex=FAR, gre=FAR, gains=NEAR, table_grad=NEAR,
)


class Batch:
    def __init__(self, wire, span):
        self.span, self.sent, self.landed = span, wire.next(), wire.next()
        wire.batches.append(self)

    def wait_recv(self):
        pltpu.make_async_copy(self.span, self.span, self.landed).wait()

    def wait_send(self):
        pltpu.make_async_copy(self.span, self.span, self.sent).wait()


class Wire:
    def __init__(self, sems, narrow, wide):
        self.sems, self.count, self.batches = sems, 0, []
        self.narrow, self.wide = narrow, wide
        self.pb, self.pa = lax.axis_index("pb"), lax.axis_index("pa")
        self.z, self.c = self.pa // 2, lax.rem(self.pa, 2)

    def next(self):
        self.count += 1
        return self.sems.at[self.count - 1]

    def local(self, src, dst):
        copy = pltpu.make_async_copy(src, dst, self.next())
        copy.start()
        return copy

    def span(self, size, dtype):
        if dtype == F32:
            return self.wide.at[pl.ds(0, size // 384), :]
        lane = next(n for n in (384, 768, 640, 512, 256, 128) if size % (16 * n) == 0 and size <= n * WIDTH)
        return self.narrow.at[0, pl.ds(0, size // lane), pl.ds(0, lane)]

    def batch(self, copies):
        first = copies[0][0]
        span = first
        if len(copies) > 1:
            span = self.span(sum(math.prod(src.shape) for src, _, _, _ in copies), first.dtype)
        out = Batch(self, span)
        for src, dst, pb, pa in copies:
            pltpu.make_async_remote_copy(
                src_ref=src,
                dst_ref=dst,
                send_sem=out.sent,
                recv_sem=out.landed,
                device_id=(pb, pa),
                device_id_type=MESH,
            ).start()
        return out

    def zpeer(self, j):
        return lax.rem(self.z + j, 4)

    def ppeer(self, j):
        return lax.rem(self.pb + j, 4)

    def xside(self):
        return self.pb + 1 - 2 * lax.rem(self.pb, 2)

    def yside(self):
        return lax.rem(self.pb + 2, 4)

    def to_core(self, *pairs):
        return self.batch([(src, dst, self.pb, self.pa + 1 - 2 * self.c) for src, dst in pairs])

    def to_z(self, src_of, dst_of):
        peers = [(self.zpeer(j), j) for j in (1, 2, 3)]
        return self.batch([(src_of(t), dst_of(j), self.pb, 2 * t + self.c) for t, j in peers])

    def to_column(self, src_of, dst_of):
        peers = [(lax.rem(self.pa + j, 8), j) for j in range(1, 8)]
        return self.batch([(src_of(t), dst_of(j), self.pb, t) for t, j in peers])

    def to_plane(self, src_of, dst_of):
        peers = [(self.ppeer(j), j) for j in (1, 2, 3)]
        return self.batch([(src_of(t), dst_of(j), t, self.pa) for t, j in peers])

    def to_sides(self, refs):
        sides = (self.xside(), self.yside())
        return self.batch([(ref, ref, side, self.pa) for ref in refs for side in sides])


class Gather:
    def __init__(self, wire, sq, index, source, wide=False):
        self.w, self.sq, self.index, self.source, self.wide = wire, sq, index, source, wide
        row = pl.multiple_of(48 * lax.rem(wire.pb, 2), 16)

        def block(t):
            lane = 384 * (wire.pb // 2) + (WIDTH * t if wide else 0)
            return source.at[pl.ds(row, 48), pl.ds(pl.multiple_of(lane, 128), 384)]

        self.a = wire.to_z(block, lambda j: self.part(wire.z, wire.pb, 0, 384))

    def part(self, z, pb, begin, size):
        row = pl.multiple_of(96 * (2 * z + self.w.c) + 48 * lax.rem(pb, 2), 16)
        lane = pl.multiple_of(384 * (pb // 2) + begin, 128)
        return self.sq.at[self.index, pl.ds(row, 48), pl.ds(lane, size)]

    def plane(self):
        w = self.w
        self.a.wait_recv()
        self.a = w.to_sides([self.part(w.zpeer(i), w.pb, 0, 384) for i in (1, 2, 3)])

    def relay(self):
        w = self.w
        self.a.wait_recv()
        copies = []
        cut = 128 if self.index % 2 else 256
        for i in (1, 2, 3):
            ref = self.part(w.zpeer(i), w.xside(), 0, cut)
            copies.append((ref, ref, w.yside(), w.pa))
            ref = self.part(w.zpeer(i), w.yside(), cut, 384 - cut)
            copies.append((ref, ref, w.xside(), w.pa))
        self.a = w.batch(copies)

    def core(self):
        w = self.w
        self.a.wait_recv()
        refs = []
        for i in (1, 2, 3):
            row = pl.multiple_of(96 * (2 * w.zpeer(i) + w.c), 16)
            refs.append(self.sq.at[self.index, pl.ds(row, 96), :])
        self.a = w.to_core(*[(ref, ref) for ref in refs])

    def finish(self):
        self.a.wait_recv()


class PlaneRows:
    def __init__(self, wire, ref):
        self.w, self.ref = wire, ref
        self.a = wire.to_sides([ref.at[wire.c, wire.pb]])

    def relay(self):
        w = self.w
        self.a.wait_recv()
        size = self.ref.shape[3]
        half = size // 256 * 128
        a = self.ref.at[w.c, w.xside(), :, pl.ds(0, half)]
        b = self.ref.at[w.c, w.yside(), :, pl.ds(half, size - half)]
        self.a = w.batch([(a, a, w.yside(), w.pa), (b, b, w.xside(), w.pa)])

    def core(self):
        self.a.wait_recv()
        src = self.ref.at[self.w.c]
        self.a = self.w.to_core((src, src))

    def finish(self):
        self.a.wait_recv()


class PlaneSmall(PlaneRows):
    def __init__(self, wire, ref):
        self.w, self.ref = wire, ref
        src = ref.at[wire.c, wire.pb]
        self.a = wire.to_plane(lambda t: src, lambda j: src)


def pack(v):
    half = v.shape[1] // 2
    last = jnp.where(
        lax.broadcasted_iota(jnp.int32, (8, v.shape[1]), 0) < 4, v[16:24], pltpu.roll(v[40:48], 4, 0)
    )
    last = jnp.concatenate([last[:, :half], last[:, half:]], 0)
    return lowered(jnp.concatenate([v[:16], v[24:40], last], 1))


def unpack(ref, begin, width):
    begin = begin * 5 // 2
    a = ref[:, :, :, begin : begin + width].reshape(128, width)
    b = ref[:, :, :, begin + width : begin + 2 * width].reshape(128, width)
    t = ref[:, :, :, begin + 2 * width : begin + width * 5 // 2].astype(F32)
    t = [t[:, :, 8 * k : 8 * k + 8, :].reshape(64, width // 2) for k in (0, 1)]
    return jnp.concatenate([a, b, lowered(jnp.concatenate(t, 1))], 0)


class CrossReduce:
    def __init__(self, wire, refs):
        self.w, self.refs = wire, refs

    def core(self):
        w, (w1, r1, w2, r2, w3, r3, w4) = self.w, self.refs
        row = pl.multiple_of(384 * (1 - w.c), 16)
        self.a = w.to_core((w1.at[pl.ds(row, 384), :], r1))

    def plane(self):
        w, (w1, r1, w2, r2, w3, r3, w4) = self.w, self.refs
        self.a.wait_recv()
        for k in range(4):
            row = pl.multiple_of(384 * w.c + 96 * k, 16)
            t = w1[pl.ds(row, 96), :].astype(F32) + r1[96 * k : 96 * (k + 1), :].astype(F32)
            w2[k] = lowered(t)
        self.b = w.to_plane(lambda t: w2.at[t], lambda j: r2.at[j - 1])

    def line(self):
        w, (w1, r1, w2, r2, w3, r3, w4) = self.w, self.refs
        self.b.wait_recv()
        t = w2[w.pb].astype(F32)
        for j in range(3):
            t = t + r2[j].astype(F32)
        for j, part in enumerate(split4(t)):
            w3[j] = lowered(part)
        self.d = w.to_z(lambda t: w3.at[t], lambda j: r3.at[j - 1])

    def spread(self):
        w, (w1, r1, w2, r2, w3, r3, w4) = self.w, self.refs
        self.d.wait_recv()
        t = w3[w.z].astype(F32)
        for j in range(3):
            t = t + r3[j].astype(F32)
        w4[w.c, w.pb] = lowered(t)
        self.rows = PlaneSmall(w, w4)

    def result(self):
        w4 = self.refs[-1]
        t = w4[...].astype(F32).reshape(WIDTH, 256)
        t = lax.select(self.w.c == 1, pltpu.roll(t, 160, 1), t)[:, :128]
        return lowered(t.T[:96])


def inputs_half(t, c):
    t = t.astype(F32)
    t = lax.select(c == 1, pltpu.roll(t, 160, 1), t)[:, :128]
    return lowered(t.T)


def layer(*refs):
    names = (*IN_KIND, *OUT_KIND)
    r = types.SimpleNamespace(**dict(zip(names, refs)))
    s = types.SimpleNamespace(**dict(zip(SCRATCH, refs[len(names) :])))
    w = Wire(refs[-1], s.sq, s.span)
    pb, pa, z, c = w.pb, w.pa, w.z, w.c
    sq, rd, enc = s.sq, s.rd, s.enc

    barrier = pltpu.get_barrier_semaphore()
    for j in range(1, 8):
        pl.semaphore_signal(
            barrier, inc=1, device_id=(pb, lax.rem(pa + j, 8)), device_id_type=MESH
        )
    for j in (1, 2, 3):
        pl.semaphore_signal(barrier, inc=1, device_id=(w.ppeer(j), pa), device_id_type=MESH)

    squares = [r.wcq, r.wck, r.wcv, r.wco, r.wo, r.wq, r.wk, r.wv]
    own_rows = pl.ds(pl.multiple_of(96 * pa, 16), 96)
    red_rows = pl.ds(pl.multiple_of(384 * c, 16), 384)
    order = (SQ, SK, SV, CQ, CK, SO, CV, CO)
    held = {i: w.local(squares[i], sq.at[i, own_rows, :]) for i in order}
    chip_cols = pl.ds(pl.multiple_of(WIDTH * z, 128), WIDTH)
    held[EX] = w.local(r.wex.at[:, chip_cols], sq.at[EX, own_rows, :])
    held[RD] = w.local(r.wre, rd.at[red_rows, :])
    held[EN] = w.local(r.enc_h, enc)

    for dst, src in ((s.xs, r.x), (s.ogs, r.og)):
        dst[...] = jnp.zeros((OWN, WIDTH), F32)
        for k in (0, 1):
            dst[PAD * k : PAD * k + ANS, :] = lax.select(c == 1, src[:, 2 + k, :], src[:, k, :])
    s.bks[...] = jnp.zeros((PAD, PAD), jnp.int32)
    s.bks[:ANS, :ANS] = r.buckets[...]
    g1, g2, g3 = [ref[...].reshape(1, WIDTH) for ref in (r.g1, r.g2, r.g3)]
    x = s.xs[...]
    rs1 = lax.rsqrt(jnp.mean(x * x, -1, keepdims=True) + epsilon)
    h1z = choose(split4(x * rs1 * g1), z)
    xz = choose(split4(x), z)
    h1b = lowered(h1z)
    s.p6[c, pb, :, 5760:6400] = pack(h1z)
    s.p1[c, pb] = pack(s.ogs[...])
    s.gz[...] = lowered(s.ogs[...])

    pl.semaphore_wait(barrier, 10)
    other = [w.to_core(*[(squares[i], sq.at[i, own_rows, :]) for i in (SQ, SK, SV)])]
    gather_q = Gather(w, sq, CQ, r.wcq)
    other += [
        w.to_core((r.wre, rd.at[red_rows, :])),
        w.to_core(*[(squares[i], sq.at[i, own_rows, :]) for i in (SO, CQ, CK)]),
        w.to_core(
            *[(squares[i], sq.at[i, own_rows, :]) for i in (CV, CO)],
            (r.wex.at[:, chip_cols], sq.at[EX, own_rows, :]),
        ),
    ]

    def chip(i):
        return sq[i, pl.ds(pl.multiple_of(PART * z, 16), PART), :]

    parts = []
    for i in (SQ, SK, SV):
        held[i].wait()
        if i == SQ:
            other[0].wait_recv()
        parts.append(split4(nn(h1b[:, :PART], chip(i))))
    blocks = [join3([parts[k][j] for k in range(3)]) for j in range(4)]
    for j in range(4):
        s.s1[j] = lowered(blocks[j])
    own_qkv = choose(blocks, z)
    f1 = w.to_z(lambda t: s.s1.at[t], lambda j: s.r1.at[j - 1])
    gather_k = Gather(w, sq, CK, r.wck)

    bucket = s.bks[...]

    def bias_head(h, carry):
        v = jnp.zeros((PAD, PAD), F32)
        for b in range(BUCKETS):
            v = jnp.where(bucket == b, r.table[3 * z + h, b], v)
        s.bias[pl.ds(pl.multiple_of(PAD * h, 8), PAD), :] = v
        return carry

    lax.fori_loop(0, 3, bias_head, 0)
    held[RD].wait()
    other[1].wait_recv()
    s.gact[...] = nt(s.gz[...], rd[...])

    gather_q.plane()
    f1.wait_recv()
    gather_q.relay()
    v = own_qkv
    for j in range(3):
        v = v + s.r1[j].astype(F32)
    q3, k3, v3 = [lowered(t).astype(F32)[:, :PART] for t in part3(v)]

    def attend(stacked, keys, bias):
        i = lax.broadcasted_iota(jnp.int32, (PAD, PAD), 0)
        j = lax.broadcasted_iota(jnp.int32, (PAD, PAD), 1)
        seen = jnp.concatenate([(j <= i).astype(F32)] * 3, 0) > 0.5
        t = jnp.where(seen, nt(lowered(stacked), lowered(keys)) + bias, masked_score)
        t = jnp.exp(t - jnp.max(t, -1, keepdims=True))
        return t / jnp.sum(t, -1, keepdims=True)

    mixes, probs, stacks = [], [], []
    for k in (0, 1):
        rows = slice(PAD * k, PAD * (k + 1))
        stacks.append(stack_heads(q3[rows] * 0.125, 3))
        probs.append(attend(stacks[k], k3[rows], s.bias[...]))
        mixes.append(pick_heads(nn(lowered(probs[k]), lowered(v3[rows])), 3))
    mixb = lowered(jnp.concatenate(mixes, 0))
    gap = jnp.zeros((OWN, 64), F32)
    s.p5[c, pb, :, 1920:2560] = pack(jnp.concatenate([jnp.concatenate(mixes, 0), gap], 1))
    held[SO].wait()
    other[2].wait_recv()
    parts = split4(nn(mixb, chip(SO)))
    for j in range(4):
        s.s2[j] = lowered(parts[j])
    own_o = choose(parts, z)
    f2 = w.to_z(lambda t: s.s2.at[t], lambda j: s.r2.at[j - 1])
    gather_q.core()
    gather_k.plane()

    f2.wait_recv()
    r1z = xz + own_o
    for j in range(3):
        r1z = r1z + s.r2[j].astype(F32)
    counts = lanes(OWN, 256) < PART
    g2z = choose(split4(jnp.broadcast_to(g2, (OWN, WIDTH))), z)
    square = jnp.sum(jnp.where(counts, r1z * r1z, 0.0), -1, keepdims=True)
    high = lowered(square).astype(F32)
    tail = jnp.where(lanes(OWN, 256) < 224, high, square - high)
    s.ag2[c, z] = lowered(jnp.where(counts, r1z * g2z, tail))
    f3 = w.to_z(lambda t: s.ag2.at[c, z], lambda j: s.ag2.at[c, z])
    gather_v = Gather(w, sq, CV, r.wcv)
    gather_k.relay()

    f3.wait_recv()
    f3c = w.to_core((s.ag2.at[c], s.ag2.at[c]))
    gather_k.core()
    gather_o = Gather(w, sq, CO, r.wco)
    gather_x = Gather(w, sq, EX, r.wex, True)
    gather_v.plane()
    f3c.wait_recv()
    blocks = [[s.ag2[k, j].astype(F32) for j in range(4)] for k in (0, 1)]
    rs2 = []
    for k in (0, 1):
        t = blocks[k][0] + blocks[k][1] + blocks[k][2] + blocks[k][3]
        lane = lanes(OWN, 256)
        t = jnp.sum(jnp.where((lane == 192) | (lane == 224), t, 0.0), -1, keepdims=True)
        rs2.append(lax.rsqrt(t * (1.0 / WIDTH) + epsilon))
    gather_q.finish()
    held[CQ].wait()
    cq = jnp.zeros((ALL, WIDTH), F32)
    for j in range(4):
        t = jnp.concatenate([s.ag2[0, j], s.ag2[1, j]], 0)[:, :PART]
        cq = cq + nn(t, sq[CQ, PART * j : PART * (j + 1), :])
    cq = cq * jnp.concatenate(rs2, 0)
    cq = lowered(cq).astype(F32) * 0.125
    gather_v.relay()
    gather_k.finish()
    held[CK].wait()
    for p in range(6):
        t = jnp.concatenate([pair_stack(cq[PAD * q : PAD * (q + 1)], p) for q in range(4)], 0)
        s.x6[p] = lowered(t)
        t = lowered(nt(s.x6[p], sq[CK, :, 128 * p : 128 * (p + 1)]))
        for q in range(4):
            s.qk[q, 48 * p : 48 * (p + 1), :] = t[48 * q : 48 * (q + 1)]
    held[EN].wait()
    s.stat[...] = jnp.zeros((384, 128), F32)

    def scores(q, carry):
        size = r.plen[q]
        per = lax.select(size <= SLOT // 2, 2, 1)
        kept = jnp.minimum(jnp.maximum(r.pcount[q] - pa * per, 0), per) * size
        valid = lanes(ROWS, SLOT) < kept
        t = jnp.where(valid, nt(s.qk[q], enc[q]), masked_score)
        top = jnp.max(t, -1, keepdims=True)
        t = jnp.where(valid, jnp.exp(t - top), 0.0)
        total = jnp.sum(t, -1, keepdims=True)
        s.es[q] = lowered(t)
        s.bs[q] = lowered(nn(s.es[q], enc[q]))
        lane = lanes(ROWS, 128)
        old = s.stat[:ROWS, :]
        s.stat[:ROWS, :] = jnp.where(lane == q, top, jnp.where(lane == 4 + q, total, old))
        return carry

    lax.fori_loop(0, 4, scores, 0)
    s.stg[pa] = s.stat[...].T[:8]
    f4 = w.to_column(lambda t: s.stg.at[pa], lambda j: s.stg.at[pa])
    gather_v.core()
    gather_o.plane()
    gather_x.plane()
    gather_v.finish()
    held[CV].wait()
    other[3].wait_recv()
    low = lanes(PAD, 128) < SIZE
    tiles = [[] for q in range(4)]
    for p in range(6):
        t = jnp.concatenate([s.bs[q, 48 * p : 48 * (p + 1), :] for q in range(4)], 0)
        t = nn(t, sq[CV, :, 128 * p : 128 * (p + 1)])
        for q in range(4):
            a = t[48 * q : 48 * (q + 1)]
            tiles[q].append(jnp.where(low, a[:PAD], a[PAD:]))
    num = jnp.concatenate([jnp.concatenate(tiles[q], 1) for q in range(4)], 0)
    for k in (0, 1):
        for j, part in enumerate(split4(num[OWN * k : OWN * (k + 1)])):
            s.s5[k, j] = lowered(part)
    f5 = w.to_column(lambda t: s.s5.at[lax.rem(t, 2), t // 2], lambda j: s.r5.at[pa])
    s.r5[pa] = s.s5[c, z]
    rows1 = PlaneRows(w, s.p1)
    r1full = join4([s.ag2[c, j].astype(F32) for j in range(4)]) / g2
    rs2o = lax.select(c == 1, rs2[1], rs2[0])
    n2 = r1full * rs2o
    s.p4[c, pb, :, 1920:2560] = pack(choose(split4(n2 * g2), z))
    gather_o.relay()
    gather_x.relay()

    f4.wait_recv()
    f5.wait_recv()
    stats = [s.stg[k] for k in range(8)]
    top = stats[0]
    for k in range(1, 8):
        top = jnp.maximum(top, stats[k])
    scale = [jnp.exp(t - top) for t in stats]
    total = jnp.zeros((8, 384), F32)
    for k in range(8):
        total = total + scale[k] * pltpu.roll(stats[k], 4, 0)
    inverse = 1.0 / total
    s.wrow[...] = jnp.zeros((128, 384), F32)
    mine = jnp.zeros((8, 384), F32)
    for k in range(8):
        t = scale[k] * inverse
        mine = lax.select(pa == k, t, mine)
        s.wrow[2 * k : 2 * k + 2, :] = lax.select(c == 1, t[2:4], t[0:2])
    s.wrow[16:20, :] = mine[0:4]
    s.wcol[...] = s.wrow[...].T
    w3 = s.wcol[pl.ds(pl.multiple_of(3 * PAD * z, 8), 3 * PAD), :]
    lane = lanes(PAD, 256)
    sums = [jnp.zeros((PAD, 256), F32) for k in (0, 1)]
    for m in range(8):
        block = s.r5[m].astype(F32)
        for k in (0, 1):
            col = [w3[PAD * h : PAD * (h + 1), 2 * m + k : 2 * m + k + 1] for h in range(3)]
            t = jnp.where(lane < 64, col[0], jnp.where(lane < 128, col[1], col[2]))
            sums[k] = sums[k] + t * block[PAD * k : PAD * (k + 1)]
    mixc = jnp.concatenate(sums, 0)
    s.mixg[c, z] = lowered(mixc)
    s.p3[c, pb, :, 1920:2560] = pack(mixc)
    f6 = w.to_z(lambda t: s.mixg.at[c, z], lambda j: s.mixg.at[c, z])
    gather_o.core()
    gather_x.core()
    held[CO].wait()
    gather_o.finish()
    f6.wait_recv()
    mix_core = w.to_core((s.mixg.at[c], s.mixg.at[c]))
    after = jnp.zeros((OWN, WIDTH), F32)
    for j in range(4):
        after = after + nn(s.mixg[c, j][:, :PART], sq[CO, PART * j : PART * (j + 1), :])
    r2z = r1z + choose(split4(after), z)
    resid = r1full + after
    rs3 = lax.rsqrt(jnp.mean(resid * resid, -1, keepdims=True) + epsilon)
    n3 = resid * rs3
    h3 = lowered(n3 * g3)
    s.p2[c, pb, :, 7680:8320] = pack(choose(split4(n3 * g3), z))
    gather_x.finish()
    held[EX].wait()
    v = nn(h3, sq[EX])
    t = jnp.tanh(GELU_A * (v + GELU_B * v * v * v))
    act = 0.5 * v * (1.0 + t)
    s.acts[...] = lowered(act)
    s.p2[c, pb, :, 8320:10240] = pack(act)
    slope = 0.5 * (1.0 + t) + 0.5 * v * (1.0 - t * t) * GELU_A * (1.0 + 3.0 * GELU_B * v * v)
    gp = s.gact[...] * slope
    gp_cols = pl.ds(pl.multiple_of(1920 * z, 128), 1920)
    s.p2[c, pb, :, gp_cols] = pack(gp)
    gp = lowered(gp)
    parts = split4(nt(gp, sq[EX]))
    for j in range(4):
        s.s9[j] = lowered(parts[j])
    own_g = choose(parts, z)
    fe = w.to_z(lambda t: s.s9.at[t], lambda j: s.r9.at[j - 1])
    rows1.relay()
    g3z = choose(split4(jnp.broadcast_to(g3, (OWN, WIDTH))), z)
    fe.wait_recv()
    t = own_g
    for j in range(3):
        t = t + s.r9[j].astype(F32)
    s.t3[z] = lowered(t * g3z)
    ff = w.to_z(lambda t: s.t3.at[z], lambda j: s.t3.at[z])
    fp = w.to_z(lambda t: s.p2.at[c, pb, :, gp_cols], lambda j: s.p2.at[c, pb, :, gp_cols])
    ff.wait_recv()
    og = s.ogs[...]
    t = join4([s.t3[j].astype(F32) for j in range(4)])
    gain3 = jnp.sum(t * n3, 0, keepdims=True) / g3
    grad_two = og + rs3 * (t - n3 * jnp.mean(t * n3, -1, keepdims=True))
    gcb = lowered(grad_two)
    s.gm[c] = lowered(nt(gcb, sq[CO]))
    f7 = w.to_core((s.gm.at[c], s.gm.at[c]))
    s.p3[c, pb, :, :1920] = pack(grad_two)
    rows3 = PlaneRows(w, s.p3)
    mix_core.wait_recv()
    f7.wait_recv()

    gms = [s.gm[k].astype(F32) for k in (0, 1)]
    mxs = [join4([s.mixg[k, j].astype(F32) for j in range(4)]) for k in (0, 1)]
    gm_q = [gms[q // 2][PAD * (q % 2) : PAD * (q % 2 + 1)] for q in range(4)]
    mx_q = [mxs[q // 2][PAD * (q % 2) : PAD * (q % 2 + 1)] for q in range(4)]
    tots = [[] for q in range(4)]
    for p in range(6):
        blocks_p = []
        for q in range(4):
            col = s.wcol[48 * p : 48 * (p + 1), 16 + q : 17 + q]
            y = pair_stack(gm_q[q], p) * col
            m = mx_q[q][:, 128 * p : 128 * (p + 1)]
            tots[q].append(-jnp.sum(y * jnp.concatenate([m, m], 0), -1, keepdims=True))
            blocks_p.append(y)
        s.y6[p] = lowered(jnp.concatenate(blocks_p, 0))
        t = lowered(nt(s.y6[p], sq[CV, :, 128 * p : 128 * (p + 1)]))
        for q in range(4):
            s.gv[q, 48 * p : 48 * (p + 1), :] = t[48 * q : 48 * (q + 1)]
    lane = lanes(ROWS, 128)
    t = jnp.zeros((ROWS, 128), F32)
    for q in range(4):
        t = jnp.where(lane == q, jnp.concatenate(tots[q], 0), t)
    s.tot[...] = t
    for p in range(6):
        t = jnp.concatenate([s.bs[q, 48 * p : 48 * (p + 1), :] for q in range(4)], 0)
        s.vw1[128 * p : 128 * (p + 1), :] = lowered(tn(s.y6[p], t))
    vred = CrossReduce(w, [s.vw1, s.vr1, s.vw2, s.vr2, s.vw3, s.vr3, s.vw4])
    vred.core()
    fp.wait_recv()
    rows2 = PlaneRows(w, s.p2)

    def grads(q, carry):
        pick = lanes(ROWS, 128) == q
        tot = jnp.sum(jnp.where(pick, s.tot[...], 0.0), -1, keepdims=True)
        t = nt(s.gv[q], enc[q]) + tot
        s.gs[q] = lowered(s.es[q].astype(F32) * t)
        s.as_[q] = lowered(nn(s.gs[q], enc[q]))
        return carry

    lax.fori_loop(0, 2, grads, 0)
    rows3.relay()
    vred.plane()
    lax.fori_loop(2, 4, grads, 0)
    tiles = [[] for q in range(4)]
    for p in range(6):
        t = jnp.concatenate([s.as_[q, 48 * p : 48 * (p + 1), :] for q in range(4)], 0)
        t = nn(t, sq[CK, :, 128 * p : 128 * (p + 1)])
        for q in range(4):
            a = t[48 * q : 48 * (q + 1)]
            tiles[q].append(jnp.where(low, a[:PAD], a[PAD:]))
    num = jnp.concatenate([jnp.concatenate(tiles[q], 1) for q in range(4)], 0) * 0.125
    for k in (0, 1):
        for j, part in enumerate(split4(num[OWN * k : OWN * (k + 1)])):
            s.s7[k, j] = lowered(part)
    fc = w.to_core((s.s7.at[1 - c], s.c7))
    for p in range(6):
        t = jnp.concatenate([s.as_[q, 48 * p : 48 * (p + 1), :] for q in range(4)], 0)
        s.kw1[128 * p : 128 * (p + 1), :] = lowered(tn(s.x6[p], t))
    kred = CrossReduce(w, [s.kw1, s.kr1, s.kw2, s.kr2, s.kw3, s.kr3, s.kw4])
    fc.wait_recv()
    for j in range(4):
        s.z7[j] = lowered(s.s7[c, j].astype(F32) + s.c7[j].astype(F32))
    f8 = w.to_z(lambda t: s.z7.at[t], lambda j: s.r7.at[j - 1])
    kred.core()
    out_copies = []

    def encoding_grad(q):
        s.eg[q] = lowered(tn(s.es[q], s.gv[q]) + tn(s.gs[q], s.qk[q]))
        out_copies.append(w.local(s.eg.at[q], r.encoding_grad.at[q]))

    encoding_grad(0)
    kred.plane()
    rows2.relay()
    encoding_grad(1)

    f8.wait_recv()
    t = s.z7[z].astype(F32)
    for k in range(3):
        t = t + s.r7[k].astype(F32)
    s.gcq[z] = lowered(t)
    f9 = w.to_z(lambda t: s.gcq.at[z], lambda j: s.gcq.at[z])
    parts = split4(nn(s.acts[...], rd[...]))
    for j in range(4):
        s.s8[j] = lowered(parts[j])
    own_d = choose(parts, z)
    fo = w.to_z(lambda t: s.s8.at[t], lambda j: s.r8.at[j - 1])
    rows1.core()
    rows3.core()
    encoding_grad(2)
    encoding_grad(3)

    f9.wait_recv()
    gcq = join4([s.gcq[j].astype(F32) for j in range(4)])
    gh2 = nt(lowered(gcq), sq[CQ])
    gain2 = jnp.sum(gh2 * n2, 0, keepdims=True)
    t = gh2 * g2
    grad_one = grad_two + rs2o * (t - n2 * jnp.mean(t * n2, -1, keepdims=True))
    gab = lowered(grad_one)
    gsm = lowered(nt(gab, chip(SO))).astype(F32)
    gsum = jnp.zeros((3 * PAD, PAD), F32)
    dq, dk, dv = [], [], []
    for k in (0, 1):
        rows = slice(PAD * k, PAD * (k + 1))
        prob = probs[k]
        stacked = lowered(stack_heads(gsm[rows], 3))
        gw = nt(stacked, lowered(v3[rows]))
        gsb = lowered(prob * (gw - jnp.sum(gw * prob, -1, keepdims=True)))
        gsum = gsum + gsb.astype(F32)
        dq.append(pick_heads(nn(gsb, lowered(k3[rows])), 3) * 0.125)
        dk.append(tn(gsb, lowered(stacks[k])))
        dv.append(tn(lowered(prob), stacked))
    three = [jnp.concatenate([jnp.concatenate(t, 0), gap], 1) for t in (dq, dk, dv)]
    s.gsg[z] = lowered(join3(three))
    f10 = w.to_z(lambda t: s.gsg.at[z], lambda j: s.gsg.at[z])
    s.p4[c, pb, :, :1920] = pack(gcq)
    rows4 = PlaneRows(w, s.p4)
    s.p5[c, pb, :, :1920] = pack(grad_one)
    rows5 = PlaneRows(w, s.p5)
    vred.line()
    s.bias[...] = gsum

    def table_head(h, carry):
        v = s.bias[pl.ds(pl.multiple_of(PAD * h, 8), PAD), :]
        rows = [jnp.sum(jnp.where(bucket == b, v, 0.0), 0, keepdims=True) for b in range(BUCKETS)]
        col = jnp.sum(jnp.concatenate(rows, 0), -1, keepdims=True)
        return jnp.where(lanes(BUCKETS, 128) == 3 * z + h, col, carry)

    s.stz[z] = lax.fori_loop(0, 3, table_head, jnp.zeros((BUCKETS, 128), F32))
    ft = w.to_z(lambda t: s.stz.at[z], lambda j: s.stz.at[z])
    rows2.core()
    fo.wait_recv()
    t = r2z + own_d
    for j in range(3):
        t = t + s.r8[j].astype(F32)
    s.dog[c, z] = lowered(t)
    fg = w.to_z(lambda t: s.dog.at[c, z], lambda j: s.dog.at[c, z])
    rows1.finish()

    def half_product(ref, begin, index, rows):
        rows.finish()
        lhs = inputs_half(unpack(ref, begin, 256), c)
        s.wg[index] = lowered(nn(lhs, unpack(ref, 0, WIDTH))[:96])
        out_copies.append(w.local(s.wg.at[index], r.squares.at[index]))

    half_product(s.p3, 768, 7, rows3)

    f10.wait_recv()
    unpacked = [part3(s.gsg[j].astype(F32)) for j in range(4)]
    three = [join4([unpacked[j][k] for j in range(4)]) for k in range(3)]
    for k in range(3):
        s.p6[c, pb, :, 1920 * k : 1920 * (k + 1)] = pack(three[k])
    three = [lowered(v) for v in three]
    rows6 = PlaneRows(w, s.p6)
    gh1 = nt(three[0], chip(SQ)) + nt(three[1], chip(SK)) + nt(three[2], chip(SV))
    g1z = choose(split4(jnp.broadcast_to(g1, (OWN, WIDTH))), z)
    s.tg[z] = lowered(jnp.concatenate([gh1 * g1z[:, :PART], gap], 1))
    f11 = w.to_z(lambda t: s.tg.at[z], lambda j: s.tg.at[z])
    ft.wait_recv()
    s.stab[c, pb] = s.stz[0] + s.stz[1] + s.stz[2] + s.stz[3]
    tab_rows = PlaneSmall(w, s.stab)
    vred.spread()
    rows4.relay()
    rows5.relay()
    kred.line()
    rows2.finish()
    p2 = s.p2
    lhs = inputs_half(unpack(p2, 3072, 256), c)
    for j in range(4):
        cols = slice(WIDTH * j, WIDTH * (j + 1))
        s.gexs[:, cols] = lowered(nn(lhs, unpack(p2, WIDTH * j, WIDTH))[:96])
    out_copies.append(w.local(s.gexs, r.gex))
    f11.wait_recv()
    fg.wait_recv()
    fgc = w.to_core((s.dog.at[c], s.dog.at[c]))
    t = join4([s.tg[j].astype(F32) for j in range(4)])
    n1 = s.xs[...] * rs1
    gain1 = jnp.sum(t * n1, 0, keepdims=True) / g1
    s.dgr[c] = grad_one + rs1 * (t - n1 * jnp.mean(t * n1, -1, keepdims=True))
    fd = w.to_core((s.dgr.at[c], s.dgr.at[c]))
    s.sgain[c, pb] = jnp.concatenate([gain1, gain2, gain3, jnp.zeros((5, WIDTH), F32)], 0)
    gain_rows = PlaneSmall(w, s.sgain)
    kred.spread()
    rows6.relay()
    vred.rows.core()
    rows4.core()
    rows5.core()
    t = unpack(p2, 3328, WIDTH).astype(F32)
    lhs = lowered(lax.select(c == 1, t[:, 384:], t[:, :384]).T)
    s.gres[...] = lowered(nn(lhs, unpack(s.p1, 0, WIDTH)))
    out_copies.append(w.local(s.gres, r.gre))
    half_product(s.p4, 768, 4, rows4)
    half_product(s.p5, 768, 3, rows5)
    tab_rows.core()
    gain_rows.core()
    fgc.wait_recv()
    fd.wait_recv()
    for k in (0, 1):
        t = join4([s.dog[k, j].astype(F32) for j in range(4)])
        for m in (0, 1):
            r.decoder_out[:, 2 * k + m, :] = t[PAD * m : PAD * m + ANS]
            r.decoder_grad[:, 2 * k + m, :] = s.dgr[k, PAD * m : PAD * m + ANS, :]
    kred.rows.core()
    rows6.core()
    vred.rows.finish()
    s.wg[6] = vred.result()
    out_copies.append(w.local(s.wg.at[6], r.squares.at[6]))
    gain_rows.finish()
    tab_rows.finish()
    t = s.sgain[0, 0]
    u = s.stab[0, 0]
    for k in range(1, 8):
        t = t + s.sgain[k // 4, k % 4]
        u = u + s.stab[k // 4, k % 4]
    r.gains[...] = t
    r.table_grad[...] = u
    kred.rows.finish()
    s.wg[5] = kred.result()
    out_copies.append(w.local(s.wg.at[5], r.squares.at[5]))
    rows6.finish()
    ref = s.p6
    lhs = inputs_half(unpack(ref, 2304, 256), c)
    for k in range(3):
        s.wg[k] = lowered(nn(lhs, unpack(ref, WIDTH * k, WIDTH))[:96])
        out_copies.append(w.local(s.wg.at[k], r.squares.at[k]))
    for copy in out_copies:
        copy.wait()
    for batch in w.batches:
        batch.wait_send()


def write(dout, dgrad, eg, sq, gex, gre, gains, table, *refs):
    outs, (veg, vsq, vex, vre, weg, wsq, wex, wre, sems) = refs[:17], refs[17:]
    o_out, o_grad, o_eg, outs = outs[0], outs[1], outs[2], outs[3:]
    jobs = [(eg.at[q], veg.at[q], weg.at[q], o_eg.at[q]) for q in range(4)]
    jobs += [(gex, vex, wex, outs[8]), (gre, vre, wre, outs[9])]
    jobs += [(sq.at[k], vsq.at[k], wsq.at[k], outs[k]) for k in range(8)]
    loads = [pltpu.make_async_copy(j[0], j[1], sems.at[k]) for k, j in enumerate(jobs)]
    for copy in loads:
        copy.start()
    o_out[...] = dout[...]
    o_grad[...] = dgrad[...]
    for k in range(3):
        outs[10 + k][...] = gains[k : k + 1, :].reshape(WIDTH)
    outs[13][...] = table[...].T[:HEADS]
    stores = []
    for k, (src, near, wide, dst) in enumerate(jobs):
        loads[k].wait()
        wide[...] = near[...].astype(F32)
        stores.append(pltpu.make_async_copy(wide, dst, sems.at[len(jobs) + k]))
        stores[-1].start()
    for copy in stores:
        copy.wait()


def fused(x, enc, og, plen, pcount, buckets, wq, wk, wv, wo, wcq, wck, wcv, wco, wex, wre, g1, g2, g3, table):
    def shape(*dims, kind=F32):
        return jax.ShapeDtypeStruct(dims, kind)

    rows = shape(ANS, 4, WIDTH)
    mid = pl.pallas_call(
        layer,
        out_shape=[
            rows,
            rows,
            shape(4, SLOT, WIDTH, kind=BF),
            shape(8, 96, WIDTH, kind=BF),
            shape(96, FF, kind=BF),
            shape(384, WIDTH, kind=BF),
            shape(8, WIDTH),
            shape(BUCKETS, 128),
        ],
        in_specs=[pl.BlockSpec(memory_space=k) for k in IN_KIND.values()],
        out_specs=[pl.BlockSpec(memory_space=k) for k in OUT_KIND.values()],
        scratch_shapes=[pltpu.VMEM(*v) for v in SCRATCH.values()]
        + [pltpu.SemaphoreType.DMA((SEMAPHORES,))],
        compiler_params=pltpu.CompilerParams(
            collective_id=0, has_side_effects=True, vmem_limit_bytes=62 * 2**20
        ),
    )(
        jnp.transpose(x, (1, 0, 2)),
        jnp.transpose(og, (1, 0, 2)),
        *(plen, pcount, buckets, table.T, g1, g2, g3, enc),
        *(wq, wk, wv, wo, wcq, wck, wcv, wco, wex, wre),
    )
    near, far = pl.BlockSpec(memory_space=NEAR), pl.BlockSpec(memory_space=FAR)
    square = shape(96, WIDTH)
    out = pl.pallas_call(
        write,
        out_shape=[
            *(rows, rows, shape(4, SLOT, WIDTH)),
            *[square] * 8,
            *(shape(96, FF), shape(384, WIDTH)),
            *[shape(WIDTH)] * 3,
            shape(HEADS, BUCKETS),
        ],
        in_specs=[near, near, far, far, far, far, near, near],
        out_specs=[near, near, far, *[far] * 10, *[near] * 4],
        scratch_shapes=[
            pltpu.VMEM(dims, kind)
            for kind in (BF, F32)
            for dims in ((4, SLOT, WIDTH), (8, 96, WIDTH), (96, FF), (384, WIDTH))
        ]
        + [pltpu.SemaphoreType.DMA((28,))],
        compiler_params=pltpu.CompilerParams(vmem_limit_bytes=62 * 2**20),
    )(*mid)
    out = list(out)
    out[0], out[1] = (jnp.transpose(v, (1, 0, 2)) for v in out[:2])
    out[16] = out[16].T
    return tuple(out)


def solution(mesh):
    if dict(mesh.shape) != {"pb": 4, "pa": 8}:
        return generic(mesh)
    wide, tall = P("pb", "pa", None), P("pa", None)
    rows, whole = P("pb", None, None), P()
    return jax.shard_map(
        fused,
        mesh=mesh,
        in_specs=(rows, wide, rows, P("pb"), P("pb"), whole, *[tall] * 10, *[whole] * 4),
        out_specs=(rows, rows, wide, *[tall] * 10, *[whole] * 4),
        check_vma=False,
    )
```

```python
import math
import types

import jax
import jax.numpy as jnp
from jax import lax
from jax.experimental import pallas as pl
from jax.experimental.pallas import tpu as pltpu
from jax.sharding import PartitionSpec as P

epsilon = 1e-06
highest = lax.Precision.HIGHEST
masked_score = -1e30


def product(left, right):
    return jnp.dot(left, right, preferred_element_type=jnp.float32)


def lowered(value):
    return value.astype(jnp.bfloat16)


def norm_forward(value):
    factor = lax.rsqrt(jnp.mean(value * value, -1, keepdims=True) + epsilon)
    return (value * factor, factor)


def norm_backward(grad_out, normal, factor, gain):
    inner_term = grad_out * gain
    grad_in = factor * (inner_term - normal * jnp.mean(inner_term * normal, -1, keepdims=True))
    grad_gain = jnp.sum(grad_out * normal, (0, 1))
    return (grad_in, grad_gain)


def activate(value):
    return jax.nn.gelu(value, approximate=True)


def shard_grad(inputs, grad_rows, device_place, row_count):
    sliced = lax.dynamic_slice_in_dim(inputs, device_place * row_count, row_count, 2)
    return jnp.einsum("qak,qae->ke", sliced, grad_rows, preferred_element_type=jnp.float32)


def shards(
    decoder_in,
    encodings,
    out_grad,
    passage_len,
    passage_count,
    buckets,
    self_query,
    self_key,
    self_value,
    self_out,
    cross_query,
    cross_key,
    cross_value,
    cross_out,
    ffn_expand,
    ffn_reduce,
    norm_self,
    norm_cross,
    norm_ffn,
    bias_table,
):
    wide_count = lax.axis_size("pa")
    device_place = lax.axis_index("pa")
    stacked = jnp.stack(
        [self_query, self_key, self_value, self_out, cross_query, cross_key, cross_value, cross_out]
    )
    squares, expand_full, reduce_full = (
        lax.all_gather(stacked, "pa", axis=1, tiled=True),
        lax.all_gather(ffn_expand, "pa", axis=0, tiled=True),
        lax.all_gather(ffn_reduce, "pa", axis=0, tiled=True),
    )
    query_self = squares[0]
    key_self = squares[1]
    value_self = squares[2]
    out_self = squares[3]
    query_cross = squares[4]
    key_cross = squares[5]
    value_cross = squares[6]
    out_cross = squares[7]
    questions, answer, model_width = decoder_in.shape
    head_count = bias_table.shape[1]
    head_size = model_width // head_count
    factor = head_size ** (-0.5)
    slot_rows = encodings.shape[1]
    rows_model = model_width // wide_count
    rows_hidden = expand_full.shape[1] // wide_count

    def heads_of(value):
        return value.reshape(value.shape[0], value.shape[1], head_count, head_size)

    normal_one, factor_one = norm_forward(decoder_in)
    hidden_one = lowered(normal_one * norm_self)
    query_heads = heads_of(lowered(product(hidden_one, query_self)))
    key_heads = heads_of(lowered(product(hidden_one, key_self)))
    value_heads = heads_of(lowered(product(hidden_one, value_self)))
    onehot = (buckets[:, :, None] == jnp.arange(bias_table.shape[0])[None, None, :]).astype(
        jnp.float32
    )
    bias_scores = jnp.einsum("ijb,bh->hij", onehot, bias_table, precision=highest)
    causal = jnp.arange(answer)[:, None] >= jnp.arange(answer)[None, :]
    scores = (
        jnp.einsum("qihd,qjhd->qhij", query_heads, key_heads, preferred_element_type=jnp.float32)
        * factor
        + bias_scores[None]
    )
    scores = jnp.where(causal[None, None], scores, masked_score)
    probabilities = jax.nn.softmax(scores, -1)
    weights_self = lowered(probabilities)
    mixed_self = lowered(
        jnp.einsum("qhij,qjhd->qihd", weights_self, value_heads, preferred_element_type=jnp.float32)
    ).reshape(questions, answer, model_width)
    resid_one = decoder_in + product(mixed_self, out_self)
    normal_two, factor_two = norm_forward(resid_one)
    hidden_two = lowered(normal_two * norm_cross)
    cquery = heads_of(lowered(product(hidden_two, query_cross)))
    per_device = slot_rows // passage_len
    held_count = jnp.clip(passage_count - device_place * per_device, 0, per_device)
    valid_rows = jnp.arange(slot_rows)[None, :] < (held_count * passage_len)[:, None]

    def project(encoded):
        ckeys = lowered(product(encoded, key_cross)).reshape(
            questions, slot_rows, head_count, head_size
        )
        cvalues = lowered(product(encoded, value_cross)).reshape(
            questions, slot_rows, head_count, head_size
        )
        cscores = (
            jnp.einsum("qihd,qjhd->qhij", cquery, ckeys, preferred_element_type=jnp.float32)
            * factor
        )
        cscores = jnp.where(valid_rows[:, None, None, :], cscores, masked_score)
        return (ckeys, cvalues, cscores)

    ckeys, cvalues, cscores = project(encodings)
    row_max = lax.pmax(jnp.max(cscores, -1), "pa")
    exp_weights = jnp.exp(cscores - row_max[..., None])
    part_num = jnp.einsum(
        "qhij,qjhd->qihd", lowered(exp_weights), cvalues, preferred_element_type=jnp.float32
    )
    part_total = jnp.sum(exp_weights, -1)
    numerator, totals = lax.psum((part_num, part_total), "pa")
    totals_t = jnp.transpose(totals, (0, 2, 1))[..., None]
    mixed_cross = lowered(numerator / totals_t).reshape(questions, answer, model_width)
    resid_two = resid_one + product(mixed_cross, out_cross)
    normal_three, factor_three = norm_forward(resid_two)
    hidden_three = lowered(normal_three * norm_ffn)
    pre_act = product(hidden_three, expand_full)
    activation = lowered(activate(pre_act))
    decoder_out = resid_two + product(activation, reduce_full)
    grad_z = lowered(out_grad)
    grad_reduce = shard_grad(activation, grad_z, device_place, rows_hidden)
    grad_act = jnp.einsum("qae,fe->qaf", grad_z, reduce_full, preferred_element_type=jnp.float32)
    unused_out, gelu_back = jax.vjp(activate, pre_act)
    grad_pre = lowered(gelu_back(grad_act)[0])
    grad_expand = shard_grad(hidden_three, grad_pre, device_place, rows_model)
    grad_three = jnp.einsum(
        "qaf,kf->qak", grad_pre, expand_full, preferred_element_type=jnp.float32
    )
    back_term, grad_gain_ffn = norm_backward(grad_three, normal_three, factor_three, norm_ffn)
    grad_two = out_grad + back_term
    grad_c = lowered(grad_two)
    grad_out_cross = shard_grad(mixed_cross, grad_c, device_place, rows_model)
    grad_mix = heads_of(
        lowered(jnp.einsum("qae,ke->qak", grad_c, out_cross, preferred_element_type=jnp.float32))
    )
    grad_mix_wide = grad_mix.astype(jnp.float32)
    grad_num = lowered(grad_mix_wide / totals_t)
    grad_tot = -jnp.sum(grad_mix_wide * numerator, -1) / (totals_t[..., 0] * totals_t[..., 0])
    ckeys, cvalues, cscores = project(encodings)
    exp_weights = jnp.exp(cscores - row_max[..., None])
    grad_expo = jnp.einsum("qihd,qjhd->qhij", grad_num, cvalues, preferred_element_type=jnp.float32)
    grad_expo = grad_expo + jnp.transpose(grad_tot, (0, 2, 1))[..., None]
    grad_score = lowered(exp_weights * grad_expo)
    part_query = (
        jnp.einsum("qhij,qjhd->qihd", grad_score, ckeys, preferred_element_type=jnp.float32)
        * factor
    )
    grad_cquery = lowered(lax.psum(part_query, "pa")).reshape(questions, answer, model_width)
    grad_ckeys = lowered(
        jnp.einsum("qhij,qihd->qjhd", grad_score, cquery, preferred_element_type=jnp.float32)
        * factor
    ).reshape(questions, slot_rows, model_width)
    grad_cvalues = lowered(
        jnp.einsum(
            "qhij,qihd->qjhd", lowered(exp_weights), grad_num, preferred_element_type=jnp.float32
        )
    ).reshape(questions, slot_rows, model_width)
    encoding_grad = jnp.einsum(
        "qse,ke->qsk", grad_ckeys, key_cross, preferred_element_type=jnp.float32
    )
    encoding_grad = encoding_grad + jnp.einsum(
        "qse,ke->qsk", grad_cvalues, value_cross, preferred_element_type=jnp.float32
    )
    full_key = jnp.einsum("qsk,qse->ke", encodings, grad_ckeys, preferred_element_type=jnp.float32)
    full_value = jnp.einsum(
        "qsk,qse->ke", encodings, grad_cvalues, preferred_element_type=jnp.float32
    )
    grad_query_cross = shard_grad(hidden_two, grad_cquery, device_place, rows_model)
    grad_hidden_two = jnp.einsum(
        "qae,ke->qak", grad_cquery, query_cross, preferred_element_type=jnp.float32
    )
    back_term, grad_gain_cross = norm_backward(grad_hidden_two, normal_two, factor_two, norm_cross)
    grad_one = grad_two + back_term
    grad_a = lowered(grad_one)
    grad_out_self = shard_grad(mixed_self, grad_a, device_place, rows_model)
    grad_smix = heads_of(
        lowered(jnp.einsum("qae,ke->qak", grad_a, out_self, preferred_element_type=jnp.float32))
    )
    grad_w = jnp.einsum(
        "qihd,qjhd->qhij", grad_smix, value_heads, preferred_element_type=jnp.float32
    )
    grad_s = lowered(probabilities * (grad_w - jnp.sum(grad_w * probabilities, -1, keepdims=True)))
    grad_table = jnp.einsum(
        "ijb,hij->bh", onehot, jnp.sum(grad_s.astype(jnp.float32), 0), precision=highest
    )
    grad_sq = lowered(
        jnp.einsum("qhij,qjhd->qihd", grad_s, key_heads, preferred_element_type=jnp.float32)
        * factor
    ).reshape(questions, answer, model_width)
    grad_sk = lowered(
        jnp.einsum("qhij,qihd->qjhd", grad_s, query_heads, preferred_element_type=jnp.float32)
        * factor
    ).reshape(questions, answer, model_width)
    grad_sv = lowered(
        jnp.einsum("qhij,qihd->qjhd", weights_self, grad_smix, preferred_element_type=jnp.float32)
    ).reshape(questions, answer, model_width)
    grad_query_self = shard_grad(hidden_one, grad_sq, device_place, rows_model)
    grad_key_self = shard_grad(hidden_one, grad_sk, device_place, rows_model)
    grad_value_self = shard_grad(hidden_one, grad_sv, device_place, rows_model)
    grad_hidden_one = jnp.einsum(
        "qae,ke->qak", grad_sq, query_self, preferred_element_type=jnp.float32
    )
    grad_hidden_one = grad_hidden_one + jnp.einsum(
        "qae,ke->qak", grad_sk, key_self, preferred_element_type=jnp.float32
    )
    grad_hidden_one = grad_hidden_one + jnp.einsum(
        "qae,ke->qak", grad_sv, value_self, preferred_element_type=jnp.float32
    )
    back_term, grad_gain_self = norm_backward(grad_hidden_one, normal_one, factor_one, norm_self)
    decoder_grad = grad_one + back_term
    key_part, value_part = (
        lax.psum_scatter(full_key, "pa", scatter_dimension=0, tiled=True),
        lax.psum_scatter(full_value, "pa", scatter_dimension=0, tiled=True),
    )
    summed = lax.psum(
        (
            grad_query_self,
            grad_key_self,
            grad_value_self,
            grad_out_self,
            grad_query_cross,
            key_part,
            value_part,
            grad_out_cross,
            grad_expand,
            grad_reduce,
            grad_gain_self,
            grad_gain_cross,
            grad_gain_ffn,
            grad_table,
        ),
        "pb",
    )
    key_total = summed[5]
    value_total = summed[6]
    rest_sums = (
        summed[0],
        summed[1],
        summed[2],
        summed[3],
        summed[4],
        summed[7],
        summed[8],
        summed[9],
        summed[10],
        summed[11],
        summed[12],
        summed[13],
    )
    return (
        decoder_out,
        decoder_grad,
        encoding_grad,
        rest_sums[0],
        rest_sums[1],
        rest_sums[2],
        rest_sums[3],
        rest_sums[4],
        key_total,
        value_total,
        rest_sums[5],
        rest_sums[6],
        rest_sums[7],
        rest_sums[8],
        rest_sums[9],
        rest_sums[10],
        rest_sums[11],
    )


def generic(mesh):
    placed = (
        P("pb", None, None),
        P("pb", "pa", None),
        P("pb", None, None),
        P("pb"),
        P("pb"),
        P(),
        P("pa", None),
        P("pa", None),
        P("pa", None),
        P("pa", None),
        P("pa", None),
        P("pa", None),
        P("pa", None),
        P("pa", None),
        P("pa", None),
        P("pa", None),
        P(),
        P(),
        P(),
        P(),
    )
    return jax.shard_map(
        shards,
        mesh=mesh,
        in_specs=placed,
        out_specs=(
            P("pb", None, None),
            P("pb", None, None),
            P("pb", "pa", None),
            P("pa", None),
            P("pa", None),
            P("pa", None),
            P("pa", None),
            P("pa", None),
            P("pa", None),
            P("pa", None),
            P("pa", None),
            P("pa", None),
            P("pa", None),
            P(),
            P(),
            P(),
            P(),
        ),
        check_vma=False,
    )


MESH = pl.DeviceIdType.MESH
F32, BF = jnp.float32, jnp.bfloat16
ANS, PAD, OWN, ALL = 20, 24, 48, 96
WIDTH, HEADS, SIZE, PART = 768, 12, 64, 192
ROWS = HEADS * PAD
SLOT, FF, BUCKETS = 512, 3072, 32
CQ, CK, CV, CO, SO, SQ, SK, SV, EX, RD, EN = range(11)
GELU_A, GELU_B = 0.7978845608028654, 0.044715


def nn(a, b):
    return lax.dot_general(a, b, (((1,), (0,)), ((), ())), preferred_element_type=F32)


def nt(a, b):
    return lax.dot_general(a, b, (((1,), (1,)), ((), ())), preferred_element_type=F32)


def tn(a, b):
    return lax.dot_general(a, b, (((0,), (0,)), ((), ())), preferred_element_type=F32)


def lanes(rows, width):
    return lax.broadcasted_iota(jnp.int32, (rows, width), 1)


def split4(v):
    out = []
    for j in range(4):
        base = PART * j // 128 * 128
        t = v[:, base : base + 256]
        out.append(pltpu.roll(t, PART, 1) if PART * j != base else t)
    return out


def join4(parts):
    low = lanes(parts[0].shape[0], 128) < 64
    tiles = []
    for a, b in ((parts[0], parts[1]), (parts[2], parts[3])):
        b = pltpu.roll(b, 64, 1)
        tiles += [a[:, :128], jnp.where(low, a[:, 128:], b[:, :128]), b[:, 128:]]
    return jnp.concatenate(tiles, 1)


def join3(parts):
    low = lanes(parts[0].shape[0], 128) < 64
    a, b = parts[0], pltpu.roll(parts[1], 64, 1)
    return jnp.concatenate([a[:, :128], jnp.where(low, a[:, 128:], b[:, :128]), b[:, 128:], parts[2]], 1)


def part3(v):
    return [v[:, :256], pltpu.roll(v[:, 128:384], PART, 1), v[:, 384:]]


def choose(parts, index):
    v = parts[0]
    for j in range(1, len(parts)):
        v = lax.select(index == j, parts[j], v)
    return v


def stack_heads(v, count):
    head = lanes(*v.shape) // SIZE
    return jnp.concatenate([jnp.where(head == h, v, 0.0) for h in range(count)], 0)


def pick_heads(v, count):
    head = lanes(PAD, v.shape[1]) // SIZE
    out = jnp.zeros((PAD, v.shape[1]), F32)
    for h in range(count):
        out = out + jnp.where(head == h, v[PAD * h : PAD * (h + 1)], 0.0)
    return out


def pair_stack(v, p):
    t = v[:, 128 * p : 128 * (p + 1)]
    low = lanes(PAD, 128) < SIZE
    return jnp.concatenate([jnp.where(low, t, 0.0), jnp.where(low, 0.0, t)], 0)


SCRATCH = dict(
    sq=((9, WIDTH, WIDTH), BF),
    rd=((WIDTH, WIDTH), BF),
    enc=((4, SLOT, WIDTH), BF),
    xs=((OWN, WIDTH), F32),
    ogs=((OWN, WIDTH), F32),
    bks=((PAD, PAD), jnp.int32),
    bias=((3 * PAD, PAD), F32),
    s1=((4, OWN, 640), BF),
    r1=((3, OWN, 640), BF),
    gact=((OWN, WIDTH), F32),
    s9=((4, OWN, 256), BF),
    r9=((3, OWN, 256), BF),
    t3=((4, OWN, 256), BF),
    s2=((4, OWN, 256), BF),
    r2=((3, OWN, 256), BF),
    ag2=((2, 4, OWN, 256), BF),
    gz=((OWN, WIDTH), BF),
    acts=((OWN, WIDTH), BF),
    span=((128, 384), F32),
    x6=((6, 192, 128), BF),
    y6=((6, 192, 128), BF),
    qk=((4, ROWS, WIDTH), BF),
    gv=((4, ROWS, WIDTH), BF),
    bs=((4, ROWS, WIDTH), BF),
    as_=((4, ROWS, WIDTH), BF),
    es=((4, ROWS, SLOT), BF),
    gs=((4, ROWS, SLOT), BF),
    stat=((384, 128), F32),
    stg=((8, 8, 384), F32),
    wrow=((128, 384), F32),
    wcol=((384, 128), F32),
    s5=((2, 4, OWN, 256), BF),
    r5=((8, OWN, 256), BF),
    mixg=((2, 4, OWN, 256), BF),
    gm=((2, OWN, WIDTH), BF),
    s7=((2, 4, OWN, 256), BF),
    c7=((4, OWN, 256), BF),
    z7=((4, OWN, 256), BF),
    r7=((3, OWN, 256), BF),
    gcq=((4, OWN, 256), BF),
    s8=((4, OWN, 256), BF),
    r8=((3, OWN, 256), BF),
    dog=((2, 4, OWN, 256), BF),
    dgr=((2, OWN, WIDTH), F32),
    tot=((ROWS, 128), F32),
    gsg=((4, OWN, 640), BF),
    tg=((4, OWN, 256), BF),
    stz=((4, BUCKETS, 128), F32),
    wg=((8, 96, WIDTH), BF),
    gexs=((96, FF), BF),
    gres=((384, WIDTH), BF),
    p1=((2, 4, 16, 1920), BF),
    p2=((2, 4, 16, 10240), BF),
    p3=((2, 4, 16, 2560), BF),
    p4=((2, 4, 16, 2560), BF),
    p5=((2, 4, 16, 2560), BF),
    p6=((2, 4, 16, 6400), BF),
    sgain=((2, 4, 8, WIDTH), F32),
    stab=((2, 4, BUCKETS, 128), F32),
    kw1=((WIDTH, WIDTH), BF),
    kr1=((384, WIDTH), BF),
    kw2=((4, 96, WIDTH), BF),
    kr2=((3, 96, WIDTH), BF),
    kw3=((4, 96, 256), BF),
    kr3=((3, 96, 256), BF),
    kw4=((2, 4, 96, 256), BF),
    vw1=((WIDTH, WIDTH), BF),
    vr1=((384, WIDTH), BF),
    vw2=((4, 96, WIDTH), BF),
    vr2=((3, 96, WIDTH), BF),
    vw3=((4, 96, 256), BF),
    vr3=((3, 96, 256), BF),
    vw4=((2, 4, 96, 256), BF),
    eg=((4, SLOT, WIDTH), BF),
)
SEMAPHORES = 181
NEAR, SCALAR, FAR = pltpu.VMEM, pltpu.SMEM, pl.ANY
IN_KIND = dict(
    x=NEAR, og=NEAR, plen=SCALAR, pcount=SCALAR, buckets=NEAR, table=SCALAR,
    g1=NEAR, g2=NEAR, g3=NEAR, enc_h=FAR,
    wq=FAR, wk=FAR, wv=FAR, wo=FAR, wcq=FAR, wck=FAR, wcv=FAR, wco=FAR, wex=FAR, wre=FAR,
)
OUT_KIND = dict(
    decoder_out=NEAR, decoder_grad=NEAR, encoding_grad=FAR, squares=FAR, gex=FAR, gre=FAR, gains=NEAR, table_grad=NEAR,
)


class Batch:
    def __init__(self, wire, span):
        self.span, self.sent, self.landed = span, wire.next(), wire.next()
        wire.batches.append(self)

    def wait_recv(self):
        pltpu.make_async_copy(self.span, self.span, self.landed).wait()

    def wait_send(self):
        pltpu.make_async_copy(self.span, self.span, self.sent).wait()


class Wire:
    def __init__(self, sems, narrow, wide):
        self.sems, self.count, self.batches = sems, 0, []
        self.narrow, self.wide = narrow, wide
        self.pb, self.pa = lax.axis_index("pb"), lax.axis_index("pa")
        self.z, self.c = self.pa // 2, lax.rem(self.pa, 2)

    def next(self):
        self.count += 1
        return self.sems.at[self.count - 1]

    def local(self, src, dst):
        copy = pltpu.make_async_copy(src, dst, self.next())
        copy.start()
        return copy

    def span(self, size, dtype):
        if dtype == F32:
            return self.wide.at[pl.ds(0, size // 384), :]
        lane = next(n for n in (384, 768, 640, 512, 256, 128) if size % (16 * n) == 0 and size <= n * WIDTH)
        return self.narrow.at[0, pl.ds(0, size // lane), pl.ds(0, lane)]

    def batch(self, copies):
        first = copies[0][0]
        span = first
        if len(copies) > 1:
            span = self.span(sum(math.prod(src.shape) for src, _, _, _ in copies), first.dtype)
        out = Batch(self, span)
        for src, dst, pb, pa in copies:
            pltpu.make_async_remote_copy(
                src_ref=src,
                dst_ref=dst,
                send_sem=out.sent,
                recv_sem=out.landed,
                device_id=(pb, pa),
                device_id_type=MESH,
            ).start()
        return out

    def zpeer(self, j):
        return lax.rem(self.z + j, 4)

    def ppeer(self, j):
        return lax.rem(self.pb + j, 4)

    def xside(self):
        return self.pb + 1 - 2 * lax.rem(self.pb, 2)

    def yside(self):
        return lax.rem(self.pb + 2, 4)

    def to_core(self, *pairs):
        return self.batch([(src, dst, self.pb, self.pa + 1 - 2 * self.c) for src, dst in pairs])

    def to_z(self, src_of, dst_of):
        peers = [(self.zpeer(j), j) for j in (1, 2, 3)]
        return self.batch([(src_of(t), dst_of(j), self.pb, 2 * t + self.c) for t, j in peers])

    def to_column(self, src_of, dst_of):
        peers = [(lax.rem(self.pa + j, 8), j) for j in range(1, 8)]
        return self.batch([(src_of(t), dst_of(j), self.pb, t) for t, j in peers])

    def to_plane(self, src_of, dst_of):
        peers = [(self.ppeer(j), j) for j in (1, 2, 3)]
        return self.batch([(src_of(t), dst_of(j), t, self.pa) for t, j in peers])

    def to_sides(self, refs):
        sides = (self.xside(), self.yside())
        return self.batch([(ref, ref, side, self.pa) for ref in refs for side in sides])


class Gather:
    def __init__(self, wire, sq, index, source, wide=False):
        self.w, self.sq, self.index, self.source, self.wide = wire, sq, index, source, wide
        row = pl.multiple_of(48 * lax.rem(wire.pb, 2), 16)

        def block(t):
            lane = 384 * (wire.pb // 2) + (WIDTH * t if wide else 0)
            return source.at[pl.ds(row, 48), pl.ds(pl.multiple_of(lane, 128), 384)]

        self.a = wire.to_z(block, lambda j: self.part(wire.z, wire.pb, 0, 384))

    def part(self, z, pb, begin, size):
        row = pl.multiple_of(96 * (2 * z + self.w.c) + 48 * lax.rem(pb, 2), 16)
        lane = pl.multiple_of(384 * (pb // 2) + begin, 128)
        return self.sq.at[self.index, pl.ds(row, 48), pl.ds(lane, size)]

    def plane(self):
        w = self.w
        self.a.wait_recv()
        self.a = w.to_sides([self.part(w.zpeer(i), w.pb, 0, 384) for i in (1, 2, 3)])

    def relay(self):
        w = self.w
        self.a.wait_recv()
        copies = []
        cut = 128 if self.index % 2 else 256
        for i in (1, 2, 3):
            ref = self.part(w.zpeer(i), w.xside(), 0, cut)
            copies.append((ref, ref, w.yside(), w.pa))
            ref = self.part(w.zpeer(i), w.yside(), cut, 384 - cut)
            copies.append((ref, ref, w.xside(), w.pa))
        self.a = w.batch(copies)

    def core(self):
        w = self.w
        self.a.wait_recv()
        refs = []
        for i in (1, 2, 3):
            row = pl.multiple_of(96 * (2 * w.zpeer(i) + w.c), 16)
            refs.append(self.sq.at[self.index, pl.ds(row, 96), :])
        self.a = w.to_core(*[(ref, ref) for ref in refs])

    def finish(self):
        self.a.wait_recv()


class PlaneRows:
    def __init__(self, wire, ref):
        self.w, self.ref = wire, ref
        self.a = wire.to_sides([ref.at[wire.c, wire.pb]])

    def relay(self):
        w = self.w
        self.a.wait_recv()
        size = self.ref.shape[3]
        half = size // 256 * 128
        a = self.ref.at[w.c, w.xside(), :, pl.ds(0, half)]
        b = self.ref.at[w.c, w.yside(), :, pl.ds(half, size - half)]
        self.a = w.batch([(a, a, w.yside(), w.pa), (b, b, w.xside(), w.pa)])

    def core(self):
        self.a.wait_recv()
        src = self.ref.at[self.w.c]
        self.a = self.w.to_core((src, src))

    def finish(self):
        self.a.wait_recv()


class PlaneSmall(PlaneRows):
    def __init__(self, wire, ref):
        self.w, self.ref = wire, ref
        src = ref.at[wire.c, wire.pb]
        self.a = wire.to_plane(lambda t: src, lambda j: src)


def pack(v):
    half = v.shape[1] // 2
    last = jnp.where(
        lax.broadcasted_iota(jnp.int32, (8, v.shape[1]), 0) < 4, v[16:24], pltpu.roll(v[40:48], 4, 0)
    )
    last = jnp.concatenate([last[:, :half], last[:, half:]], 0)
    return lowered(jnp.concatenate([v[:16], v[24:40], last], 1))


def unpack(ref, begin, width):
    begin = begin * 5 // 2
    a = ref[:, :, :, begin : begin + width].reshape(128, width)
    b = ref[:, :, :, begin + width : begin + 2 * width].reshape(128, width)
    t = ref[:, :, :, begin + 2 * width : begin + width * 5 // 2].astype(F32)
    t = [t[:, :, 8 * k : 8 * k + 8, :].reshape(64, width // 2) for k in (0, 1)]
    return jnp.concatenate([a, b, lowered(jnp.concatenate(t, 1))], 0)


class CrossReduce:
    def __init__(self, wire, refs):
        self.w, self.refs = wire, refs

    def core(self):
        w, (w1, r1, w2, r2, w3, r3, w4) = self.w, self.refs
        row = pl.multiple_of(384 * (1 - w.c), 16)
        self.a = w.to_core((w1.at[pl.ds(row, 384), :], r1))

    def plane(self):
        w, (w1, r1, w2, r2, w3, r3, w4) = self.w, self.refs
        self.a.wait_recv()
        for k in range(4):
            row = pl.multiple_of(384 * w.c + 96 * k, 16)
            t = w1[pl.ds(row, 96), :].astype(F32) + r1[96 * k : 96 * (k + 1), :].astype(F32)
            w2[k] = lowered(t)
        self.b = w.to_plane(lambda t: w2.at[t], lambda j: r2.at[j - 1])

    def line(self):
        w, (w1, r1, w2, r2, w3, r3, w4) = self.w, self.refs
        self.b.wait_recv()
        t = w2[w.pb].astype(F32)
        for j in range(3):
            t = t + r2[j].astype(F32)
        for j, part in enumerate(split4(t)):
            w3[j] = lowered(part)
        self.d = w.to_z(lambda t: w3.at[t], lambda j: r3.at[j - 1])

    def spread(self):
        w, (w1, r1, w2, r2, w3, r3, w4) = self.w, self.refs
        self.d.wait_recv()
        t = w3[w.z].astype(F32)
        for j in range(3):
            t = t + r3[j].astype(F32)
        w4[w.c, w.pb] = lowered(t)
        self.rows = PlaneSmall(w, w4)

    def result(self):
        w4 = self.refs[-1]
        t = w4[...].astype(F32).reshape(WIDTH, 256)
        t = lax.select(self.w.c == 1, pltpu.roll(t, 160, 1), t)[:, :128]
        return lowered(t.T[:96])


def inputs_half(t, c):
    t = t.astype(F32)
    t = lax.select(c == 1, pltpu.roll(t, 160, 1), t)[:, :128]
    return lowered(t.T)


def layer(*refs):
    names = (*IN_KIND, *OUT_KIND)
    r = types.SimpleNamespace(**dict(zip(names, refs)))
    s = types.SimpleNamespace(**dict(zip(SCRATCH, refs[len(names) :])))
    w = Wire(refs[-1], s.sq, s.span)
    pb, pa, z, c = w.pb, w.pa, w.z, w.c
    sq, rd, enc = s.sq, s.rd, s.enc

    barrier = pltpu.get_barrier_semaphore()
    for j in range(1, 8):
        pl.semaphore_signal(
            barrier, inc=1, device_id=(pb, lax.rem(pa + j, 8)), device_id_type=MESH
        )
    for j in (1, 2, 3):
        pl.semaphore_signal(barrier, inc=1, device_id=(w.ppeer(j), pa), device_id_type=MESH)

    squares = [r.wcq, r.wck, r.wcv, r.wco, r.wo, r.wq, r.wk, r.wv]
    own_rows = pl.ds(pl.multiple_of(96 * pa, 16), 96)
    red_rows = pl.ds(pl.multiple_of(384 * c, 16), 384)
    order = (SQ, SK, SV, CQ, CK, SO, CV, CO)
    held = {i: w.local(squares[i], sq.at[i, own_rows, :]) for i in order}
    chip_cols = pl.ds(pl.multiple_of(WIDTH * z, 128), WIDTH)
    held[EX] = w.local(r.wex.at[:, chip_cols], sq.at[EX, own_rows, :])
    held[RD] = w.local(r.wre, rd.at[red_rows, :])
    held[EN] = w.local(r.enc_h, enc)

    for dst, src in ((s.xs, r.x), (s.ogs, r.og)):
        dst[...] = jnp.zeros((OWN, WIDTH), F32)
        for k in (0, 1):
            dst[PAD * k : PAD * k + ANS, :] = lax.select(c == 1, src[:, 2 + k, :], src[:, k, :])
    s.bks[...] = jnp.zeros((PAD, PAD), jnp.int32)
    s.bks[:ANS, :ANS] = r.buckets[...]
    g1, g2, g3 = [ref[...].reshape(1, WIDTH) for ref in (r.g1, r.g2, r.g3)]
    x = s.xs[...]
    rs1 = lax.rsqrt(jnp.mean(x * x, -1, keepdims=True) + epsilon)
    h1z = choose(split4(x * rs1 * g1), z)
    xz = choose(split4(x), z)
    h1b = lowered(h1z)
    s.p6[c, pb, :, 5760:6400] = pack(h1z)
    s.p1[c, pb] = pack(s.ogs[...])
    s.gz[...] = lowered(s.ogs[...])

    pl.semaphore_wait(barrier, 10)
    other = [w.to_core(*[(squares[i], sq.at[i, own_rows, :]) for i in (SQ, SK, SV)])]
    gather_q = Gather(w, sq, CQ, r.wcq)
    other += [
        w.to_core((r.wre, rd.at[red_rows, :])),
        w.to_core(*[(squares[i], sq.at[i, own_rows, :]) for i in (SO, CQ, CK)]),
        w.to_core(
            *[(squares[i], sq.at[i, own_rows, :]) for i in (CV, CO)],
            (r.wex.at[:, chip_cols], sq.at[EX, own_rows, :]),
        ),
    ]

    def chip(i):
        return sq[i, pl.ds(pl.multiple_of(PART * z, 16), PART), :]

    parts = []
    for i in (SQ, SK, SV):
        held[i].wait()
        if i == SQ:
            other[0].wait_recv()
        parts.append(split4(nn(h1b[:, :PART], chip(i))))
    blocks = [join3([parts[k][j] for k in range(3)]) for j in range(4)]
    for j in range(4):
        s.s1[j] = lowered(blocks[j])
    own_qkv = choose(blocks, z)
    f1 = w.to_z(lambda t: s.s1.at[t], lambda j: s.r1.at[j - 1])
    gather_k = Gather(w, sq, CK, r.wck)

    bucket = s.bks[...]

    def bias_head(h, carry):
        v = jnp.zeros((PAD, PAD), F32)
        for b in range(BUCKETS):
            v = jnp.where(bucket == b, r.table[3 * z + h, b], v)
        s.bias[pl.ds(pl.multiple_of(PAD * h, 8), PAD), :] = v
        return carry

    lax.fori_loop(0, 3, bias_head, 0)
    held[RD].wait()
    other[1].wait_recv()
    s.gact[...] = nt(s.gz[...], rd[...])

    gather_q.plane()
    f1.wait_recv()
    gather_q.relay()
    v = own_qkv
    for j in range(3):
        v = v + s.r1[j].astype(F32)
    q3, k3, v3 = [lowered(t).astype(F32)[:, :PART] for t in part3(v)]

    def attend(stacked, keys, bias):
        i = lax.broadcasted_iota(jnp.int32, (PAD, PAD), 0)
        j = lax.broadcasted_iota(jnp.int32, (PAD, PAD), 1)
        seen = jnp.concatenate([(j <= i).astype(F32)] * 3, 0) > 0.5
        t = jnp.where(seen, nt(lowered(stacked), lowered(keys)) + bias, masked_score)
        t = jnp.exp(t - jnp.max(t, -1, keepdims=True))
        return t / jnp.sum(t, -1, keepdims=True)

    mixes, probs, stacks = [], [], []
    for k in (0, 1):
        rows = slice(PAD * k, PAD * (k + 1))
        stacks.append(stack_heads(q3[rows] * 0.125, 3))
        probs.append(attend(stacks[k], k3[rows], s.bias[...]))
        mixes.append(pick_heads(nn(lowered(probs[k]), lowered(v3[rows])), 3))
    mixb = lowered(jnp.concatenate(mixes, 0))
    gap = jnp.zeros((OWN, 64), F32)
    s.p5[c, pb, :, 1920:2560] = pack(jnp.concatenate([jnp.concatenate(mixes, 0), gap], 1))
    held[SO].wait()
    other[2].wait_recv()
    parts = split4(nn(mixb, chip(SO)))
    for j in range(4):
        s.s2[j] = lowered(parts[j])
    own_o = choose(parts, z)
    f2 = w.to_z(lambda t: s.s2.at[t], lambda j: s.r2.at[j - 1])
    gather_q.core()
    gather_k.plane()
    gather_v = Gather(w, sq, CV, r.wcv)

    f2.wait_recv()
    r1z = xz + own_o
    for j in range(3):
        r1z = r1z + s.r2[j].astype(F32)
    counts = lanes(OWN, 256) < PART
    g2z = choose(split4(jnp.broadcast_to(g2, (OWN, WIDTH))), z)
    square = jnp.sum(jnp.where(counts, r1z * r1z, 0.0), -1, keepdims=True)
    high = lowered(square).astype(F32)
    tail = jnp.where(lanes(OWN, 256) < 224, high, square - high)
    s.ag2[c, z] = lowered(jnp.where(counts, r1z * g2z, tail))
    f3 = w.to_z(lambda t: s.ag2.at[c, z], lambda j: s.ag2.at[c, z])
    gather_k.relay()
    gather_v.plane()

    f3.wait_recv()
    f3c = w.to_core((s.ag2.at[c], s.ag2.at[c]))
    gather_k.core()
    gather_o = Gather(w, sq, CO, r.wco)
    gather_x = Gather(w, sq, EX, r.wex, True)
    f3c.wait_recv()
    blocks = [[s.ag2[k, j].astype(F32) for j in range(4)] for k in (0, 1)]
    rs2 = []
    for k in (0, 1):
        t = blocks[k][0] + blocks[k][1] + blocks[k][2] + blocks[k][3]
        lane = lanes(OWN, 256)
        t = jnp.sum(jnp.where((lane == 192) | (lane == 224), t, 0.0), -1, keepdims=True)
        rs2.append(lax.rsqrt(t * (1.0 / WIDTH) + epsilon))
    gather_q.finish()
    held[CQ].wait()
    cq = jnp.zeros((ALL, WIDTH), F32)
    for j in range(4):
        t = jnp.concatenate([s.ag2[0, j], s.ag2[1, j]], 0)[:, :PART]
        cq = cq + nn(t, sq[CQ, PART * j : PART * (j + 1), :])
    cq = cq * jnp.concatenate(rs2, 0)
    cq = lowered(cq).astype(F32) * 0.125
    gather_k.finish()
    gather_v.relay()
    held[CK].wait()
    for p in range(6):
        t = jnp.concatenate([pair_stack(cq[PAD * q : PAD * (q + 1)], p) for q in range(4)], 0)
        s.x6[p] = lowered(t)
        t = lowered(nt(s.x6[p], sq[CK, :, 128 * p : 128 * (p + 1)]))
        for q in range(4):
            s.qk[q, 48 * p : 48 * (p + 1), :] = t[48 * q : 48 * (q + 1)]
    held[EN].wait()
    gather_v.core()
    s.stat[...] = jnp.zeros((384, 128), F32)

    def scores(q, carry):
        size = r.plen[q]
        per = lax.select(size <= SLOT // 2, 2, 1)
        kept = jnp.minimum(jnp.maximum(r.pcount[q] - pa * per, 0), per) * size
        valid = lanes(ROWS, SLOT) < kept
        t = jnp.where(valid, nt(s.qk[q], enc[q]), masked_score)
        top = jnp.max(t, -1, keepdims=True)
        t = jnp.where(valid, jnp.exp(t - top), 0.0)
        total = jnp.sum(t, -1, keepdims=True)
        s.es[q] = lowered(t)
        s.bs[q] = lowered(nn(s.es[q], enc[q]))
        lane = lanes(ROWS, 128)
        old = s.stat[:ROWS, :]
        s.stat[:ROWS, :] = jnp.where(lane == q, top, jnp.where(lane == 4 + q, total, old))
        return carry

    lax.fori_loop(0, 4, scores, 0)
    s.stg[pa] = s.stat[...].T[:8]
    f4 = w.to_column(lambda t: s.stg.at[pa], lambda j: s.stg.at[pa])
    gather_o.plane()
    gather_x.plane()
    gather_v.finish()
    held[CV].wait()
    other[3].wait_recv()
    low = lanes(PAD, 128) < SIZE
    tiles = [[] for q in range(4)]
    for p in range(6):
        t = jnp.concatenate([s.bs[q, 48 * p : 48 * (p + 1), :] for q in range(4)], 0)
        t = nn(t, sq[CV, :, 128 * p : 128 * (p + 1)])
        for q in range(4):
            a = t[48 * q : 48 * (q + 1)]
            tiles[q].append(jnp.where(low, a[:PAD], a[PAD:]))
    num = jnp.concatenate([jnp.concatenate(tiles[q], 1) for q in range(4)], 0)
    for k in (0, 1):
        for j, part in enumerate(split4(num[OWN * k : OWN * (k + 1)])):
            s.s5[k, j] = lowered(part)
    f5 = w.to_column(lambda t: s.s5.at[lax.rem(t, 2), t // 2], lambda j: s.r5.at[pa])
    s.r5[pa] = s.s5[c, z]
    rows1 = PlaneRows(w, s.p1)
    r1full = join4([s.ag2[c, j].astype(F32) for j in range(4)]) / g2
    rs2o = lax.select(c == 1, rs2[1], rs2[0])
    n2 = r1full * rs2o
    s.p4[c, pb, :, 1920:2560] = pack(choose(split4(n2 * g2), z))
    gather_o.relay()
    gather_x.relay()

    f4.wait_recv()
    f5.wait_recv()
    stats = [s.stg[k] for k in range(8)]
    top = stats[0]
    for k in range(1, 8):
        top = jnp.maximum(top, stats[k])
    scale = [jnp.exp(t - top) for t in stats]
    total = jnp.zeros((8, 384), F32)
    for k in range(8):
        total = total + scale[k] * pltpu.roll(stats[k], 4, 0)
    inverse = 1.0 / total
    s.wrow[...] = jnp.zeros((128, 384), F32)
    mine = jnp.zeros((8, 384), F32)
    for k in range(8):
        t = scale[k] * inverse
        mine = lax.select(pa == k, t, mine)
        s.wrow[2 * k : 2 * k + 2, :] = lax.select(c == 1, t[2:4], t[0:2])
    s.wrow[16:20, :] = mine[0:4]
    s.wcol[...] = s.wrow[...].T
    w3 = s.wcol[pl.ds(pl.multiple_of(3 * PAD * z, 8), 3 * PAD), :]
    lane = lanes(PAD, 256)
    sums = [jnp.zeros((PAD, 256), F32) for k in (0, 1)]
    for m in range(8):
        block = s.r5[m].astype(F32)
        for k in (0, 1):
            col = [w3[PAD * h : PAD * (h + 1), 2 * m + k : 2 * m + k + 1] for h in range(3)]
            t = jnp.where(lane < 64, col[0], jnp.where(lane < 128, col[1], col[2]))
            sums[k] = sums[k] + t * block[PAD * k : PAD * (k + 1)]
    mixc = jnp.concatenate(sums, 0)
    s.mixg[c, z] = lowered(mixc)
    s.p3[c, pb, :, 1920:2560] = pack(mixc)
    f6 = w.to_z(lambda t: s.mixg.at[c, z], lambda j: s.mixg.at[c, z])
    gather_o.core()
    gather_x.core()
    held[CO].wait()
    gather_o.finish()
    f6.wait_recv()
    mix_core = w.to_core((s.mixg.at[c], s.mixg.at[c]))
    after = jnp.zeros((OWN, WIDTH), F32)
    for j in range(4):
        after = after + nn(s.mixg[c, j][:, :PART], sq[CO, PART * j : PART * (j + 1), :])
    r2z = r1z + choose(split4(after), z)
    resid = r1full + after
    rs3 = lax.rsqrt(jnp.mean(resid * resid, -1, keepdims=True) + epsilon)
    n3 = resid * rs3
    h3 = lowered(n3 * g3)
    s.p2[c, pb, :, 7680:8320] = pack(choose(split4(n3 * g3), z))
    gather_x.finish()
    held[EX].wait()
    v = nn(h3, sq[EX])
    t = jnp.tanh(GELU_A * (v + GELU_B * v * v * v))
    act = 0.5 * v * (1.0 + t)
    s.acts[...] = lowered(act)
    s.p2[c, pb, :, 8320:10240] = pack(act)
    slope = 0.5 * (1.0 + t) + 0.5 * v * (1.0 - t * t) * GELU_A * (1.0 + 3.0 * GELU_B * v * v)
    gp = s.gact[...] * slope
    gp_cols = pl.ds(pl.multiple_of(1920 * z, 128), 1920)
    s.p2[c, pb, :, gp_cols] = pack(gp)
    gp = lowered(gp)
    parts = split4(nt(gp, sq[EX]))
    for j in range(4):
        s.s9[j] = lowered(parts[j])
    own_g = choose(parts, z)
    fe = w.to_z(lambda t: s.s9.at[t], lambda j: s.r9.at[j - 1])
    rows1.relay()
    g3z = choose(split4(jnp.broadcast_to(g3, (OWN, WIDTH))), z)
    fe.wait_recv()
    t = own_g
    for j in range(3):
        t = t + s.r9[j].astype(F32)
    s.t3[z] = lowered(t * g3z)
    ff = w.to_z(lambda t: s.t3.at[z], lambda j: s.t3.at[z])
    fp = w.to_z(lambda t: s.p2.at[c, pb, :, gp_cols], lambda j: s.p2.at[c, pb, :, gp_cols])
    ff.wait_recv()
    og = s.ogs[...]
    t = join4([s.t3[j].astype(F32) for j in range(4)])
    gain3 = jnp.sum(t * n3, 0, keepdims=True) / g3
    grad_two = og + rs3 * (t - n3 * jnp.mean(t * n3, -1, keepdims=True))
    gcb = lowered(grad_two)
    s.gm[c] = lowered(nt(gcb, sq[CO]))
    f7 = w.to_core((s.gm.at[c], s.gm.at[c]))
    s.p3[c, pb, :, :1920] = pack(grad_two)
    rows3 = PlaneRows(w, s.p3)
    mix_core.wait_recv()
    f7.wait_recv()

    gms = [s.gm[k].astype(F32) for k in (0, 1)]
    mxs = [join4([s.mixg[k, j].astype(F32) for j in range(4)]) for k in (0, 1)]
    gm_q = [gms[q // 2][PAD * (q % 2) : PAD * (q % 2 + 1)] for q in range(4)]
    mx_q = [mxs[q // 2][PAD * (q % 2) : PAD * (q % 2 + 1)] for q in range(4)]
    tots = [[] for q in range(4)]
    for p in range(6):
        blocks_p = []
        for q in range(4):
            col = s.wcol[48 * p : 48 * (p + 1), 16 + q : 17 + q]
            y = pair_stack(gm_q[q], p) * col
            m = mx_q[q][:, 128 * p : 128 * (p + 1)]
            tots[q].append(-jnp.sum(y * jnp.concatenate([m, m], 0), -1, keepdims=True))
            blocks_p.append(y)
        s.y6[p] = lowered(jnp.concatenate(blocks_p, 0))
        t = lowered(nt(s.y6[p], sq[CV, :, 128 * p : 128 * (p + 1)]))
        for q in range(4):
            s.gv[q, 48 * p : 48 * (p + 1), :] = t[48 * q : 48 * (q + 1)]
    lane = lanes(ROWS, 128)
    t = jnp.zeros((ROWS, 128), F32)
    for q in range(4):
        t = jnp.where(lane == q, jnp.concatenate(tots[q], 0), t)
    s.tot[...] = t
    for p in range(6):
        t = jnp.concatenate([s.bs[q, 48 * p : 48 * (p + 1), :] for q in range(4)], 0)
        s.vw1[128 * p : 128 * (p + 1), :] = lowered(tn(s.y6[p], t))
    vred = CrossReduce(w, [s.vw1, s.vr1, s.vw2, s.vr2, s.vw3, s.vr3, s.vw4])
    vred.core()
    fp.wait_recv()
    rows2 = PlaneRows(w, s.p2)

    def grads(q, carry):
        pick = lanes(ROWS, 128) == q
        tot = jnp.sum(jnp.where(pick, s.tot[...], 0.0), -1, keepdims=True)
        t = nt(s.gv[q], enc[q]) + tot
        s.gs[q] = lowered(s.es[q].astype(F32) * t)
        s.as_[q] = lowered(nn(s.gs[q], enc[q]))
        return carry

    lax.fori_loop(0, 2, grads, 0)
    rows3.relay()
    vred.plane()
    lax.fori_loop(2, 4, grads, 0)
    tiles = [[] for q in range(4)]
    for p in range(6):
        t = jnp.concatenate([s.as_[q, 48 * p : 48 * (p + 1), :] for q in range(4)], 0)
        t = nn(t, sq[CK, :, 128 * p : 128 * (p + 1)])
        for q in range(4):
            a = t[48 * q : 48 * (q + 1)]
            tiles[q].append(jnp.where(low, a[:PAD], a[PAD:]))
    num = jnp.concatenate([jnp.concatenate(tiles[q], 1) for q in range(4)], 0) * 0.125
    for k in (0, 1):
        for j, part in enumerate(split4(num[OWN * k : OWN * (k + 1)])):
            s.s7[k, j] = lowered(part)
    fc = w.to_core((s.s7.at[1 - c], s.c7))
    for p in range(6):
        t = jnp.concatenate([s.as_[q, 48 * p : 48 * (p + 1), :] for q in range(4)], 0)
        s.kw1[128 * p : 128 * (p + 1), :] = lowered(tn(s.x6[p], t))
    kred = CrossReduce(w, [s.kw1, s.kr1, s.kw2, s.kr2, s.kw3, s.kr3, s.kw4])
    fc.wait_recv()
    for j in range(4):
        s.z7[j] = lowered(s.s7[c, j].astype(F32) + s.c7[j].astype(F32))
    f8 = w.to_z(lambda t: s.z7.at[t], lambda j: s.r7.at[j - 1])
    kred.core()
    out_copies = []

    def encoding_grad(q):
        s.eg[q] = lowered(tn(s.es[q], s.gv[q]) + tn(s.gs[q], s.qk[q]))
        out_copies.append(w.local(s.eg.at[q], r.encoding_grad.at[q]))

    encoding_grad(0)
    kred.plane()
    rows2.relay()
    encoding_grad(1)

    f8.wait_recv()
    t = s.z7[z].astype(F32)
    for k in range(3):
        t = t + s.r7[k].astype(F32)
    s.gcq[z] = lowered(t)
    f9 = w.to_z(lambda t: s.gcq.at[z], lambda j: s.gcq.at[z])
    parts = split4(nn(s.acts[...], rd[...]))
    for j in range(4):
        s.s8[j] = lowered(parts[j])
    own_d = choose(parts, z)
    fo = w.to_z(lambda t: s.s8.at[t], lambda j: s.r8.at[j - 1])
    rows1.core()
    rows3.core()
    encoding_grad(2)
    encoding_grad(3)

    f9.wait_recv()
    gcq = join4([s.gcq[j].astype(F32) for j in range(4)])
    gh2 = nt(lowered(gcq), sq[CQ])
    gain2 = jnp.sum(gh2 * n2, 0, keepdims=True)
    t = gh2 * g2
    grad_one = grad_two + rs2o * (t - n2 * jnp.mean(t * n2, -1, keepdims=True))
    gab = lowered(grad_one)
    gsm = lowered(nt(gab, chip(SO))).astype(F32)
    gsum = jnp.zeros((3 * PAD, PAD), F32)
    dq, dk, dv = [], [], []
    for k in (0, 1):
        rows = slice(PAD * k, PAD * (k + 1))
        prob = probs[k]
        stacked = lowered(stack_heads(gsm[rows], 3))
        gw = nt(stacked, lowered(v3[rows]))
        gsb = lowered(prob * (gw - jnp.sum(gw * prob, -1, keepdims=True)))
        gsum = gsum + gsb.astype(F32)
        dq.append(pick_heads(nn(gsb, lowered(k3[rows])), 3) * 0.125)
        dk.append(tn(gsb, lowered(stacks[k])))
        dv.append(tn(lowered(prob), stacked))
    three = [jnp.concatenate([jnp.concatenate(t, 0), gap], 1) for t in (dq, dk, dv)]
    s.gsg[z] = lowered(join3(three))
    f10 = w.to_z(lambda t: s.gsg.at[z], lambda j: s.gsg.at[z])
    s.p4[c, pb, :, :1920] = pack(gcq)
    rows4 = PlaneRows(w, s.p4)
    s.p5[c, pb, :, :1920] = pack(grad_one)
    rows5 = PlaneRows(w, s.p5)
    vred.line()
    s.bias[...] = gsum

    def table_head(h, carry):
        v = s.bias[pl.ds(pl.multiple_of(PAD * h, 8), PAD), :]
        rows = [jnp.sum(jnp.where(bucket == b, v, 0.0), 0, keepdims=True) for b in range(BUCKETS)]
        col = jnp.sum(jnp.concatenate(rows, 0), -1, keepdims=True)
        return jnp.where(lanes(BUCKETS, 128) == 3 * z + h, col, carry)

    s.stz[z] = lax.fori_loop(0, 3, table_head, jnp.zeros((BUCKETS, 128), F32))
    ft = w.to_z(lambda t: s.stz.at[z], lambda j: s.stz.at[z])
    rows2.core()
    fo.wait_recv()
    t = r2z + own_d
    for j in range(3):
        t = t + s.r8[j].astype(F32)
    s.dog[c, z] = lowered(t)
    fg = w.to_z(lambda t: s.dog.at[c, z], lambda j: s.dog.at[c, z])
    rows1.finish()

    def half_product(ref, begin, index, rows):
        rows.finish()
        lhs = inputs_half(unpack(ref, begin, 256), c)
        s.wg[index] = lowered(nn(lhs, unpack(ref, 0, WIDTH))[:96])
        out_copies.append(w.local(s.wg.at[index], r.squares.at[index]))

    half_product(s.p3, 768, 7, rows3)

    f10.wait_recv()
    unpacked = [part3(s.gsg[j].astype(F32)) for j in range(4)]
    three = [join4([unpacked[j][k] for j in range(4)]) for k in range(3)]
    for k in range(3):
        s.p6[c, pb, :, 1920 * k : 1920 * (k + 1)] = pack(three[k])
    three = [lowered(v) for v in three]
    rows6 = PlaneRows(w, s.p6)
    gh1 = nt(three[0], chip(SQ)) + nt(three[1], chip(SK)) + nt(three[2], chip(SV))
    g1z = choose(split4(jnp.broadcast_to(g1, (OWN, WIDTH))), z)
    s.tg[z] = lowered(jnp.concatenate([gh1 * g1z[:, :PART], gap], 1))
    f11 = w.to_z(lambda t: s.tg.at[z], lambda j: s.tg.at[z])
    ft.wait_recv()
    s.stab[c, pb] = s.stz[0] + s.stz[1] + s.stz[2] + s.stz[3]
    tab_rows = PlaneSmall(w, s.stab)
    kred.line()
    vred.spread()
    rows2.finish()
    p2 = s.p2
    lhs = inputs_half(unpack(p2, 3072, 256), c)
    for j in range(4):
        cols = slice(WIDTH * j, WIDTH * (j + 1))
        s.gexs[:, cols] = lowered(nn(lhs, unpack(p2, WIDTH * j, WIDTH))[:96])
    out_copies.append(w.local(s.gexs, r.gex))
    rows4.relay()
    rows5.relay()
    f11.wait_recv()
    fg.wait_recv()
    fgc = w.to_core((s.dog.at[c], s.dog.at[c]))
    t = join4([s.tg[j].astype(F32) for j in range(4)])
    n1 = s.xs[...] * rs1
    gain1 = jnp.sum(t * n1, 0, keepdims=True) / g1
    s.dgr[c] = grad_one + rs1 * (t - n1 * jnp.mean(t * n1, -1, keepdims=True))
    fd = w.to_core((s.dgr.at[c], s.dgr.at[c]))
    s.sgain[c, pb] = jnp.concatenate([gain1, gain2, gain3, jnp.zeros((5, WIDTH), F32)], 0)
    gain_rows = PlaneSmall(w, s.sgain)
    kred.spread()
    rows6.relay()
    vred.rows.core()
    rows4.core()
    rows5.core()
    t = unpack(p2, 3328, WIDTH).astype(F32)
    lhs = lowered(lax.select(c == 1, t[:, 384:], t[:, :384]).T)
    s.gres[...] = lowered(nn(lhs, unpack(s.p1, 0, WIDTH)))
    out_copies.append(w.local(s.gres, r.gre))
    half_product(s.p4, 768, 4, rows4)
    half_product(s.p5, 768, 3, rows5)
    tab_rows.core()
    gain_rows.core()
    fgc.wait_recv()
    fd.wait_recv()
    for k in (0, 1):
        t = join4([s.dog[k, j].astype(F32) for j in range(4)])
        for m in (0, 1):
            r.decoder_out[:, 2 * k + m, :] = t[PAD * m : PAD * m + ANS]
            r.decoder_grad[:, 2 * k + m, :] = s.dgr[k, PAD * m : PAD * m + ANS, :]
    kred.rows.core()
    rows6.core()
    vred.rows.finish()
    s.wg[6] = vred.result()
    out_copies.append(w.local(s.wg.at[6], r.squares.at[6]))
    gain_rows.finish()
    tab_rows.finish()
    t = s.sgain[0, 0]
    u = s.stab[0, 0]
    for k in range(1, 8):
        t = t + s.sgain[k // 4, k % 4]
        u = u + s.stab[k // 4, k % 4]
    r.gains[...] = t
    r.table_grad[...] = u
    kred.rows.finish()
    s.wg[5] = kred.result()
    out_copies.append(w.local(s.wg.at[5], r.squares.at[5]))
    rows6.finish()
    ref = s.p6
    lhs = inputs_half(unpack(ref, 2304, 256), c)
    for k in range(3):
        s.wg[k] = lowered(nn(lhs, unpack(ref, WIDTH * k, WIDTH))[:96])
        out_copies.append(w.local(s.wg.at[k], r.squares.at[k]))
    for copy in out_copies:
        copy.wait()
    for batch in w.batches:
        batch.wait_send()


def write(dout, dgrad, eg, sq, gex, gre, gains, table, *refs):
    outs, (veg, vsq, vex, vre, weg, wsq, wex, wre, sems) = refs[:17], refs[17:]
    o_out, o_grad, o_eg, outs = outs[0], outs[1], outs[2], outs[3:]
    jobs = [(eg.at[q], veg.at[q], weg.at[q], o_eg.at[q]) for q in range(4)]
    jobs += [(gex, vex, wex, outs[8]), (gre, vre, wre, outs[9])]
    jobs += [(sq.at[k], vsq.at[k], wsq.at[k], outs[k]) for k in range(8)]
    loads = [pltpu.make_async_copy(j[0], j[1], sems.at[k]) for k, j in enumerate(jobs)]
    for copy in loads:
        copy.start()
    o_out[...] = dout[...]
    o_grad[...] = dgrad[...]
    for k in range(3):
        outs[10 + k][...] = gains[k : k + 1, :].reshape(WIDTH)
    outs[13][...] = table[...].T[:HEADS]
    stores = []
    for k, (src, near, wide, dst) in enumerate(jobs):
        loads[k].wait()
        wide[...] = near[...].astype(F32)
        stores.append(pltpu.make_async_copy(wide, dst, sems.at[len(jobs) + k]))
        stores[-1].start()
    for copy in stores:
        copy.wait()


def fused(x, enc, og, plen, pcount, buckets, wq, wk, wv, wo, wcq, wck, wcv, wco, wex, wre, g1, g2, g3, table):
    def shape(*dims, kind=F32):
        return jax.ShapeDtypeStruct(dims, kind)

    rows = shape(ANS, 4, WIDTH)
    mid = pl.pallas_call(
        layer,
        out_shape=[
            rows,
            rows,
            shape(4, SLOT, WIDTH, kind=BF),
            shape(8, 96, WIDTH, kind=BF),
            shape(96, FF, kind=BF),
            shape(384, WIDTH, kind=BF),
            shape(8, WIDTH),
            shape(BUCKETS, 128),
        ],
        in_specs=[pl.BlockSpec(memory_space=k) for k in IN_KIND.values()],
        out_specs=[pl.BlockSpec(memory_space=k) for k in OUT_KIND.values()],
        scratch_shapes=[pltpu.VMEM(*v) for v in SCRATCH.values()]
        + [pltpu.SemaphoreType.DMA((SEMAPHORES,))],
        compiler_params=pltpu.CompilerParams(
            collective_id=0, has_side_effects=True, vmem_limit_bytes=62 * 2**20
        ),
    )(
        jnp.transpose(x, (1, 0, 2)),
        jnp.transpose(og, (1, 0, 2)),
        *(plen, pcount, buckets, table.T, g1, g2, g3, enc),
        *(wq, wk, wv, wo, wcq, wck, wcv, wco, wex, wre),
    )
    near, far = pl.BlockSpec(memory_space=NEAR), pl.BlockSpec(memory_space=FAR)
    square = shape(96, WIDTH)
    out = pl.pallas_call(
        write,
        out_shape=[
            *(rows, rows, shape(4, SLOT, WIDTH)),
            *[square] * 8,
            *(shape(96, FF), shape(384, WIDTH)),
            *[shape(WIDTH)] * 3,
            shape(HEADS, BUCKETS),
        ],
        in_specs=[near, near, far, far, far, far, near, near],
        out_specs=[near, near, far, *[far] * 10, *[near] * 4],
        scratch_shapes=[
            pltpu.VMEM(dims, kind)
            for kind in (BF, F32)
            for dims in ((4, SLOT, WIDTH), (8, 96, WIDTH), (96, FF), (384, WIDTH))
        ]
        + [pltpu.SemaphoreType.DMA((28,))],
        compiler_params=pltpu.CompilerParams(vmem_limit_bytes=62 * 2**20),
    )(*mid)
    out = list(out)
    out[0], out[1] = (jnp.transpose(v, (1, 0, 2)) for v in out[:2])
    out[16] = out[16].T
    return tuple(out)


def solution(mesh):
    if dict(mesh.shape) != {"pb": 4, "pa": 8}:
        return generic(mesh)
    wide, tall = P("pb", "pa", None), P("pa", None)
    rows, whole = P("pb", None, None), P()
    return jax.shard_map(
        fused,
        mesh=mesh,
        in_specs=(rows, wide, rows, P("pb"), P("pb"), whole, *[tall] * 10, *[whole] * 4),
        out_specs=(rows, rows, wide, *[tall] * 10, *[whole] * 4),
        check_vma=False,
    )
```

```python
import math
import types

import jax
import jax.numpy as jnp
from jax import lax
from jax.experimental import pallas as pl
from jax.experimental.pallas import tpu as pltpu
from jax.sharding import PartitionSpec as P

epsilon = 1e-06
highest = lax.Precision.HIGHEST
masked_score = -1e30


def product(left, right):
    return jnp.dot(left, right, preferred_element_type=jnp.float32)


def lowered(value):
    return value.astype(jnp.bfloat16)


def norm_forward(value):
    factor = lax.rsqrt(jnp.mean(value * value, -1, keepdims=True) + epsilon)
    return (value * factor, factor)


def norm_backward(grad_out, normal, factor, gain):
    inner_term = grad_out * gain
    grad_in = factor * (inner_term - normal * jnp.mean(inner_term * normal, -1, keepdims=True))
    grad_gain = jnp.sum(grad_out * normal, (0, 1))
    return (grad_in, grad_gain)


def activate(value):
    return jax.nn.gelu(value, approximate=True)


def shard_grad(inputs, grad_rows, device_place, row_count):
    sliced = lax.dynamic_slice_in_dim(inputs, device_place * row_count, row_count, 2)
    return jnp.einsum("qak,qae->ke", sliced, grad_rows, preferred_element_type=jnp.float32)


def shards(
    decoder_in,
    encodings,
    out_grad,
    passage_len,
    passage_count,
    buckets,
    self_query,
    self_key,
    self_value,
    self_out,
    cross_query,
    cross_key,
    cross_value,
    cross_out,
    ffn_expand,
    ffn_reduce,
    norm_self,
    norm_cross,
    norm_ffn,
    bias_table,
):
    wide_count = lax.axis_size("pa")
    device_place = lax.axis_index("pa")
    stacked = jnp.stack(
        [self_query, self_key, self_value, self_out, cross_query, cross_key, cross_value, cross_out]
    )
    squares, expand_full, reduce_full = (
        lax.all_gather(stacked, "pa", axis=1, tiled=True),
        lax.all_gather(ffn_expand, "pa", axis=0, tiled=True),
        lax.all_gather(ffn_reduce, "pa", axis=0, tiled=True),
    )
    query_self = squares[0]
    key_self = squares[1]
    value_self = squares[2]
    out_self = squares[3]
    query_cross = squares[4]
    key_cross = squares[5]
    value_cross = squares[6]
    out_cross = squares[7]
    questions, answer, model_width = decoder_in.shape
    head_count = bias_table.shape[1]
    head_size = model_width // head_count
    factor = head_size ** (-0.5)
    slot_rows = encodings.shape[1]
    rows_model = model_width // wide_count
    rows_hidden = expand_full.shape[1] // wide_count

    def heads_of(value):
        return value.reshape(value.shape[0], value.shape[1], head_count, head_size)

    normal_one, factor_one = norm_forward(decoder_in)
    hidden_one = lowered(normal_one * norm_self)
    query_heads = heads_of(lowered(product(hidden_one, query_self)))
    key_heads = heads_of(lowered(product(hidden_one, key_self)))
    value_heads = heads_of(lowered(product(hidden_one, value_self)))
    onehot = (buckets[:, :, None] == jnp.arange(bias_table.shape[0])[None, None, :]).astype(
        jnp.float32
    )
    bias_scores = jnp.einsum("ijb,bh->hij", onehot, bias_table, precision=highest)
    causal = jnp.arange(answer)[:, None] >= jnp.arange(answer)[None, :]
    scores = (
        jnp.einsum("qihd,qjhd->qhij", query_heads, key_heads, preferred_element_type=jnp.float32)
        * factor
        + bias_scores[None]
    )
    scores = jnp.where(causal[None, None], scores, masked_score)
    probabilities = jax.nn.softmax(scores, -1)
    weights_self = lowered(probabilities)
    mixed_self = lowered(
        jnp.einsum("qhij,qjhd->qihd", weights_self, value_heads, preferred_element_type=jnp.float32)
    ).reshape(questions, answer, model_width)
    resid_one = decoder_in + product(mixed_self, out_self)
    normal_two, factor_two = norm_forward(resid_one)
    hidden_two = lowered(normal_two * norm_cross)
    cquery = heads_of(lowered(product(hidden_two, query_cross)))
    per_device = slot_rows // passage_len
    held_count = jnp.clip(passage_count - device_place * per_device, 0, per_device)
    valid_rows = jnp.arange(slot_rows)[None, :] < (held_count * passage_len)[:, None]

    def project(encoded):
        ckeys = lowered(product(encoded, key_cross)).reshape(
            questions, slot_rows, head_count, head_size
        )
        cvalues = lowered(product(encoded, value_cross)).reshape(
            questions, slot_rows, head_count, head_size
        )
        cscores = (
            jnp.einsum("qihd,qjhd->qhij", cquery, ckeys, preferred_element_type=jnp.float32)
            * factor
        )
        cscores = jnp.where(valid_rows[:, None, None, :], cscores, masked_score)
        return (ckeys, cvalues, cscores)

    ckeys, cvalues, cscores = project(encodings)
    row_max = lax.pmax(jnp.max(cscores, -1), "pa")
    exp_weights = jnp.exp(cscores - row_max[..., None])
    part_num = jnp.einsum(
        "qhij,qjhd->qihd", lowered(exp_weights), cvalues, preferred_element_type=jnp.float32
    )
    part_total = jnp.sum(exp_weights, -1)
    numerator, totals = lax.psum((part_num, part_total), "pa")
    totals_t = jnp.transpose(totals, (0, 2, 1))[..., None]
    mixed_cross = lowered(numerator / totals_t).reshape(questions, answer, model_width)
    resid_two = resid_one + product(mixed_cross, out_cross)
    normal_three, factor_three = norm_forward(resid_two)
    hidden_three = lowered(normal_three * norm_ffn)
    pre_act = product(hidden_three, expand_full)
    activation = lowered(activate(pre_act))
    decoder_out = resid_two + product(activation, reduce_full)
    grad_z = lowered(out_grad)
    grad_reduce = shard_grad(activation, grad_z, device_place, rows_hidden)
    grad_act = jnp.einsum("qae,fe->qaf", grad_z, reduce_full, preferred_element_type=jnp.float32)
    unused_out, gelu_back = jax.vjp(activate, pre_act)
    grad_pre = lowered(gelu_back(grad_act)[0])
    grad_expand = shard_grad(hidden_three, grad_pre, device_place, rows_model)
    grad_three = jnp.einsum(
        "qaf,kf->qak", grad_pre, expand_full, preferred_element_type=jnp.float32
    )
    back_term, grad_gain_ffn = norm_backward(grad_three, normal_three, factor_three, norm_ffn)
    grad_two = out_grad + back_term
    grad_c = lowered(grad_two)
    grad_out_cross = shard_grad(mixed_cross, grad_c, device_place, rows_model)
    grad_mix = heads_of(
        lowered(jnp.einsum("qae,ke->qak", grad_c, out_cross, preferred_element_type=jnp.float32))
    )
    grad_mix_wide = grad_mix.astype(jnp.float32)
    grad_num = lowered(grad_mix_wide / totals_t)
    grad_tot = -jnp.sum(grad_mix_wide * numerator, -1) / (totals_t[..., 0] * totals_t[..., 0])
    ckeys, cvalues, cscores = project(encodings)
    exp_weights = jnp.exp(cscores - row_max[..., None])
    grad_expo = jnp.einsum("qihd,qjhd->qhij", grad_num, cvalues, preferred_element_type=jnp.float32)
    grad_expo = grad_expo + jnp.transpose(grad_tot, (0, 2, 1))[..., None]
    grad_score = lowered(exp_weights * grad_expo)
    part_query = (
        jnp.einsum("qhij,qjhd->qihd", grad_score, ckeys, preferred_element_type=jnp.float32)
        * factor
    )
    grad_cquery = lowered(lax.psum(part_query, "pa")).reshape(questions, answer, model_width)
    grad_ckeys = lowered(
        jnp.einsum("qhij,qihd->qjhd", grad_score, cquery, preferred_element_type=jnp.float32)
        * factor
    ).reshape(questions, slot_rows, model_width)
    grad_cvalues = lowered(
        jnp.einsum(
            "qhij,qihd->qjhd", lowered(exp_weights), grad_num, preferred_element_type=jnp.float32
        )
    ).reshape(questions, slot_rows, model_width)
    encoding_grad = jnp.einsum(
        "qse,ke->qsk", grad_ckeys, key_cross, preferred_element_type=jnp.float32
    )
    encoding_grad = encoding_grad + jnp.einsum(
        "qse,ke->qsk", grad_cvalues, value_cross, preferred_element_type=jnp.float32
    )
    full_key = jnp.einsum("qsk,qse->ke", encodings, grad_ckeys, preferred_element_type=jnp.float32)
    full_value = jnp.einsum(
        "qsk,qse->ke", encodings, grad_cvalues, preferred_element_type=jnp.float32
    )
    grad_query_cross = shard_grad(hidden_two, grad_cquery, device_place, rows_model)
    grad_hidden_two = jnp.einsum(
        "qae,ke->qak", grad_cquery, query_cross, preferred_element_type=jnp.float32
    )
    back_term, grad_gain_cross = norm_backward(grad_hidden_two, normal_two, factor_two, norm_cross)
    grad_one = grad_two + back_term
    grad_a = lowered(grad_one)
    grad_out_self = shard_grad(mixed_self, grad_a, device_place, rows_model)
    grad_smix = heads_of(
        lowered(jnp.einsum("qae,ke->qak", grad_a, out_self, preferred_element_type=jnp.float32))
    )
    grad_w = jnp.einsum(
        "qihd,qjhd->qhij", grad_smix, value_heads, preferred_element_type=jnp.float32
    )
    grad_s = lowered(probabilities * (grad_w - jnp.sum(grad_w * probabilities, -1, keepdims=True)))
    grad_table = jnp.einsum(
        "ijb,hij->bh", onehot, jnp.sum(grad_s.astype(jnp.float32), 0), precision=highest
    )
    grad_sq = lowered(
        jnp.einsum("qhij,qjhd->qihd", grad_s, key_heads, preferred_element_type=jnp.float32)
        * factor
    ).reshape(questions, answer, model_width)
    grad_sk = lowered(
        jnp.einsum("qhij,qihd->qjhd", grad_s, query_heads, preferred_element_type=jnp.float32)
        * factor
    ).reshape(questions, answer, model_width)
    grad_sv = lowered(
        jnp.einsum("qhij,qihd->qjhd", weights_self, grad_smix, preferred_element_type=jnp.float32)
    ).reshape(questions, answer, model_width)
    grad_query_self = shard_grad(hidden_one, grad_sq, device_place, rows_model)
    grad_key_self = shard_grad(hidden_one, grad_sk, device_place, rows_model)
    grad_value_self = shard_grad(hidden_one, grad_sv, device_place, rows_model)
    grad_hidden_one = jnp.einsum(
        "qae,ke->qak", grad_sq, query_self, preferred_element_type=jnp.float32
    )
    grad_hidden_one = grad_hidden_one + jnp.einsum(
        "qae,ke->qak", grad_sk, key_self, preferred_element_type=jnp.float32
    )
    grad_hidden_one = grad_hidden_one + jnp.einsum(
        "qae,ke->qak", grad_sv, value_self, preferred_element_type=jnp.float32
    )
    back_term, grad_gain_self = norm_backward(grad_hidden_one, normal_one, factor_one, norm_self)
    decoder_grad = grad_one + back_term
    key_part, value_part = (
        lax.psum_scatter(full_key, "pa", scatter_dimension=0, tiled=True),
        lax.psum_scatter(full_value, "pa", scatter_dimension=0, tiled=True),
    )
    summed = lax.psum(
        (
            grad_query_self,
            grad_key_self,
            grad_value_self,
            grad_out_self,
            grad_query_cross,
            key_part,
            value_part,
            grad_out_cross,
            grad_expand,
            grad_reduce,
            grad_gain_self,
            grad_gain_cross,
            grad_gain_ffn,
            grad_table,
        ),
        "pb",
    )
    key_total = summed[5]
    value_total = summed[6]
    rest_sums = (
        summed[0],
        summed[1],
        summed[2],
        summed[3],
        summed[4],
        summed[7],
        summed[8],
        summed[9],
        summed[10],
        summed[11],
        summed[12],
        summed[13],
    )
    return (
        decoder_out,
        decoder_grad,
        encoding_grad,
        rest_sums[0],
        rest_sums[1],
        rest_sums[2],
        rest_sums[3],
        rest_sums[4],
        key_total,
        value_total,
        rest_sums[5],
        rest_sums[6],
        rest_sums[7],
        rest_sums[8],
        rest_sums[9],
        rest_sums[10],
        rest_sums[11],
    )


def generic(mesh):
    placed = (
        P("pb", None, None),
        P("pb", "pa", None),
        P("pb", None, None),
        P("pb"),
        P("pb"),
        P(),
        P("pa", None),
        P("pa", None),
        P("pa", None),
        P("pa", None),
        P("pa", None),
        P("pa", None),
        P("pa", None),
        P("pa", None),
        P("pa", None),
        P("pa", None),
        P(),
        P(),
        P(),
        P(),
    )
    return jax.shard_map(
        shards,
        mesh=mesh,
        in_specs=placed,
        out_specs=(
            P("pb", None, None),
            P("pb", None, None),
            P("pb", "pa", None),
            P("pa", None),
            P("pa", None),
            P("pa", None),
            P("pa", None),
            P("pa", None),
            P("pa", None),
            P("pa", None),
            P("pa", None),
            P("pa", None),
            P("pa", None),
            P(),
            P(),
            P(),
            P(),
        ),
        check_vma=False,
    )


MESH = pl.DeviceIdType.MESH
F32, BF = jnp.float32, jnp.bfloat16
ANS, PAD, OWN, ALL = 20, 24, 48, 96
WIDTH, HEADS, SIZE, PART = 768, 12, 64, 192
ROWS = HEADS * PAD
SLOT, FF, BUCKETS = 512, 3072, 32
CQ, CK, CV, CO, SO, SQ, SK, SV, EX, RD, EN = range(11)
GELU_A, GELU_B = 0.7978845608028654, 0.044715


def nn(a, b):
    return lax.dot_general(a, b, (((1,), (0,)), ((), ())), preferred_element_type=F32)


def nt(a, b):
    return lax.dot_general(a, b, (((1,), (1,)), ((), ())), preferred_element_type=F32)


def tn(a, b):
    return lax.dot_general(a, b, (((0,), (0,)), ((), ())), preferred_element_type=F32)


def lanes(rows, width):
    return lax.broadcasted_iota(jnp.int32, (rows, width), 1)


def split4(v):
    out = []
    for j in range(4):
        base = PART * j // 128 * 128
        t = v[:, base : base + 256]
        out.append(pltpu.roll(t, PART, 1) if PART * j != base else t)
    return out


def join4(parts):
    low = lanes(parts[0].shape[0], 128) < 64
    tiles = []
    for a, b in ((parts[0], parts[1]), (parts[2], parts[3])):
        b = pltpu.roll(b, 64, 1)
        tiles += [a[:, :128], jnp.where(low, a[:, 128:], b[:, :128]), b[:, 128:]]
    return jnp.concatenate(tiles, 1)


def join3(parts):
    low = lanes(parts[0].shape[0], 128) < 64
    a, b = parts[0], pltpu.roll(parts[1], 64, 1)
    return jnp.concatenate([a[:, :128], jnp.where(low, a[:, 128:], b[:, :128]), b[:, 128:], parts[2]], 1)


def part3(v):
    return [v[:, :256], pltpu.roll(v[:, 128:384], PART, 1), v[:, 384:]]


def choose(parts, index):
    v = parts[0]
    for j in range(1, len(parts)):
        v = lax.select(index == j, parts[j], v)
    return v


def stack_heads(v, count):
    head = lanes(*v.shape) // SIZE
    return jnp.concatenate([jnp.where(head == h, v, 0.0) for h in range(count)], 0)


def pick_heads(v, count):
    head = lanes(PAD, v.shape[1]) // SIZE
    out = jnp.zeros((PAD, v.shape[1]), F32)
    for h in range(count):
        out = out + jnp.where(head == h, v[PAD * h : PAD * (h + 1)], 0.0)
    return out


def pair_stack(v, p):
    t = v[:, 128 * p : 128 * (p + 1)]
    low = lanes(PAD, 128) < SIZE
    return jnp.concatenate([jnp.where(low, t, 0.0), jnp.where(low, 0.0, t)], 0)


SCRATCH = dict(
    sq=((9, WIDTH, WIDTH), BF),
    rd=((WIDTH, WIDTH), BF),
    enc=((4, SLOT, WIDTH), BF),
    xs=((OWN, WIDTH), F32),
    ogs=((OWN, WIDTH), F32),
    bks=((PAD, PAD), jnp.int32),
    bias=((3 * PAD, PAD), F32),
    s1=((4, OWN, 640), BF),
    r1=((3, OWN, 640), BF),
    gact=((OWN, WIDTH), F32),
    s9=((4, OWN, 256), BF),
    r9=((3, OWN, 256), BF),
    t3=((4, OWN, 256), BF),
    s2=((4, OWN, 256), BF),
    r2=((3, OWN, 256), BF),
    ag2=((2, 4, OWN, 256), BF),
    gz=((OWN, WIDTH), BF),
    acts=((OWN, WIDTH), BF),
    span=((128, 384), F32),
    x6=((6, 192, 128), BF),
    y6=((6, 192, 128), BF),
    qk=((4, ROWS, WIDTH), BF),
    gv=((4, ROWS, WIDTH), BF),
    bs=((4, ROWS, WIDTH), BF),
    as_=((4, ROWS, WIDTH), BF),
    es=((4, ROWS, SLOT), BF),
    gs=((4, ROWS, SLOT), BF),
    stat=((384, 128), F32),
    stg=((8, 8, 384), F32),
    wrow=((128, 384), F32),
    wcol=((384, 128), F32),
    s5=((2, 4, OWN, 256), BF),
    r5=((8, OWN, 256), BF),
    mixg=((2, 4, OWN, 256), BF),
    gm=((2, OWN, WIDTH), BF),
    s7=((2, 4, OWN, 256), BF),
    c7=((4, OWN, 256), BF),
    z7=((4, OWN, 256), BF),
    r7=((3, OWN, 256), BF),
    gcq=((4, OWN, 256), BF),
    s8=((4, OWN, 256), BF),
    r8=((3, OWN, 256), BF),
    dog=((2, 4, OWN, 256), BF),
    dgr=((2, OWN, WIDTH), F32),
    tot=((ROWS, 128), F32),
    gsg=((4, OWN, 640), BF),
    tg=((4, OWN, 256), BF),
    stz=((4, BUCKETS, 128), F32),
    wg=((8, 96, WIDTH), BF),
    gexs=((96, FF), BF),
    gres=((384, WIDTH), BF),
    p1=((2, 4, 16, 1920), BF),
    p2=((2, 4, 16, 10240), BF),
    p3=((2, 4, 16, 2560), BF),
    p4=((2, 4, 16, 2560), BF),
    p5=((2, 4, 16, 2560), BF),
    p6=((2, 4, 16, 6400), BF),
    sgain=((2, 4, 8, WIDTH), F32),
    stab=((2, 4, BUCKETS, 128), F32),
    kw1=((WIDTH, WIDTH), BF),
    kr1=((384, WIDTH), BF),
    kw2=((4, 96, WIDTH), BF),
    kr2=((3, 96, WIDTH), BF),
    kw3=((4, 96, 256), BF),
    kr3=((3, 96, 256), BF),
    kw4=((2, 4, 96, 256), BF),
    vw1=((WIDTH, WIDTH), BF),
    vr1=((384, WIDTH), BF),
    vw2=((4, 96, WIDTH), BF),
    vr2=((3, 96, WIDTH), BF),
    vw3=((4, 96, 256), BF),
    vr3=((3, 96, 256), BF),
    vw4=((2, 4, 96, 256), BF),
    eg=((4, SLOT, WIDTH), BF),
)
SEMAPHORES = 181
NEAR, SCALAR, FAR = pltpu.VMEM, pltpu.SMEM, pl.ANY
IN_KIND = dict(
    x=NEAR, og=NEAR, plen=SCALAR, pcount=SCALAR, buckets=NEAR, table=SCALAR,
    g1=NEAR, g2=NEAR, g3=NEAR, enc_h=FAR,
    wq=FAR, wk=FAR, wv=FAR, wo=FAR, wcq=FAR, wck=FAR, wcv=FAR, wco=FAR, wex=FAR, wre=FAR,
)
OUT_KIND = dict(
    decoder_out=NEAR, decoder_grad=NEAR, encoding_grad=FAR, squares=FAR, gex=FAR, gre=FAR, gains=NEAR, table_grad=NEAR,
)


class Batch:
    def __init__(self, wire, span):
        self.span, self.sent, self.landed = span, wire.next(), wire.next()
        wire.batches.append(self)

    def wait_recv(self):
        pltpu.make_async_copy(self.span, self.span, self.landed).wait()

    def wait_send(self):
        pltpu.make_async_copy(self.span, self.span, self.sent).wait()


class Wire:
    def __init__(self, sems, narrow, wide):
        self.sems, self.count, self.batches = sems, 0, []
        self.narrow, self.wide = narrow, wide
        self.pb, self.pa = lax.axis_index("pb"), lax.axis_index("pa")
        self.z, self.c = self.pa // 2, lax.rem(self.pa, 2)

    def next(self):
        self.count += 1
        return self.sems.at[self.count - 1]

    def local(self, src, dst):
        copy = pltpu.make_async_copy(src, dst, self.next())
        copy.start()
        return copy

    def span(self, size, dtype):
        if dtype == F32:
            return self.wide.at[pl.ds(0, size // 384), :]
        lane = next(n for n in (384, 768, 640, 512, 256, 128) if size % (16 * n) == 0 and size <= n * WIDTH)
        return self.narrow.at[0, pl.ds(0, size // lane), pl.ds(0, lane)]

    def batch(self, copies):
        first = copies[0][0]
        span = first
        if len(copies) > 1:
            span = self.span(sum(math.prod(src.shape) for src, _, _, _ in copies), first.dtype)
        out = Batch(self, span)
        for src, dst, pb, pa in copies:
            pltpu.make_async_remote_copy(
                src_ref=src,
                dst_ref=dst,
                send_sem=out.sent,
                recv_sem=out.landed,
                device_id=(pb, pa),
                device_id_type=MESH,
            ).start()
        return out

    def zpeer(self, j):
        return lax.rem(self.z + j, 4)

    def ppeer(self, j):
        return lax.rem(self.pb + j, 4)

    def xside(self):
        return self.pb + 1 - 2 * lax.rem(self.pb, 2)

    def yside(self):
        return lax.rem(self.pb + 2, 4)

    def to_core(self, *pairs):
        return self.batch([(src, dst, self.pb, self.pa + 1 - 2 * self.c) for src, dst in pairs])

    def to_z(self, src_of, dst_of):
        peers = [(self.zpeer(j), j) for j in (1, 2, 3)]
        return self.batch([(src_of(t), dst_of(j), self.pb, 2 * t + self.c) for t, j in peers])

    def to_column(self, src_of, dst_of):
        peers = [(lax.rem(self.pa + j, 8), j) for j in range(1, 8)]
        return self.batch([(src_of(t), dst_of(j), self.pb, t) for t, j in peers])

    def to_plane(self, src_of, dst_of):
        peers = [(self.ppeer(j), j) for j in (1, 2, 3)]
        return self.batch([(src_of(t), dst_of(j), t, self.pa) for t, j in peers])

    def to_sides(self, refs):
        sides = (self.xside(), self.yside())
        return self.batch([(ref, ref, side, self.pa) for ref in refs for side in sides])


class Gather:
    def __init__(self, wire, sq, index, source, wide=False):
        self.w, self.sq, self.index, self.source, self.wide = wire, sq, index, source, wide
        row = pl.multiple_of(48 * lax.rem(wire.pb, 2), 16)

        def block(t):
            lane = 384 * (wire.pb // 2) + (WIDTH * t if wide else 0)
            return source.at[pl.ds(row, 48), pl.ds(pl.multiple_of(lane, 128), 384)]

        self.a = wire.to_z(block, lambda j: self.part(wire.z, wire.pb, 0, 384))

    def part(self, z, pb, begin, size):
        row = pl.multiple_of(96 * (2 * z + self.w.c) + 48 * lax.rem(pb, 2), 16)
        lane = pl.multiple_of(384 * (pb // 2) + begin, 128)
        return self.sq.at[self.index, pl.ds(row, 48), pl.ds(lane, size)]

    def plane(self):
        w = self.w
        self.a.wait_recv()
        self.a = w.to_sides([self.part(w.zpeer(i), w.pb, 0, 384) for i in (1, 2, 3)])

    def relay(self):
        w = self.w
        self.a.wait_recv()
        copies = []
        cut = 128 if self.index % 2 else 256
        for i in (1, 2, 3):
            ref = self.part(w.zpeer(i), w.xside(), 0, cut)
            copies.append((ref, ref, w.yside(), w.pa))
            ref = self.part(w.zpeer(i), w.yside(), cut, 384 - cut)
            copies.append((ref, ref, w.xside(), w.pa))
        self.a = w.batch(copies)

    def core(self):
        w = self.w
        self.a.wait_recv()
        refs = []
        for i in (1, 2, 3):
            row = pl.multiple_of(96 * (2 * w.zpeer(i) + w.c), 16)
            refs.append(self.sq.at[self.index, pl.ds(row, 96), :])
        self.a = w.to_core(*[(ref, ref) for ref in refs])

    def finish(self):
        self.a.wait_recv()


class PlaneRows:
    def __init__(self, wire, ref):
        self.w, self.ref = wire, ref
        self.a = wire.to_sides([ref.at[wire.c, wire.pb]])

    def relay(self):
        w = self.w
        self.a.wait_recv()
        size = self.ref.shape[3]
        half = size // 256 * 128
        a = self.ref.at[w.c, w.xside(), :, pl.ds(0, half)]
        b = self.ref.at[w.c, w.yside(), :, pl.ds(half, size - half)]
        self.a = w.batch([(a, a, w.yside(), w.pa), (b, b, w.xside(), w.pa)])

    def core(self):
        self.a.wait_recv()
        src = self.ref.at[self.w.c]
        self.a = self.w.to_core((src, src))

    def finish(self):
        self.a.wait_recv()


class PlaneSmall(PlaneRows):
    def __init__(self, wire, ref):
        self.w, self.ref = wire, ref
        src = ref.at[wire.c, wire.pb]
        self.a = wire.to_plane(lambda t: src, lambda j: src)


def pack(v):
    half = v.shape[1] // 2
    last = jnp.where(
        lax.broadcasted_iota(jnp.int32, (8, v.shape[1]), 0) < 4, v[16:24], pltpu.roll(v[40:48], 4, 0)
    )
    last = jnp.concatenate([last[:, :half], last[:, half:]], 0)
    return lowered(jnp.concatenate([v[:16], v[24:40], last], 1))


def unpack(ref, begin, width):
    begin = begin * 5 // 2
    a = ref[:, :, :, begin : begin + width].reshape(128, width)
    b = ref[:, :, :, begin + width : begin + 2 * width].reshape(128, width)
    t = ref[:, :, :, begin + 2 * width : begin + width * 5 // 2].astype(F32)
    t = [t[:, :, 8 * k : 8 * k + 8, :].reshape(64, width // 2) for k in (0, 1)]
    return jnp.concatenate([a, b, lowered(jnp.concatenate(t, 1))], 0)


class CrossReduce:
    def __init__(self, wire, refs):
        self.w, self.refs = wire, refs

    def core(self):
        w, (w1, r1, w2, r2, w3, r3, w4) = self.w, self.refs
        row = pl.multiple_of(384 * (1 - w.c), 16)
        self.a = w.to_core((w1.at[pl.ds(row, 384), :], r1))

    def plane(self):
        w, (w1, r1, w2, r2, w3, r3, w4) = self.w, self.refs
        self.a.wait_recv()
        for k in range(4):
            row = pl.multiple_of(384 * w.c + 96 * k, 16)
            t = w1[pl.ds(row, 96), :].astype(F32) + r1[96 * k : 96 * (k + 1), :].astype(F32)
            w2[k] = lowered(t)
        self.b = w.to_plane(lambda t: w2.at[t], lambda j: r2.at[j - 1])

    def line(self):
        w, (w1, r1, w2, r2, w3, r3, w4) = self.w, self.refs
        self.b.wait_recv()
        t = w2[w.pb].astype(F32)
        for j in range(3):
            t = t + r2[j].astype(F32)
        for j, part in enumerate(split4(t)):
            w3[j] = lowered(part)
        self.d = w.to_z(lambda t: w3.at[t], lambda j: r3.at[j - 1])

    def spread(self):
        w, (w1, r1, w2, r2, w3, r3, w4) = self.w, self.refs
        self.d.wait_recv()
        t = w3[w.z].astype(F32)
        for j in range(3):
            t = t + r3[j].astype(F32)
        w4[w.c, w.pb] = lowered(t)
        self.rows = PlaneSmall(w, w4)

    def result(self):
        w4 = self.refs[-1]
        t = w4[...].astype(F32).reshape(WIDTH, 256)
        t = lax.select(self.w.c == 1, pltpu.roll(t, 160, 1), t)[:, :128]
        return lowered(t.T[:96])


def inputs_half(t, c):
    t = t.astype(F32)
    t = lax.select(c == 1, pltpu.roll(t, 160, 1), t)[:, :128]
    return lowered(t.T)


def layer(*refs):
    names = (*IN_KIND, *OUT_KIND)
    r = types.SimpleNamespace(**dict(zip(names, refs)))
    s = types.SimpleNamespace(**dict(zip(SCRATCH, refs[len(names) :])))
    w = Wire(refs[-1], s.sq, s.span)
    pb, pa, z, c = w.pb, w.pa, w.z, w.c
    sq, rd, enc = s.sq, s.rd, s.enc

    barrier = pltpu.get_barrier_semaphore()
    for j in range(1, 8):
        pl.semaphore_signal(
            barrier, inc=1, device_id=(pb, lax.rem(pa + j, 8)), device_id_type=MESH
        )
    for j in (1, 2, 3):
        pl.semaphore_signal(barrier, inc=1, device_id=(w.ppeer(j), pa), device_id_type=MESH)

    squares = [r.wcq, r.wck, r.wcv, r.wco, r.wo, r.wq, r.wk, r.wv]
    own_rows = pl.ds(pl.multiple_of(96 * pa, 16), 96)
    red_rows = pl.ds(pl.multiple_of(384 * c, 16), 384)
    order = (SQ, SK, SV, CQ, CK, SO, CV, CO)
    held = {i: w.local(squares[i], sq.at[i, own_rows, :]) for i in order}
    chip_cols = pl.ds(pl.multiple_of(WIDTH * z, 128), WIDTH)
    held[EX] = w.local(r.wex.at[:, chip_cols], sq.at[EX, own_rows, :])
    held[RD] = w.local(r.wre, rd.at[red_rows, :])
    held[EN] = w.local(r.enc_h, enc)

    for dst, src in ((s.xs, r.x), (s.ogs, r.og)):
        dst[...] = jnp.zeros((OWN, WIDTH), F32)
        for k in (0, 1):
            dst[PAD * k : PAD * k + ANS, :] = lax.select(c == 1, src[:, 2 + k, :], src[:, k, :])
    s.bks[...] = jnp.zeros((PAD, PAD), jnp.int32)
    s.bks[:ANS, :ANS] = r.buckets[...]
    g1, g2, g3 = [ref[...].reshape(1, WIDTH) for ref in (r.g1, r.g2, r.g3)]
    x = s.xs[...]
    rs1 = lax.rsqrt(jnp.mean(x * x, -1, keepdims=True) + epsilon)
    h1z = choose(split4(x * rs1 * g1), z)
    xz = choose(split4(x), z)
    h1b = lowered(h1z)
    s.p6[c, pb, :, 5760:6400] = pack(h1z)
    s.p1[c, pb] = pack(s.ogs[...])
    s.gz[...] = lowered(s.ogs[...])

    pl.semaphore_wait(barrier, 10)
    other = [w.to_core(*[(squares[i], sq.at[i, own_rows, :]) for i in (SQ, SK, SV)])]
    gather_q = Gather(w, sq, CQ, r.wcq)
    other += [
        w.to_core((r.wre, rd.at[red_rows, :])),
        w.to_core(*[(squares[i], sq.at[i, own_rows, :]) for i in (SO, CQ, CK)]),
        w.to_core(
            *[(squares[i], sq.at[i, own_rows, :]) for i in (CV, CO)],
            (r.wex.at[:, chip_cols], sq.at[EX, own_rows, :]),
        ),
    ]

    def chip(i):
        return sq[i, pl.ds(pl.multiple_of(PART * z, 16), PART), :]

    parts = []
    for i in (SQ, SK, SV):
        held[i].wait()
        if i == SQ:
            other[0].wait_recv()
        parts.append(split4(nn(h1b[:, :PART], chip(i))))
    blocks = [join3([parts[k][j] for k in range(3)]) for j in range(4)]
    for j in range(4):
        s.s1[j] = lowered(blocks[j])
    own_qkv = choose(blocks, z)
    f1 = w.to_z(lambda t: s.s1.at[t], lambda j: s.r1.at[j - 1])
    gather_k = Gather(w, sq, CK, r.wck)

    bucket = s.bks[...]

    def bias_head(h, carry):
        v = jnp.zeros((PAD, PAD), F32)
        for b in range(BUCKETS):
            v = jnp.where(bucket == b, r.table[3 * z + h, b], v)
        s.bias[pl.ds(pl.multiple_of(PAD * h, 8), PAD), :] = v
        return carry

    lax.fori_loop(0, 3, bias_head, 0)
    held[RD].wait()
    other[1].wait_recv()
    s.gact[...] = nt(s.gz[...], rd[...])

    gather_q.plane()
    f1.wait_recv()
    gather_q.relay()
    v = own_qkv
    for j in range(3):
        v = v + s.r1[j].astype(F32)
    q3, k3, v3 = [lowered(t).astype(F32)[:, :PART] for t in part3(v)]

    def attend(stacked, keys, bias):
        i = lax.broadcasted_iota(jnp.int32, (PAD, PAD), 0)
        j = lax.broadcasted_iota(jnp.int32, (PAD, PAD), 1)
        seen = jnp.concatenate([(j <= i).astype(F32)] * 3, 0) > 0.5
        t = jnp.where(seen, nt(lowered(stacked), lowered(keys)) + bias, masked_score)
        t = jnp.exp(t - jnp.max(t, -1, keepdims=True))
        return t / jnp.sum(t, -1, keepdims=True)

    mixes, probs, stacks = [], [], []
    for k in (0, 1):
        rows = slice(PAD * k, PAD * (k + 1))
        stacks.append(stack_heads(q3[rows] * 0.125, 3))
        probs.append(attend(stacks[k], k3[rows], s.bias[...]))
        mixes.append(pick_heads(nn(lowered(probs[k]), lowered(v3[rows])), 3))
    mixb = lowered(jnp.concatenate(mixes, 0))
    gap = jnp.zeros((OWN, 64), F32)
    s.p5[c, pb, :, 1920:2560] = pack(jnp.concatenate([jnp.concatenate(mixes, 0), gap], 1))
    held[SO].wait()
    other[2].wait_recv()
    parts = split4(nn(mixb, chip(SO)))
    for j in range(4):
        s.s2[j] = lowered(parts[j])
    own_o = choose(parts, z)
    f2 = w.to_z(lambda t: s.s2.at[t], lambda j: s.r2.at[j - 1])
    gather_q.core()
    gather_k.plane()
    gather_v = Gather(w, sq, CV, r.wcv)

    f2.wait_recv()
    r1z = xz + own_o
    for j in range(3):
        r1z = r1z + s.r2[j].astype(F32)
    counts = lanes(OWN, 256) < PART
    g2z = choose(split4(jnp.broadcast_to(g2, (OWN, WIDTH))), z)
    square = jnp.sum(jnp.where(counts, r1z * r1z, 0.0), -1, keepdims=True)
    high = lowered(square).astype(F32)
    tail = jnp.where(lanes(OWN, 256) < 224, high, square - high)
    s.ag2[c, z] = lowered(jnp.where(counts, r1z * g2z, tail))
    f3 = w.to_z(lambda t: s.ag2.at[c, z], lambda j: s.ag2.at[c, z])
    gather_k.relay()
    gather_v.plane()

    f3.wait_recv()
    f3c = w.to_core((s.ag2.at[c], s.ag2.at[c]))
    gather_k.core()
    gather_o = Gather(w, sq, CO, r.wco)
    gather_x = Gather(w, sq, EX, r.wex, True)
    f3c.wait_recv()
    blocks = [[s.ag2[k, j].astype(F32) for j in range(4)] for k in (0, 1)]
    rs2 = []
    for k in (0, 1):
        t = blocks[k][0] + blocks[k][1] + blocks[k][2] + blocks[k][3]
        lane = lanes(OWN, 256)
        t = jnp.sum(jnp.where((lane == 192) | (lane == 224), t, 0.0), -1, keepdims=True)
        rs2.append(lax.rsqrt(t * (1.0 / WIDTH) + epsilon))
    gather_q.finish()
    held[CQ].wait()
    cq = jnp.zeros((ALL, WIDTH), F32)
    for j in range(4):
        t = jnp.concatenate([s.ag2[0, j], s.ag2[1, j]], 0)[:, :PART]
        cq = cq + nn(t, sq[CQ, PART * j : PART * (j + 1), :])
    cq = cq * jnp.concatenate(rs2, 0)
    cq = lowered(cq).astype(F32) * 0.125
    gather_k.finish()
    gather_v.relay()
    held[CK].wait()
    for p in range(6):
        t = jnp.concatenate([pair_stack(cq[PAD * q : PAD * (q + 1)], p) for q in range(4)], 0)
        s.x6[p] = lowered(t)
        t = lowered(nt(s.x6[p], sq[CK, :, 128 * p : 128 * (p + 1)]))
        for q in range(4):
            s.qk[q, 48 * p : 48 * (p + 1), :] = t[48 * q : 48 * (q + 1)]
    held[EN].wait()
    s.stat[...] = jnp.zeros((384, 128), F32)

    def scores(q, carry):
        size = r.plen[q]
        per = lax.select(size <= SLOT // 2, 2, 1)
        kept = jnp.minimum(jnp.maximum(r.pcount[q] - pa * per, 0), per) * size
        valid = lanes(ROWS, SLOT) < kept
        t = jnp.where(valid, nt(s.qk[q], enc[q]), masked_score)
        top = jnp.max(t, -1, keepdims=True)
        t = jnp.where(valid, jnp.exp(t - top), 0.0)
        total = jnp.sum(t, -1, keepdims=True)
        s.es[q] = lowered(t)
        s.bs[q] = lowered(nn(s.es[q], enc[q]))
        lane = lanes(ROWS, 128)
        old = s.stat[:ROWS, :]
        s.stat[:ROWS, :] = jnp.where(lane == q, top, jnp.where(lane == 4 + q, total, old))
        return carry

    lax.fori_loop(0, 1, scores, 0)
    gather_v.core()
    lax.fori_loop(1, 4, scores, 0)
    gather_o.plane()
    gather_x.plane()
    s.stg[pa] = s.stat[...].T[:8]
    f4 = w.to_column(lambda t: s.stg.at[pa], lambda j: s.stg.at[pa])
    gather_v.finish()
    held[CV].wait()
    other[3].wait_recv()
    low = lanes(PAD, 128) < SIZE
    tiles = [[] for q in range(4)]
    for p in range(6):
        t = jnp.concatenate([s.bs[q, 48 * p : 48 * (p + 1), :] for q in range(4)], 0)
        t = nn(t, sq[CV, :, 128 * p : 128 * (p + 1)])
        for q in range(4):
            a = t[48 * q : 48 * (q + 1)]
            tiles[q].append(jnp.where(low, a[:PAD], a[PAD:]))
    num = jnp.concatenate([jnp.concatenate(tiles[q], 1) for q in range(4)], 0)
    for k in (0, 1):
        for j, part in enumerate(split4(num[OWN * k : OWN * (k + 1)])):
            s.s5[k, j] = lowered(part)
    f5 = w.to_column(lambda t: s.s5.at[lax.rem(t, 2), t // 2], lambda j: s.r5.at[pa])
    s.r5[pa] = s.s5[c, z]
    rows1 = PlaneRows(w, s.p1)
    r1full = join4([s.ag2[c, j].astype(F32) for j in range(4)]) / g2
    rs2o = lax.select(c == 1, rs2[1], rs2[0])
    n2 = r1full * rs2o
    s.p4[c, pb, :, 1920:2560] = pack(choose(split4(n2 * g2), z))
    gather_o.relay()
    gather_x.relay()

    f4.wait_recv()
    f5.wait_recv()
    stats = [s.stg[k] for k in range(8)]
    top = stats[0]
    for k in range(1, 8):
        top = jnp.maximum(top, stats[k])
    scale = [jnp.exp(t - top) for t in stats]
    total = jnp.zeros((8, 384), F32)
    for k in range(8):
        total = total + scale[k] * pltpu.roll(stats[k], 4, 0)
    inverse = 1.0 / total
    s.wrow[...] = jnp.zeros((128, 384), F32)
    mine = jnp.zeros((8, 384), F32)
    for k in range(8):
        t = scale[k] * inverse
        mine = lax.select(pa == k, t, mine)
        s.wrow[2 * k : 2 * k + 2, :] = lax.select(c == 1, t[2:4], t[0:2])
    s.wrow[16:20, :] = mine[0:4]
    s.wcol[...] = s.wrow[...].T
    w3 = s.wcol[pl.ds(pl.multiple_of(3 * PAD * z, 8), 3 * PAD), :]
    lane = lanes(PAD, 256)
    sums = [jnp.zeros((PAD, 256), F32) for k in (0, 1)]
    for m in range(8):
        block = s.r5[m].astype(F32)
        for k in (0, 1):
            col = [w3[PAD * h : PAD * (h + 1), 2 * m + k : 2 * m + k + 1] for h in range(3)]
            t = jnp.where(lane < 64, col[0], jnp.where(lane < 128, col[1], col[2]))
            sums[k] = sums[k] + t * block[PAD * k : PAD * (k + 1)]
    mixc = jnp.concatenate(sums, 0)
    s.mixg[c, z] = lowered(mixc)
    s.p3[c, pb, :, 1920:2560] = pack(mixc)
    f6 = w.to_z(lambda t: s.mixg.at[c, z], lambda j: s.mixg.at[c, z])
    gather_o.core()
    gather_x.core()
    held[CO].wait()
    gather_o.finish()
    f6.wait_recv()
    mix_core = w.to_core((s.mixg.at[c], s.mixg.at[c]))
    after = jnp.zeros((OWN, WIDTH), F32)
    for j in range(4):
        after = after + nn(s.mixg[c, j][:, :PART], sq[CO, PART * j : PART * (j + 1), :])
    r2z = r1z + choose(split4(after), z)
    resid = r1full + after
    rs3 = lax.rsqrt(jnp.mean(resid * resid, -1, keepdims=True) + epsilon)
    n3 = resid * rs3
    h3 = lowered(n3 * g3)
    s.p2[c, pb, :, 7680:8320] = pack(choose(split4(n3 * g3), z))
    gather_x.finish()
    held[EX].wait()
    v = nn(h3, sq[EX])
    t = jnp.tanh(GELU_A * (v + GELU_B * v * v * v))
    act = 0.5 * v * (1.0 + t)
    s.acts[...] = lowered(act)
    s.p2[c, pb, :, 8320:10240] = pack(act)
    slope = 0.5 * (1.0 + t) + 0.5 * v * (1.0 - t * t) * GELU_A * (1.0 + 3.0 * GELU_B * v * v)
    gp = s.gact[...] * slope
    gp_cols = pl.ds(pl.multiple_of(1920 * z, 128), 1920)
    s.p2[c, pb, :, gp_cols] = pack(gp)
    gp = lowered(gp)
    parts = split4(nt(gp, sq[EX]))
    for j in range(4):
        s.s9[j] = lowered(parts[j])
    own_g = choose(parts, z)
    fe = w.to_z(lambda t: s.s9.at[t], lambda j: s.r9.at[j - 1])
    rows1.relay()
    g3z = choose(split4(jnp.broadcast_to(g3, (OWN, WIDTH))), z)
    fe.wait_recv()
    t = own_g
    for j in range(3):
        t = t + s.r9[j].astype(F32)
    s.t3[z] = lowered(t * g3z)
    ff = w.to_z(lambda t: s.t3.at[z], lambda j: s.t3.at[z])
    fp = w.to_z(lambda t: s.p2.at[c, pb, :, gp_cols], lambda j: s.p2.at[c, pb, :, gp_cols])
    ff.wait_recv()
    og = s.ogs[...]
    t = join4([s.t3[j].astype(F32) for j in range(4)])
    gain3 = jnp.sum(t * n3, 0, keepdims=True) / g3
    grad_two = og + rs3 * (t - n3 * jnp.mean(t * n3, -1, keepdims=True))
    gcb = lowered(grad_two)
    s.gm[c] = lowered(nt(gcb, sq[CO]))
    f7 = w.to_core((s.gm.at[c], s.gm.at[c]))
    s.p3[c, pb, :, :1920] = pack(grad_two)
    rows3 = PlaneRows(w, s.p3)
    mix_core.wait_recv()
    f7.wait_recv()

    gms = [s.gm[k].astype(F32) for k in (0, 1)]
    mxs = [join4([s.mixg[k, j].astype(F32) for j in range(4)]) for k in (0, 1)]
    gm_q = [gms[q // 2][PAD * (q % 2) : PAD * (q % 2 + 1)] for q in range(4)]
    mx_q = [mxs[q // 2][PAD * (q % 2) : PAD * (q % 2 + 1)] for q in range(4)]
    tots = [[] for q in range(4)]
    for p in range(6):
        blocks_p = []
        for q in range(4):
            col = s.wcol[48 * p : 48 * (p + 1), 16 + q : 17 + q]
            y = pair_stack(gm_q[q], p) * col
            m = mx_q[q][:, 128 * p : 128 * (p + 1)]
            tots[q].append(-jnp.sum(y * jnp.concatenate([m, m], 0), -1, keepdims=True))
            blocks_p.append(y)
        s.y6[p] = lowered(jnp.concatenate(blocks_p, 0))
        t = lowered(nt(s.y6[p], sq[CV, :, 128 * p : 128 * (p + 1)]))
        for q in range(4):
            s.gv[q, 48 * p : 48 * (p + 1), :] = t[48 * q : 48 * (q + 1)]
    lane = lanes(ROWS, 128)
    t = jnp.zeros((ROWS, 128), F32)
    for q in range(4):
        t = jnp.where(lane == q, jnp.concatenate(tots[q], 0), t)
    s.tot[...] = t
    for p in range(6):
        t = jnp.concatenate([s.bs[q, 48 * p : 48 * (p + 1), :] for q in range(4)], 0)
        s.vw1[128 * p : 128 * (p + 1), :] = lowered(tn(s.y6[p], t))
    vred = CrossReduce(w, [s.vw1, s.vr1, s.vw2, s.vr2, s.vw3, s.vr3, s.vw4])
    vred.core()
    fp.wait_recv()
    rows2 = PlaneRows(w, s.p2)

    def grads(q, carry):
        pick = lanes(ROWS, 128) == q
        tot = jnp.sum(jnp.where(pick, s.tot[...], 0.0), -1, keepdims=True)
        t = nt(s.gv[q], enc[q]) + tot
        s.gs[q] = lowered(s.es[q].astype(F32) * t)
        s.as_[q] = lowered(nn(s.gs[q], enc[q]))
        return carry

    lax.fori_loop(0, 2, grads, 0)
    rows3.relay()
    vred.plane()
    lax.fori_loop(2, 4, grads, 0)
    tiles = [[] for q in range(4)]
    for p in range(6):
        t = jnp.concatenate([s.as_[q, 48 * p : 48 * (p + 1), :] for q in range(4)], 0)
        t = nn(t, sq[CK, :, 128 * p : 128 * (p + 1)])
        for q in range(4):
            a = t[48 * q : 48 * (q + 1)]
            tiles[q].append(jnp.where(low, a[:PAD], a[PAD:]))
    num = jnp.concatenate([jnp.concatenate(tiles[q], 1) for q in range(4)], 0) * 0.125
    for k in (0, 1):
        for j, part in enumerate(split4(num[OWN * k : OWN * (k + 1)])):
            s.s7[k, j] = lowered(part)
    fc = w.to_core((s.s7.at[1 - c], s.c7))
    for p in range(6):
        t = jnp.concatenate([s.as_[q, 48 * p : 48 * (p + 1), :] for q in range(4)], 0)
        s.kw1[128 * p : 128 * (p + 1), :] = lowered(tn(s.x6[p], t))
    kred = CrossReduce(w, [s.kw1, s.kr1, s.kw2, s.kr2, s.kw3, s.kr3, s.kw4])
    fc.wait_recv()
    for j in range(4):
        s.z7[j] = lowered(s.s7[c, j].astype(F32) + s.c7[j].astype(F32))
    f8 = w.to_z(lambda t: s.z7.at[t], lambda j: s.r7.at[j - 1])
    kred.core()
    out_copies = []

    def encoding_grad(q):
        s.eg[q] = lowered(tn(s.es[q], s.gv[q]) + tn(s.gs[q], s.qk[q]))
        out_copies.append(w.local(s.eg.at[q], r.encoding_grad.at[q]))

    encoding_grad(0)
    kred.plane()
    rows2.relay()
    encoding_grad(1)

    f8.wait_recv()
    t = s.z7[z].astype(F32)
    for k in range(3):
        t = t + s.r7[k].astype(F32)
    s.gcq[z] = lowered(t)
    f9 = w.to_z(lambda t: s.gcq.at[z], lambda j: s.gcq.at[z])
    parts = split4(nn(s.acts[...], rd[...]))
    for j in range(4):
        s.s8[j] = lowered(parts[j])
    own_d = choose(parts, z)
    fo = w.to_z(lambda t: s.s8.at[t], lambda j: s.r8.at[j - 1])
    rows1.core()
    rows3.core()
    encoding_grad(2)
    encoding_grad(3)

    f9.wait_recv()
    gcq = join4([s.gcq[j].astype(F32) for j in range(4)])
    gh2 = nt(lowered(gcq), sq[CQ])
    gain2 = jnp.sum(gh2 * n2, 0, keepdims=True)
    t = gh2 * g2
    grad_one = grad_two + rs2o * (t - n2 * jnp.mean(t * n2, -1, keepdims=True))
    gab = lowered(grad_one)
    gsm = lowered(nt(gab, chip(SO))).astype(F32)
    gsum = jnp.zeros((3 * PAD, PAD), F32)
    dq, dk, dv = [], [], []
    for k in (0, 1):
        rows = slice(PAD * k, PAD * (k + 1))
        prob = probs[k]
        stacked = lowered(stack_heads(gsm[rows], 3))
        gw = nt(stacked, lowered(v3[rows]))
        gsb = lowered(prob * (gw - jnp.sum(gw * prob, -1, keepdims=True)))
        gsum = gsum + gsb.astype(F32)
        dq.append(pick_heads(nn(gsb, lowered(k3[rows])), 3) * 0.125)
        dk.append(tn(gsb, lowered(stacks[k])))
        dv.append(tn(lowered(prob), stacked))
    three = [jnp.concatenate([jnp.concatenate(t, 0), gap], 1) for t in (dq, dk, dv)]
    s.gsg[z] = lowered(join3(three))
    f10 = w.to_z(lambda t: s.gsg.at[z], lambda j: s.gsg.at[z])
    s.p4[c, pb, :, :1920] = pack(gcq)
    rows4 = PlaneRows(w, s.p4)
    s.p5[c, pb, :, :1920] = pack(grad_one)
    rows5 = PlaneRows(w, s.p5)
    vred.line()
    s.bias[...] = gsum

    def table_head(h, carry):
        v = s.bias[pl.ds(pl.multiple_of(PAD * h, 8), PAD), :]
        rows = [jnp.sum(jnp.where(bucket == b, v, 0.0), 0, keepdims=True) for b in range(BUCKETS)]
        col = jnp.sum(jnp.concatenate(rows, 0), -1, keepdims=True)
        return jnp.where(lanes(BUCKETS, 128) == 3 * z + h, col, carry)

    s.stz[z] = lax.fori_loop(0, 3, table_head, jnp.zeros((BUCKETS, 128), F32))
    ft = w.to_z(lambda t: s.stz.at[z], lambda j: s.stz.at[z])
    rows2.core()
    fo.wait_recv()
    t = r2z + own_d
    for j in range(3):
        t = t + s.r8[j].astype(F32)
    s.dog[c, z] = lowered(t)
    fg = w.to_z(lambda t: s.dog.at[c, z], lambda j: s.dog.at[c, z])
    rows1.finish()

    def half_product(ref, begin, index, rows):
        rows.finish()
        lhs = inputs_half(unpack(ref, begin, 256), c)
        s.wg[index] = lowered(nn(lhs, unpack(ref, 0, WIDTH))[:96])
        out_copies.append(w.local(s.wg.at[index], r.squares.at[index]))

    half_product(s.p3, 768, 7, rows3)

    f10.wait_recv()
    unpacked = [part3(s.gsg[j].astype(F32)) for j in range(4)]
    three = [join4([unpacked[j][k] for j in range(4)]) for k in range(3)]
    for k in range(3):
        s.p6[c, pb, :, 1920 * k : 1920 * (k + 1)] = pack(three[k])
    three = [lowered(v) for v in three]
    rows6 = PlaneRows(w, s.p6)
    gh1 = nt(three[0], chip(SQ)) + nt(three[1], chip(SK)) + nt(three[2], chip(SV))
    g1z = choose(split4(jnp.broadcast_to(g1, (OWN, WIDTH))), z)
    s.tg[z] = lowered(jnp.concatenate([gh1 * g1z[:, :PART], gap], 1))
    f11 = w.to_z(lambda t: s.tg.at[z], lambda j: s.tg.at[z])
    ft.wait_recv()
    s.stab[c, pb] = s.stz[0] + s.stz[1] + s.stz[2] + s.stz[3]
    tab_rows = PlaneSmall(w, s.stab)
    kred.line()
    vred.spread()
    rows2.finish()
    p2 = s.p2
    lhs = inputs_half(unpack(p2, 3072, 256), c)
    for j in range(4):
        cols = slice(WIDTH * j, WIDTH * (j + 1))
        s.gexs[:, cols] = lowered(nn(lhs, unpack(p2, WIDTH * j, WIDTH))[:96])
    out_copies.append(w.local(s.gexs, r.gex))
    rows4.relay()
    rows5.relay()
    f11.wait_recv()
    fg.wait_recv()
    fgc = w.to_core((s.dog.at[c], s.dog.at[c]))
    t = join4([s.tg[j].astype(F32) for j in range(4)])
    n1 = s.xs[...] * rs1
    gain1 = jnp.sum(t * n1, 0, keepdims=True) / g1
    s.dgr[c] = grad_one + rs1 * (t - n1 * jnp.mean(t * n1, -1, keepdims=True))
    fd = w.to_core((s.dgr.at[c], s.dgr.at[c]))
    s.sgain[c, pb] = jnp.concatenate([gain1, gain2, gain3, jnp.zeros((5, WIDTH), F32)], 0)
    gain_rows = PlaneSmall(w, s.sgain)
    rows6.relay()
    kred.spread()
    vred.rows.core()
    rows4.core()
    rows5.core()
    t = unpack(p2, 3328, WIDTH).astype(F32)
    lhs = lowered(lax.select(c == 1, t[:, 384:], t[:, :384]).T)
    s.gres[...] = lowered(nn(lhs, unpack(s.p1, 0, WIDTH)))
    out_copies.append(w.local(s.gres, r.gre))
    half_product(s.p4, 768, 4, rows4)
    half_product(s.p5, 768, 3, rows5)
    tab_rows.core()
    gain_rows.core()
    fgc.wait_recv()
    fd.wait_recv()
    for k in (0, 1):
        t = join4([s.dog[k, j].astype(F32) for j in range(4)])
        for m in (0, 1):
            r.decoder_out[:, 2 * k + m, :] = t[PAD * m : PAD * m + ANS]
            r.decoder_grad[:, 2 * k + m, :] = s.dgr[k, PAD * m : PAD * m + ANS, :]
    kred.rows.core()
    rows6.core()
    vred.rows.finish()
    s.wg[6] = vred.result()
    out_copies.append(w.local(s.wg.at[6], r.squares.at[6]))
    gain_rows.finish()
    tab_rows.finish()
    t = s.sgain[0, 0]
    u = s.stab[0, 0]
    for k in range(1, 8):
        t = t + s.sgain[k // 4, k % 4]
        u = u + s.stab[k // 4, k % 4]
    r.gains[...] = t
    r.table_grad[...] = u
    kred.rows.finish()
    s.wg[5] = kred.result()
    out_copies.append(w.local(s.wg.at[5], r.squares.at[5]))
    rows6.finish()
    ref = s.p6
    lhs = inputs_half(unpack(ref, 2304, 256), c)
    for k in range(3):
        s.wg[k] = lowered(nn(lhs, unpack(ref, WIDTH * k, WIDTH))[:96])
        out_copies.append(w.local(s.wg.at[k], r.squares.at[k]))
    for copy in out_copies:
        copy.wait()
    for batch in w.batches:
        batch.wait_send()


def write(dout, dgrad, eg, sq, gex, gre, gains, table, *refs):
    outs, (veg, vsq, vex, vre, weg, wsq, wex, wre, sems) = refs[:17], refs[17:]
    o_out, o_grad, o_eg, outs = outs[0], outs[1], outs[2], outs[3:]
    jobs = [(eg.at[q], veg.at[q], weg.at[q], o_eg.at[q]) for q in range(4)]
    jobs += [(gex, vex, wex, outs[8]), (gre, vre, wre, outs[9])]
    jobs += [(sq.at[k], vsq.at[k], wsq.at[k], outs[k]) for k in range(8)]
    loads = [pltpu.make_async_copy(j[0], j[1], sems.at[k]) for k, j in enumerate(jobs)]
    for copy in loads:
        copy.start()
    o_out[...] = dout[...]
    o_grad[...] = dgrad[...]
    for k in range(3):
        outs[10 + k][...] = gains[k : k + 1, :].reshape(WIDTH)
    outs[13][...] = table[...].T[:HEADS]
    stores = []
    for k, (src, near, wide, dst) in enumerate(jobs):
        loads[k].wait()
        wide[...] = near[...].astype(F32)
        stores.append(pltpu.make_async_copy(wide, dst, sems.at[len(jobs) + k]))
        stores[-1].start()
    for copy in stores:
        copy.wait()


def fused(x, enc, og, plen, pcount, buckets, wq, wk, wv, wo, wcq, wck, wcv, wco, wex, wre, g1, g2, g3, table):
    def shape(*dims, kind=F32):
        return jax.ShapeDtypeStruct(dims, kind)

    rows = shape(ANS, 4, WIDTH)
    mid = pl.pallas_call(
        layer,
        out_shape=[
            rows,
            rows,
            shape(4, SLOT, WIDTH, kind=BF),
            shape(8, 96, WIDTH, kind=BF),
            shape(96, FF, kind=BF),
            shape(384, WIDTH, kind=BF),
            shape(8, WIDTH),
            shape(BUCKETS, 128),
        ],
        in_specs=[pl.BlockSpec(memory_space=k) for k in IN_KIND.values()],
        out_specs=[pl.BlockSpec(memory_space=k) for k in OUT_KIND.values()],
        scratch_shapes=[pltpu.VMEM(*v) for v in SCRATCH.values()]
        + [pltpu.SemaphoreType.DMA((SEMAPHORES,))],
        compiler_params=pltpu.CompilerParams(
            collective_id=0, has_side_effects=True, vmem_limit_bytes=62 * 2**20
        ),
    )(
        jnp.transpose(x, (1, 0, 2)),
        jnp.transpose(og, (1, 0, 2)),
        *(plen, pcount, buckets, table.T, g1, g2, g3, enc),
        *(wq, wk, wv, wo, wcq, wck, wcv, wco, wex, wre),
    )
    near, far = pl.BlockSpec(memory_space=NEAR), pl.BlockSpec(memory_space=FAR)
    square = shape(96, WIDTH)
    out = pl.pallas_call(
        write,
        out_shape=[
            *(rows, rows, shape(4, SLOT, WIDTH)),
            *[square] * 8,
            *(shape(96, FF), shape(384, WIDTH)),
            *[shape(WIDTH)] * 3,
            shape(HEADS, BUCKETS),
        ],
        in_specs=[near, near, far, far, far, far, near, near],
        out_specs=[near, near, far, *[far] * 10, *[near] * 4],
        scratch_shapes=[
            pltpu.VMEM(dims, kind)
            for kind in (BF, F32)
            for dims in ((4, SLOT, WIDTH), (8, 96, WIDTH), (96, FF), (384, WIDTH))
        ]
        + [pltpu.SemaphoreType.DMA((28,))],
        compiler_params=pltpu.CompilerParams(vmem_limit_bytes=62 * 2**20),
    )(*mid)
    out = list(out)
    out[0], out[1] = (jnp.transpose(v, (1, 0, 2)) for v in out[:2])
    out[16] = out[16].T
    return tuple(out)


def solution(mesh):
    if dict(mesh.shape) != {"pb": 4, "pa": 8}:
        return generic(mesh)
    wide, tall = P("pb", "pa", None), P("pa", None)
    rows, whole = P("pb", None, None), P()
    return jax.shard_map(
        fused,
        mesh=mesh,
        in_specs=(rows, wide, rows, P("pb"), P("pb"), whole, *[tall] * 10, *[whole] * 4),
        out_specs=(rows, rows, wide, *[tall] * 10, *[whole] * 4),
        check_vma=False,
    )
```
